32 devices in a mesh: slab: 2 (over y), tile: 4 (over z), gz: 2 (over x), rep: 2 (over core).
Axes of the slice: x: 2, y: 2, z: 4, core: 2. Of those that a mesh axis runs over, the one named last changes fastest.
Arguments:
- fixed_image: bfloat16 [16, 256, 512], P(('slab', 'gz'), 'tile', 'rep'), parts along dimension 0, may hold values from -6 to 6
- moving_image: bfloat16 [16, 256, 512], P(('slab', 'gz'), 'tile', 'rep'), parts along dimension 0, may hold values from -6 to 6
- source_tile: int32 [8, 2, 8, 1], P('slab', 'rep'), parts along dimension 0, may hold values from 0 to 3; in each aligned block of 8 rows (0 to 7, 8 to 15, ..., all dimensions but the last counted through in order) at most 4 rows name the same one
- block_shifts: int32 [8, 2, 8, 2], P(('slab', 'tile'), 'rep'), parts along dimension 0, may hold values from 0 to 63
Outputs:
- spline_grad: float32 [3, 2, 16, 32], P(None, 'slab', 'tile', 'rep'), parts along dimension 1
The draws below stay inside these ranges and needn't reach their ends.
There are 2 independent parts, one for each index of `slab`. The reference program is written for one: setup_inputs(seed, part) draws one part's arguments, and reference() takes and returns one part's arrays. A program takes and returns all parts, laid end to end along the dimension named above; each array names one. Nothing has to cross between parts.
Inputs may be any that keep to these rules, and one draw needn't show every extreme that they name: `source_tile`: among the 8 blocks of one device (one index pair of the first two dimensions) no tile is named more than 4 times; in every draw some device names one tile exactly 4 times.
All inputs are finite; a program needn't handle non-finite values.
Results may differ from the reference program's by a relative error of at most 0.00085.
Values may be sent and summed in bfloat16 or wider, within the bound.
No kernel may reach another device: no remote copies, remote signals or barrier semaphores. Data moves between devices by JAX's collectives and lax.ppermute only.
A program may use at most 64 MiB of HBM per device.

```python
import math
import jax
import jax.numpy as jnp
import numpy as np
from jax import lax

TY = 64
XD = 256
BLK_Y = 16
BLK_X = 128
RAD = 2
SPACING = 16
NB_DEV = 8
CAP = 4
Z = 8
NY = 256
NX = 512
N_TILE = 4
N_REP = 2


def plant(entries, own_key, smallest, largest):
    longest = entries.shape.index(max(entries.shape))
    spots = []
    for shift in (0, 1):
        where = [jax.random.randint(jax.random.fold_in(own_key, axis), (), 0, length) for axis, length in enumerate(entries.shape)]
        where[longest] = (where[longest] + shift) % entries.shape[longest]
        spots.append(tuple(where))
    return entries.at[spots[0]].set(smallest).at[spots[1]].set(largest)


def steps_of(rng, dims, split, low, top_value):
    loudness, own = 1.0, jax.random.fold_in(rng, 6)
    for axis_at, blocks in split:
        draws = jnp.exp(jax.random.uniform(jax.random.fold_in(own, axis_at), (blocks,), jnp.float32, low / len(split), top_value / len(split)))
        loudness = loudness * jnp.repeat(draws, dims[axis_at] // blocks).reshape([-1 if axis == axis_at else 1 for axis in range(len(dims))])
    return loudness


def routed_block(key, own, number, rows, count, top, bound, lean):
    ranking = jax.random.permutation(key, count)
    packed, common = portions_of(count, rows * top, bound, lean, True), portions_of(count, rows * top, bound, lean, False)
    places = jnp.arange(count)

    def named(lengths, rotation):
        used = int((lengths > 0).sum())
        fixed = max(1, used // 4)
        shifted = fixed + (places - fixed + rotation * (used - fixed)) % max(1, count - fixed)
        return jnp.zeros((count,), jnp.int32).at[ranking[jnp.where(places < fixed, places, shifted)]].set(jnp.asarray(lengths, jnp.int32))

    lengths = jnp.where(number % 4 == 0, named(packed, number // 4), named(common, number - number // 4 - 1))
    mixed = jax.random.permutation(jax.random.fold_in(own, 3), count)
    source_of, taker = mixed[0:count // 2 * 2:2], mixed[1:count // 2 * 2:2]
    slack = jnp.minimum(lengths[source_of] - 1, bound - lengths[taker]) // 2
    slack = jnp.where((source_of == ranking[0]) | (taker == ranking[0]) | (lengths[taker] == 0), 0, jnp.maximum(slack, 0))
    shifted = jax.random.randint(jax.random.fold_in(own, 4), (count // 2,), 0, 1 << 20) % (slack + 1)
    lengths = lengths.at[source_of].add(-shifted).at[taker].add(shifted)
    items = jnp.searchsorted(jnp.cumsum(lengths), jnp.arange(rows * top), side="right").astype(jnp.int32)
    table = items.reshape(top, rows).T
    table = table[jax.random.permutation(jax.random.fold_in(own, 1), rows)]
    rotation = jax.random.randint(jax.random.fold_in(own, 2), (rows, 1), 0, top)
    return jnp.take_along_axis(table, (jnp.arange(top)[None, :] + rotation) % top, axis=1)


def portions_of(amount, total, most, skew, full):
    portions = [(1 << 20) // math.isqrt(standing ** skew) + 1 for standing in range(1, amount + 1)]
    largest = most if full else min(most, max(-(-total // amount), total * portions[0] // sum(portions)))
    least = 1 if total - largest >= amount - 1 else 0
    counts, spare = [largest] + [least] * (amount - 1), total - largest - least * (amount - 1)
    while spare > 0:
        movable = [i for i in range(1, amount) if counts[i] < largest] or [i for i in range(1, amount) if counts[i] < most]
        whole, remaining = sum([portions[i] for i in movable]), spare
        for i in movable:
            addition = min(most - counts[i], max(1, remaining * portions[i] // whole), spare)
            counts[i] = counts[i] + addition
            spare = spare - addition
    return np.array(counts)


def scatter_about(own_key, dims, deviation, bound, cuts=(), kind=jnp.bfloat16):
    entries = jax.random.normal(own_key, dims, jnp.float32) * deviation
    if len(cuts) > 0:
        entries = steps_of(own_key, dims, cuts, -0.22, 0.18) * entries
    return jnp.clip(entries, min=-bound, max=bound).astype(kind)


def setup_inputs(seed: int = 0, part: int = 0) -> dict:
    key_of = jax.random.split(jax.random.key(seed), 5)
    part_keys = jax.random.split(jax.random.fold_in(key_of[4], part), 5)
    fixed_image = scatter_about(part_keys[0], (Z, NY, NX), 1.0, 6.0, ((0, 2), (1, 4), (2, 2)))
    moving_image = scatter_about(part_keys[1], (Z, NY, NX), 1.0, 6.0, ((0, 2), (1, 4), (2, 2)))
    source_tile_keys = jax.random.split(jax.random.fold_in(part_keys[2], 1), N_TILE * N_REP * NB_DEV // NB_DEV)
    source_tile_turns = jax.random.permutation(jax.random.fold_in(part_keys[2], 3), N_TILE * N_REP * NB_DEV // NB_DEV)
    source_tile = jax.vmap(lambda own, number: routed_block(jax.random.fold_in(part_keys[2], 2), own, number, NB_DEV, N_TILE, 1, CAP, 2))(source_tile_keys, source_tile_turns).reshape((N_TILE, N_REP, NB_DEV, 1))
    block_shifts = plant(jax.random.randint(part_keys[3], (N_TILE, N_REP, NB_DEV, 2), 0, 64), jax.random.fold_in(part_keys[3], 1), 0, 63).astype(jnp.int32)
    return dict(fixed_image=fixed_image, moving_image=moving_image, source_tile=source_tile, block_shifts=block_shifts)


den_floor = 1e-5


def window_sum(extended, radius):
    result = extended
    for axis_id in range(3):
        length = result.shape[axis_id] - 2 * radius
        summed = lax.slice_in_dim(result, 0, length, axis=axis_id)
        for offset in range(1, 2 * radius + 1):
            summed = summed + lax.slice_in_dim(result, offset, offset + length, axis=axis_id)
        result = summed
    return result


def window_terms(ext_fixed, ext_warp, radius):
    volume = float((2 * radius + 1) ** 3)
    sum_fixed = window_sum(ext_fixed, radius)
    sum_warp = window_sum(ext_warp, radius)
    sum_fixed_sq = window_sum(ext_fixed * ext_fixed, radius)
    sum_warp_sq = window_sum(ext_warp * ext_warp, radius)
    sum_product = window_sum(ext_fixed * ext_warp, radius)
    cross_term = sum_product - sum_fixed * sum_warp / volume
    fixed_var = sum_fixed_sq - sum_fixed * sum_fixed / volume
    warp_var = sum_warp_sq - sum_warp * sum_warp / volume
    denominator = fixed_var * warp_var + den_floor
    term_a = 2.0 * cross_term / denominator
    term_b = -cross_term * cross_term * fixed_var / (denominator * denominator)
    term_c = -(term_a * sum_fixed + 2.0 * term_b * sum_warp) / volume
    return term_a, term_b, term_c


def slopes(extended, margin, extent):
    result = []
    for axis_id in range(3):
        ahead = [margin, margin, margin]
        behind = [margin, margin, margin]
        ahead[axis_id] += 1
        behind[axis_id] -= 1
        upper = lax.slice(extended, tuple(ahead), (ahead[0] + extent[0], ahead[1] + extent[1], ahead[2] + extent[2]))
        lower = lax.slice(extended, tuple(behind), (behind[0] + extent[0], behind[1] + extent[1], behind[2] + extent[2]))
        result.append(0.5 * (upper - lower))
    return result


def spline_table(first_pos, length, first_col, columns):
    places = first_pos + jnp.arange(length, dtype=jnp.int32)
    knots = places // SPACING
    within = (places - knots * SPACING).astype(jnp.float32) / SPACING
    squares = within * within
    cubes = squares * within
    weights = ((1.0 - within) ** 3 / 6.0, (3.0 * cubes - 6.0 * squares + 4.0) / 6.0,
               (-3.0 * cubes + 3.0 * squares + 3.0 * within + 1.0) / 6.0, cubes / 6.0)
    targets = first_col + jnp.arange(columns, dtype=jnp.int32)
    table = jnp.zeros((length, columns), jnp.float32)
    for offset in range(4):
        table = table + jnp.where(targets[None, :] == (knots + offset - 1)[:, None], weights[offset][:, None], 0.0)
    return table


def contract(pieces, table_z, table_y, table_x):
    highest = lax.Precision.HIGHEST
    along_x = jnp.einsum("czyx,xk->czyk", pieces, table_x, precision=highest)
    along_y = jnp.einsum("czyk,yj->czjk", along_x, table_y, precision=highest)
    return jnp.einsum("czjk,zl->cljk", along_y, table_z, precision=highest)


def in_range(first_pos, length, limit):
    places = first_pos + jnp.arange(length, dtype=jnp.int32)
    return (places >= 0) & (places < limit)


def roll_block(block, amounts):
    return jnp.roll(jnp.roll(block, amounts[0], axis=1), amounts[1], axis=2)


def reference(fixed_image, moving_image, source_tile, block_shifts):
    depth, height_all, width_all = fixed_image.shape
    yblocks = TY // BLK_Y
    xblocks = XD // BLK_X
    arranged = moving_image.reshape(depth, N_TILE, yblocks, BLK_Y, N_REP, xblocks, BLK_X).transpose(1, 4, 2, 5, 0, 3, 6)
    sources = source_tile[..., 0].reshape(N_TILE, N_REP, yblocks, xblocks)
    rep_ids = jnp.arange(N_REP, dtype=jnp.int32)[None, :, None, None]
    row_ids = jnp.arange(yblocks, dtype=jnp.int32)[None, None, :, None]
    col_ids = jnp.arange(xblocks, dtype=jnp.int32)[None, None, None, :]
    picked = arranged[sources, rep_ids, row_ids, col_ids]
    flatten = picked.reshape(-1, depth, BLK_Y, BLK_X)
    rolled = jax.vmap(roll_block)(flatten, block_shifts.reshape(-1, 2))
    warped = rolled.reshape(N_TILE, N_REP, yblocks, xblocks, depth, BLK_Y, BLK_X).transpose(4, 0, 2, 5, 1, 3, 6)
    warped = warped.reshape(depth, height_all, width_all)

    margin = 2 * RAD
    fixed_padded = jnp.pad(fixed_image, margin)
    warp_padded = jnp.pad(warped, margin)
    depth_knots = (depth + SPACING - 1) // SPACING
    table_z = spline_table(0, depth, 0, depth_knots)
    col_knots = width_all // SPACING
    table_x = spline_table(0, width_all, -2, col_knots + 4)
    row_knots = TY // SPACING
    inside_depth = in_range(-RAD, depth + 2 * RAD, depth)
    inside_cols = in_range(-RAD, width_all + 2 * RAD, width_all)

    def strip(totals, tile_id):
        ext_fixed = lax.dynamic_slice_in_dim(fixed_padded, tile_id * TY, TY + 2 * margin, axis=1).astype(jnp.float32)
        ext_warp = lax.dynamic_slice_in_dim(warp_padded, tile_id * TY, TY + 2 * margin, axis=1).astype(jnp.float32)
        term_a, term_b, term_c = window_terms(ext_fixed, ext_warp, RAD)
        inside_rows = in_range(tile_id * TY - RAD, TY + 2 * RAD, height_all)
        inside = inside_depth[:, None, None] & inside_rows[None, :, None] & inside_cols[None, None, :]
        box_a = window_sum(jnp.where(inside, term_a, 0.0), RAD)
        box_b = window_sum(jnp.where(inside, term_b, 0.0), RAD)
        box_c = window_sum(jnp.where(inside, term_c, 0.0), RAD)
        extent = (depth, TY, width_all)
        fixed_own = lax.slice(ext_fixed, (margin, margin, margin), (margin + depth, margin + TY, margin + width_all))
        warp_own = lax.slice(ext_warp, (margin, margin, margin), (margin + depth, margin + TY, margin + width_all))
        gain = -(fixed_own * box_a + 2.0 * warp_own * box_b + box_c)
        slope_z, slope_y, slope_x = slopes(ext_warp, margin, extent)
        pieces = jnp.stack((gain * slope_z, gain * slope_y, gain * slope_x))
        table_y = spline_table(tile_id * TY, TY, tile_id * row_knots - 2, row_knots + 4)
        local_grad = contract(pieces, table_z, table_y, table_x)
        current = lax.dynamic_slice_in_dim(totals, tile_id * row_knots, row_knots + 4, axis=2)
        totals = lax.dynamic_update_slice_in_dim(totals, current + local_grad, tile_id * row_knots, axis=2)
        return totals, None

    totals = jnp.zeros((3, depth_knots, N_TILE * row_knots + 4, col_knots + 4), jnp.float32)
    totals, unused = lax.scan(strip, totals, jnp.arange(N_TILE, dtype=jnp.int32))
    return totals[:, :, 2:-2, 2:-2]
```

```python
import functools

import jax
import jax.numpy as jnp
from jax import lax
from jax.experimental import pallas as pl
from jax.experimental.pallas import tpu as pltpu
from jax.sharding import PartitionSpec as P

BLK_Y = 16
BLK_X = 128
RAD = 2
SPACING = 16
MAX_NAMED = 4


den_floor = 1e-05

def with_halo(array, sides, width):
    for axis, dim in sides:
        count, length = (lax.axis_size(axis), array.shape[dim])
        up = [(i, (i + 1) % count) for i in range(count - 1)]
        down = [(j, i) for i, j in up]
        last = lax.slice_in_dim(array, length - width, length, axis=dim)
        first = lax.slice_in_dim(array, 0, width, axis=dim)
        before = lax.ppermute(last, axis, up)
        after = lax.ppermute(first, axis, down)
        array = jnp.concatenate([before, array, after], axis=dim)
    return array


def window_sum(extended, radius):
    result = extended
    for axis_id in range(3):
        length = result.shape[axis_id] - 2 * radius
        summed = lax.slice_in_dim(result, 0, length, axis=axis_id)
        for offset in range(1, 2 * radius + 1):
            summed = summed + lax.slice_in_dim(result, offset, offset + length, axis=axis_id)
        result = summed
    return result


def window_terms(ext_fixed, ext_warp, radius):
    volume = float((2 * radius + 1) ** 3)
    sum_fixed = window_sum(ext_fixed, radius)
    sum_warp = window_sum(ext_warp, radius)
    sum_fixed_sq = window_sum(ext_fixed * ext_fixed, radius)
    sum_warp_sq = window_sum(ext_warp * ext_warp, radius)
    sum_product = window_sum(ext_fixed * ext_warp, radius)
    cross_term = sum_product - sum_fixed * sum_warp / volume
    fixed_var = sum_fixed_sq - sum_fixed * sum_fixed / volume
    warp_var = sum_warp_sq - sum_warp * sum_warp / volume
    denominator = fixed_var * warp_var + den_floor
    term_a = 2.0 * cross_term / denominator
    term_b = -cross_term * cross_term * fixed_var / (denominator * denominator)
    term_c = -(term_a * sum_fixed + 2.0 * term_b * sum_warp) / volume
    return (term_a, term_b, term_c)


def slopes(extended, margin, extent):
    result = []
    for axis_id in range(3):
        ahead = [margin, margin, margin]
        behind = [margin, margin, margin]
        ahead[axis_id] += 1
        behind[axis_id] -= 1
        upper = lax.slice(
            extended,
            tuple(ahead),
            (ahead[0] + extent[0], ahead[1] + extent[1], ahead[2] + extent[2]),
        )
        lower = lax.slice(
            extended,
            tuple(behind),
            (behind[0] + extent[0], behind[1] + extent[1], behind[2] + extent[2]),
        )
        result.append(0.5 * (upper - lower))
    return result


def spline_table(first_pos, length, first_col, columns):
    places = first_pos + jnp.arange(length, dtype=jnp.int32)
    knots = places // SPACING
    within = (places - knots * SPACING).astype(jnp.float32) / SPACING
    squares = within * within
    cubes = squares * within
    weights = (
        (1.0 - within) ** 3 / 6.0,
        (3.0 * cubes - 6.0 * squares + 4.0) / 6.0,
        (-3.0 * cubes + 3.0 * squares + 3.0 * within + 1.0) / 6.0,
        cubes / 6.0,
    )
    targets = first_col + jnp.arange(columns, dtype=jnp.int32)
    table = jnp.zeros((length, columns), jnp.float32)
    for offset in range(4):
        table = table + jnp.where(
            targets[None, :] == (knots + offset - 1)[:, None], weights[offset][:, None], 0.0
        )
    return table


def contract(pieces, table_z, table_y, table_x):
    highest = lax.Precision.HIGHEST
    along_x = jnp.einsum("czyx,xk->czyk", pieces, table_x, precision=highest)
    along_y = jnp.einsum("czyk,yj->czjk", along_x, table_y, precision=highest)
    return jnp.einsum("czjk,zl->cljk", along_y, table_z, precision=highest)


def roll_block(block, amounts):
    return jnp.roll(jnp.roll(block, amounts[0], axis=1), amounts[1], axis=2)


def fold_rims(extended, axis_id, owned):
    middle = lax.slice_in_dim(extended, 4, owned + 4, axis=axis_id)
    leading = lax.slice_in_dim(extended, 0, 2, axis=axis_id)
    trailing = lax.slice_in_dim(extended, owned + 6, owned + 8, axis=axis_id)
    lead_pad = [(0, 0), (0, 0), (0, 0), (0, 0)]
    trail_pad = [(0, 0), (0, 0), (0, 0), (0, 0)]
    lead_pad[axis_id] = (0, owned - 2)
    trail_pad[axis_id] = (owned - 2, 0)
    return middle + jnp.pad(leading, lead_pad) + jnp.pad(trailing, trail_pad)


def body(fixed_image, moving_image, source_tile, block_shifts):
    depth, height, width = fixed_image.shape
    yblocks = height // BLK_Y
    xblocks = width // BLK_X
    block_count = yblocks * xblocks
    tile_lists = source_tile[:, 0, :, 0]
    my_tile = lax.axis_index("tile")
    own_list = lax.dynamic_index_in_dim(tile_lists, my_tile, 0, keepdims=False)
    row_steps = jnp.arange(BLK_Y, dtype=jnp.int32)
    initial = jnp.zeros((block_count, depth, BLK_Y, BLK_X), jnp.bfloat16)
    piece = lax.all_gather(moving_image, "tile", axis=1, tiled=True)
    length = piece.shape[1]
    held_blocks = []
    for block_id in range(block_count):
        row_block = block_id // xblocks
        col_block = block_id % xblocks
        wanted = own_list[block_id] * height + row_block * BLK_Y + row_steps
        usable = (wanted >= 0) & (wanted < length)
        columns_part = lax.slice_in_dim(piece, col_block * BLK_X, (col_block + 1) * BLK_X, axis=2)
        taken = jnp.take(columns_part, jnp.clip(wanted, 0, length - 1), axis=1)
        held_blocks.append(jnp.where(usable[None, :, None], taken, initial[block_id]))
    blocks = jnp.stack(held_blocks)
    rolled = jax.vmap(roll_block)(blocks, block_shifts[0, 0])
    warped = (
        rolled.reshape(yblocks, xblocks, depth, BLK_Y, BLK_X)
        .transpose(2, 0, 3, 1, 4)
        .reshape(depth, height, width)
    )
    image_pair = jnp.stack((fixed_image, warped))
    fixed_own = fixed_image.astype(jnp.float32)
    warp_own = warped.astype(jnp.float32)
    extended = with_halo(image_pair, (("tile", 2), ("gz", 1), ("rep", 3)), RAD).astype(jnp.float32)
    term_a, term_b, term_c = window_terms(extended[0], extended[1], RAD)
    terms_ext = with_halo(
        jnp.stack((term_a, term_b, term_c)).astype(jnp.bfloat16),
        (("tile", 2), ("gz", 1), ("rep", 3)),
        RAD,
    ).astype(jnp.float32)
    box_a = window_sum(terms_ext[0], RAD)
    box_b = window_sum(terms_ext[1], RAD)
    box_c = window_sum(terms_ext[2], RAD)
    margin = RAD
    gain = -(fixed_own * box_a + 2.0 * warp_own * box_b + box_c)
    slope_z, slope_y, slope_x = slopes(extended[1], margin, (depth, height, width))
    pieces = jnp.stack((gain * slope_z, gain * slope_y, gain * slope_x))
    depth_total = depth * lax.axis_size("gz")
    depth_knots = (depth_total + SPACING - 1) // SPACING
    table_z = spline_table(lax.axis_index("gz") * depth, depth, 0, depth_knots)
    row_knots = height // SPACING
    table_y = spline_table(my_tile * height, height, my_tile * row_knots - 2, row_knots + 4)
    col_knots = width // SPACING
    rep_index = lax.axis_index("rep")
    table_x = spline_table(rep_index * width, width, rep_index * col_knots - 2, col_knots + 4)
    local_grad = contract(pieces, table_z, table_y, table_x)
    spread = with_halo(local_grad, (("tile", 2), ("rep", 3)), 2)
    owned_grad = fold_rims(fold_rims(spread, 2, row_knots), 3, col_knots)
    return lax.psum(owned_grad, "gz")


EDGE = 2 * RAD
SEND_ROWS = 48


def pack_kernel(tiles, source_ref, place_ref, moving_ref, fixed_ref, *out_refs):
    me, half = place_ref[0], place_ref[1]
    packs, fixed_out = out_refs[:-1], out_refs[-1]
    height, width = moving_ref.shape[1:]
    xblocks = width // BLK_X
    blocks = (height // BLK_Y) * xblocks
    for step in range(1, tiles):
        pack = packs[step - 1]
        pack[...] = jnp.zeros_like(pack)
        other = lax.bitwise_xor(me, step)
        count = jnp.int32(0)
        for block in range(blocks):
            row, col = (block // xblocks) * BLK_Y, (block % xblocks) * BLK_X
            named = source_ref[other, block] == me

            @pl.when(named)
            def _(pack=pack, count=count, row=row, col=col):
                slot = jnp.minimum(count, pack.shape[0] - 1)
                pack[slot] = moving_ref[:, row : row + BLK_Y, col : col + BLK_X]

            count = count + named.astype(jnp.int32)
    start = pl.multiple_of((1 - half) * BLK_Y, BLK_Y)
    fixed_out[...] = fixed_ref[:, pl.ds(start, SEND_ROWS), :]


def unpack_kernel(tiles, source_ref, shift_ref, place_ref, moving_ref, fixed_ref, *refs):
    recvs = refs[: tiles - 1]
    own_ref, send_ref, straight_ref, slant_ref, rims = refs[tiles - 1 :]
    me, half = place_ref[0], place_ref[1]
    depth, height, width = moving_ref.shape
    xblocks = width // BLK_X
    blocks = (height // BLK_Y) * xblocks
    cap = recvs[0].shape[0]
    for block in range(blocks):
        row, col = (block // xblocks) * BLK_Y, (block % xblocks) * BLK_X
        source = source_ref[me, block]
        slot = jnp.int32(0)
        for earlier in range(block):
            slot = slot + (source_ref[me, earlier] == source).astype(jnp.int32)
        slot = jnp.minimum(slot, cap - 1)
        step = lax.bitwise_xor(source, me)
        value = moving_ref[:, row : row + BLK_Y, col : col + BLK_X].astype(jnp.float32)
        for other in range(1, tiles):
            value = jnp.where(step == other, recvs[other - 1][slot].astype(jnp.float32), value)
        down = lax.rem(shift_ref[block, 0], BLK_Y)
        right = lax.rem(shift_ref[block, 1], BLK_X)
        value = pltpu.roll(value, right, 2)
        for bit in (1, 2, 4, 8):
            value = jnp.where(lax.bitwise_and(down, bit) != 0, pltpu.roll(value, bit, 1), value)
        own_ref[:, row : row + BLK_Y, col : col + BLK_X] = value.astype(own_ref.dtype)
        if row == 0:
            for plane in range(depth):
                rims[1, 0, plane * EDGE : (plane + 1) * EDGE, col : col + BLK_X] = value[plane, :EDGE]
        if row == height - BLK_Y:
            for plane in range(depth):
                rims[1, 1, plane * EDGE : (plane + 1) * EDGE, col : col + BLK_X] = value[plane, -EDGE:]
    for plane in range(depth):
        top = fixed_ref[plane, :BLK_Y, :].astype(jnp.float32)
        bottom = fixed_ref[plane, height - BLK_Y :, :].astype(jnp.float32)
        rims[0, 0, plane * EDGE : (plane + 1) * EDGE, :] = top[:EDGE]
        rims[0, 1, plane * EDGE : (plane + 1) * EDGE, :] = bottom[-EDGE:]
    for image in range(2):
        straight_ref[image] = rims[image, 1 - half].astype(straight_ref.dtype)
        slant_ref[image] = rims[image, half].astype(slant_ref.dtype)
    start = pl.multiple_of((1 - half) * BLK_Y, BLK_Y)
    send_ref[...] = own_ref[:, pl.ds(start, SEND_ROWS), :]


def five(array, axis):
    size = array.shape[axis]
    pair = array + pltpu.roll(array, 1, axis)
    return pltpu.roll(pair, size - 2, axis) + pair + pltpu.roll(array, 2, axis)


def main_kernel(
    place_ref, fixed_own, fixed_got, warp_own, warp_got, straight, slant,
    fixed_own_n, fixed_got_n, warp_own_n, warp_got_n, straight_n, slant_n,
    table_y, table_x, out_ref, images, terms, sums,
):
    half, side, first, last = place_ref[1], place_ref[2], place_ref[3], place_ref[4]
    depth, rows, _ = fixed_own.shape
    planes = 2 * depth
    window, span = images.shape[2:]
    width = 2 * BLK_X
    own_col = pl.multiple_of(side * BLK_X, BLK_X)
    new_col = pl.multiple_of((1 - side) * width, BLK_X)
    take = pl.multiple_of(side * BLK_X, BLK_X)
    start = pl.multiple_of(half * BLK_Y, BLK_Y)
    lanes = lax.broadcasted_iota(jnp.int32, (window, span), 1)
    levels = lax.broadcasted_iota(jnp.int32, (window, span), 0)
    low_lane = jnp.where(side == 0, 0, BLK_X - 48)
    high_lane = jnp.where(side == 0, width + 32, span)
    inside = (lanes >= low_lane) & (lanes < high_lane)
    low_row = jnp.where(first != 0, EDGE, RAD)
    high_row = jnp.where(last != 0, window - EDGE, window - RAD)
    inside = inside & (levels >= low_row) & (levels < high_row)
    near = lax.broadcasted_iota(jnp.int32, (window, BLK_X), 1)
    near = (near >= low_lane) & (near < jnp.where(side == 0, 32, BLK_X))
    zero_plane = jnp.zeros((window, span), jnp.float32)
    for pad in (0, 1, planes + 2, planes + 3):
        for which in range(2):
            images[which, pad] = zero_plane
        for which in range(3):
            terms[which, pad] = zero_plane

    def place(which, plane, value, value_n):
        images[which, plane, :, pl.ds(own_col, width)] = value
        images[which, plane, :, pl.ds(new_col, BLK_X)] = jnp.where(near, value_n, 0.0)

    def shift_in(piece):
        return pltpu.roll(piece, jnp.where(half == 0, EDGE, SEND_ROWS - BLK_Y + EDGE), 0)[:window]

    for which, (own, got, own_n, got_n) in enumerate(
        ((fixed_own, fixed_got, fixed_own_n, fixed_got_n), (warp_own, warp_got, warp_own_n, warp_got_n))
    ):
        for i in range(depth):
            mine, theirs = 2 + half * depth + i, 2 + (1 - half) * depth + i
            place(
                which, mine,
                shift_in(own[i, pl.ds(start, SEND_ROWS), :].astype(jnp.float32)),
                shift_in(own_n[i, pl.ds(start, SEND_ROWS), pl.ds(take, BLK_X)].astype(jnp.float32)),
            )
            place(
                which, theirs,
                shift_in(got[i].astype(jnp.float32)),
                shift_in(got_n[i, :, pl.ds(take, BLK_X)].astype(jnp.float32)),
            )
        outer = (first + last) != 0
        for rim, rim_n, base in ((straight, straight_n, half), (slant, slant_n, 1 - half)):
            value = jnp.where(outer, 0.0, rim[which].astype(jnp.float32))
            value_n = jnp.where(outer, 0.0, rim_n[which, :, pl.ds(take, BLK_X)].astype(jnp.float32))
            value_n = jnp.where(near[: value_n.shape[0]], value_n, 0.0)
            for i in range(depth):
                plane = 2 + base * depth + i
                for at_half, row in ((0, 0), (1, window - EDGE)):

                    @pl.when(half == at_half)
                    def _(plane=plane, row=row, i=i, value=value, value_n=value_n, which=which):
                        images[which, plane, row : row + EDGE, pl.ds(own_col, width)] = value[i * EDGE : (i + 1) * EDGE]
                        images[which, plane, row : row + EDGE, pl.ds(new_col, BLK_X)] = value_n[i * EDGE : (i + 1) * EDGE]

    volume = float((2 * RAD + 1) ** 3)

    def box(total):
        return five(five(total, 0), 1)

    def first_pass(z, carry):
        f = [images[0, z + k] for k in range(5)]
        w = [images[1, z + k] for k in range(5)]
        sum_f = box(f[0] + f[1] + f[2] + f[3] + f[4])
        sum_w = box(w[0] + w[1] + w[2] + w[3] + w[4])
        sum_ff = box(sum(a * a for a in f[1:]) + f[0] * f[0])
        sum_ww = box(sum(a * a for a in w[1:]) + w[0] * w[0])
        sum_fw = box(sum(a * b for a, b in zip(f[1:], w[1:])) + f[0] * w[0])
        cross = sum_fw - sum_f * sum_w / volume
        var_f = sum_ff - sum_f * sum_f / volume
        var_w = sum_ww - sum_w * sum_w / volume
        inverse = 1.0 / (var_f * var_w + den_floor)
        ratio = cross * inverse
        term_a = 2.0 * ratio
        term_b = -(ratio * ratio) * var_f
        term_c = -(term_a * sum_f + 2.0 * term_b * sum_w) / volume
        terms[0, z + 2] = jnp.where(inside, term_a, 0.0)
        terms[1, z + 2] = jnp.where(inside, term_b, 0.0)
        terms[2, z + 2] = jnp.where(inside, term_c, 0.0)
        return carry

    lax.fori_loop(0, planes, first_pass, 0)
    for d in range(3):
        sums[d] = zero_plane
    owned = (levels >= EDGE) & (levels < window - EDGE)

    def second_pass(z, carry):
        boxes = []
        for which in range(3):
            t = [terms[which, z + k] for k in range(5)]
            boxes.append(box(t[0] + t[1] + t[2] + t[3] + t[4]))
        f, w = images[0, z + 2], images[1, z + 2]
        gain = -(f * boxes[0] + 2.0 * w * boxes[1] + boxes[2])
        u = z.astype(jnp.float32) * (1.0 / SPACING)
        weight = (3.0 * u * u * u - 6.0 * u * u + 4.0) * (0.5 / 6.0)
        gain = jnp.where(owned, gain, 0.0) * weight
        sums[0] += gain * (images[1, z + 3] - images[1, z + 1])
        sums[1] += gain * (pltpu.roll(w, window - 1, 0) - pltpu.roll(w, 1, 0))
        sums[2] += gain * (pltpu.roll(w, span - 1, 1) - pltpu.roll(w, 1, 1))
        return carry

    lax.fori_loop(0, planes, second_pass, 0)
    for d in range(3):
        along_x = lax.dot_general(
            sums[d], table_x[...], (((1,), (1,)), ((), ())),
            precision=lax.Precision.HIGHEST, preferred_element_type=jnp.float32,
        )
        out_ref[d] = lax.dot_general(
            table_y[...], along_x, (((1,), (0,)), ((), ())),
            precision=lax.Precision.HIGHEST, preferred_element_type=jnp.float32,
        )


def fast_body(tiles, fixed_image, moving_image, source_tile, block_shifts):
    depth, height, width = fixed_image.shape
    me, half, side = lax.axis_index("tile"), lax.axis_index("gz"), lax.axis_index("rep")
    sources = source_tile[:, 0, :, 0]
    shifts = block_shifts[0, 0]
    first, last = (me == 0) & (half == 0), (me == tiles - 1) & (half == 1)
    place = jnp.stack([me, half, side, first.astype(jnp.int32), last.astype(jnp.int32)])
    blocks = sources.shape[1]
    cap = MAX_NAMED if tiles == 4 else blocks
    smem = pl.BlockSpec(memory_space=pltpu.SMEM)
    vmem = pl.BlockSpec(memory_space=pltpu.VMEM)
    pack_shape = jax.ShapeDtypeStruct((cap, depth, BLK_Y, BLK_X), jnp.bfloat16)
    send_shape = jax.ShapeDtypeStruct((depth, SEND_ROWS, width), jnp.bfloat16)
    rim_shape = jax.ShapeDtypeStruct((2, depth * EDGE, width), jnp.bfloat16)
    *packs, fixed_send = pl.pallas_call(
        functools.partial(pack_kernel, tiles),
        out_shape=[pack_shape] * (tiles - 1) + [send_shape],
        in_specs=[smem, smem, vmem, vmem],
        out_specs=[vmem] * tiles,
    )(sources, place, moving_image, fixed_image)

    trio = ("tile", "gz", "rep")

    def number(t, g, r):
        return (t * 2 + g) * 2 + r

    swap = [(0, 1), (1, 0)]
    straight, slant = [], []
    for r in range(2):
        for t in range(tiles):
            for g in range(2):
                to = t + 1 if g == 0 else t - 1
                straight.append((number(t, g, r), number(to, g, r) if 0 <= to < tiles else number(t, 1 - g, r)))
                to = t - 1 if g == 0 else t + 1
                slant.append((number(t, g, r), number(to, 1 - g, r) if 0 <= to < tiles else number(t, g, 1 - r)))

    got = [
        lax.ppermute(pack, "tile", [(t, t ^ step) for t in range(tiles)])
        for step, pack in zip(range(1, tiles), packs)
    ]
    fixed_got = lax.ppermute(fixed_send, "gz", swap)
    fixed_own_n = lax.ppermute(fixed_image, "rep", swap)
    own, send, rim_straight, rim_slant = pl.pallas_call(
        functools.partial(unpack_kernel, tiles),
        out_shape=[jax.ShapeDtypeStruct(moving_image.shape, jnp.bfloat16), send_shape, rim_shape, rim_shape],
        in_specs=[smem, smem, smem] + [vmem] * (tiles + 1),
        out_specs=[vmem] * 4,
        scratch_shapes=[pltpu.VMEM((2, 2, depth * EDGE, width), jnp.float32)],
    )(sources, shifts, place, moving_image, fixed_image, *got)

    warp_got = lax.ppermute(send, "gz", swap)
    straight_got = lax.ppermute(rim_straight, trio, straight)
    slant_got = lax.ppermute(rim_slant, trio, slant)
    fixed_got_n = lax.ppermute(fixed_got, "rep", swap)
    warp_own_n = lax.ppermute(own, "rep", swap)
    warp_got_n = lax.ppermute(warp_got, "rep", swap)
    straight_n = lax.ppermute(straight_got, "rep", swap)
    slant_n = lax.ppermute(slant_got, "rep", swap)

    window = height // 2 + 2 * EDGE
    span = width + BLK_X
    row_knots, col_knots = height // SPACING, width // SPACING
    row_at = jnp.arange(window, dtype=jnp.int32)
    table_y = spline_table(half * (height // 2) - EDGE, window, -2, row_knots + 4)
    table_y = jnp.where(((row_at >= EDGE) & (row_at < window - EDGE))[:, None], table_y, 0.0).T
    table_x = spline_table(side * BLK_X, span, side * col_knots, col_knots).T
    planes = 2 * depth + 4
    part = pl.pallas_call(
        main_kernel,
        out_shape=jax.ShapeDtypeStruct((3, row_knots + 4, col_knots), jnp.float32),
        in_specs=[smem] + [vmem] * 14,
        out_specs=vmem,
        scratch_shapes=[
            pltpu.VMEM((2, planes, window, span), jnp.float32),
            pltpu.VMEM((3, planes, window, span), jnp.float32),
            pltpu.VMEM((3, window, span), jnp.float32),
        ],
    )(
        place, fixed_image, fixed_got, own, warp_got, straight_got, slant_got,
        fixed_own_n, fixed_got_n, warp_own_n, warp_got_n, straight_n, slant_n, table_y, table_x,
    )
    back = [(b, a) for a, b in straight]
    across = lax.ppermute(part, "gz", swap)
    part_straight = lax.ppermute(part, trio, back)
    part_slant = lax.ppermute(part, trio, slant)
    below = jnp.where(half == 0, part_straight, part_slant)
    above = jnp.where(half == 0, part_slant, part_straight)
    below = jnp.where(me == tiles - 1, 0.0, below[:, :2])
    above = jnp.where(me == 0, 0.0, above[:, row_knots + 2 :])
    middle = part[:, 2 : row_knots + 2] + across[:, 2 : row_knots + 2]
    return (middle + jnp.concatenate([above, below], axis=1))[:, None]


def solution(mesh):
    sizes = mesh.shape
    tiles = sizes["tile"]
    fast = sizes["gz"] == 2 and sizes["rep"] == 2 and tiles & (tiles - 1) == 0 and tiles > 1
    return jax.shard_map(
        functools.partial(fast_body, tiles) if fast else body,
        mesh=mesh,
        in_specs=(
            P(("slab", "gz"), "tile", "rep"),
            P(("slab", "gz"), "tile", "rep"),
            P("slab", "rep", None, None),
            P(("slab", "tile"), "rep", None, None),
        ),
        out_specs=P(None, "slab", "tile", "rep"),
        check_vma=False,
    )
```

```python
import functools

import jax
import jax.numpy as jnp
from jax import lax
from jax.experimental import pallas as pl
from jax.experimental.pallas import tpu as pltpu
from jax.sharding import PartitionSpec as P

BLK_Y = 16
BLK_X = 128
RAD = 2
SPACING = 16
MAX_NAMED = 4


den_floor = 1e-05

def with_halo(array, sides, width):
    for axis, dim in sides:
        count, length = (lax.axis_size(axis), array.shape[dim])
        up = [(i, (i + 1) % count) for i in range(count - 1)]
        down = [(j, i) for i, j in up]
        last = lax.slice_in_dim(array, length - width, length, axis=dim)
        first = lax.slice_in_dim(array, 0, width, axis=dim)
        before = lax.ppermute(last, axis, up)
        after = lax.ppermute(first, axis, down)
        array = jnp.concatenate([before, array, after], axis=dim)
    return array


def window_sum(extended, radius):
    result = extended
    for axis_id in range(3):
        length = result.shape[axis_id] - 2 * radius
        summed = lax.slice_in_dim(result, 0, length, axis=axis_id)
        for offset in range(1, 2 * radius + 1):
            summed = summed + lax.slice_in_dim(result, offset, offset + length, axis=axis_id)
        result = summed
    return result


def window_terms(ext_fixed, ext_warp, radius):
    volume = float((2 * radius + 1) ** 3)
    sum_fixed = window_sum(ext_fixed, radius)
    sum_warp = window_sum(ext_warp, radius)
    sum_fixed_sq = window_sum(ext_fixed * ext_fixed, radius)
    sum_warp_sq = window_sum(ext_warp * ext_warp, radius)
    sum_product = window_sum(ext_fixed * ext_warp, radius)
    cross_term = sum_product - sum_fixed * sum_warp / volume
    fixed_var = sum_fixed_sq - sum_fixed * sum_fixed / volume
    warp_var = sum_warp_sq - sum_warp * sum_warp / volume
    denominator = fixed_var * warp_var + den_floor
    term_a = 2.0 * cross_term / denominator
    term_b = -cross_term * cross_term * fixed_var / (denominator * denominator)
    term_c = -(term_a * sum_fixed + 2.0 * term_b * sum_warp) / volume
    return (term_a, term_b, term_c)


def slopes(extended, margin, extent):
    result = []
    for axis_id in range(3):
        ahead = [margin, margin, margin]
        behind = [margin, margin, margin]
        ahead[axis_id] += 1
        behind[axis_id] -= 1
        upper = lax.slice(
            extended,
            tuple(ahead),
            (ahead[0] + extent[0], ahead[1] + extent[1], ahead[2] + extent[2]),
        )
        lower = lax.slice(
            extended,
            tuple(behind),
            (behind[0] + extent[0], behind[1] + extent[1], behind[2] + extent[2]),
        )
        result.append(0.5 * (upper - lower))
    return result


def spline_table(first_pos, length, first_col, columns):
    places = first_pos + jnp.arange(length, dtype=jnp.int32)
    knots = places // SPACING
    within = (places - knots * SPACING).astype(jnp.float32) / SPACING
    squares = within * within
    cubes = squares * within
    weights = (
        (1.0 - within) ** 3 / 6.0,
        (3.0 * cubes - 6.0 * squares + 4.0) / 6.0,
        (-3.0 * cubes + 3.0 * squares + 3.0 * within + 1.0) / 6.0,
        cubes / 6.0,
    )
    targets = first_col + jnp.arange(columns, dtype=jnp.int32)
    table = jnp.zeros((length, columns), jnp.float32)
    for offset in range(4):
        table = table + jnp.where(
            targets[None, :] == (knots + offset - 1)[:, None], weights[offset][:, None], 0.0
        )
    return table


def contract(pieces, table_z, table_y, table_x):
    highest = lax.Precision.HIGHEST
    along_x = jnp.einsum("czyx,xk->czyk", pieces, table_x, precision=highest)
    along_y = jnp.einsum("czyk,yj->czjk", along_x, table_y, precision=highest)
    return jnp.einsum("czjk,zl->cljk", along_y, table_z, precision=highest)


def roll_block(block, amounts):
    return jnp.roll(jnp.roll(block, amounts[0], axis=1), amounts[1], axis=2)


def fold_rims(extended, axis_id, owned):
    middle = lax.slice_in_dim(extended, 4, owned + 4, axis=axis_id)
    leading = lax.slice_in_dim(extended, 0, 2, axis=axis_id)
    trailing = lax.slice_in_dim(extended, owned + 6, owned + 8, axis=axis_id)
    lead_pad = [(0, 0), (0, 0), (0, 0), (0, 0)]
    trail_pad = [(0, 0), (0, 0), (0, 0), (0, 0)]
    lead_pad[axis_id] = (0, owned - 2)
    trail_pad[axis_id] = (owned - 2, 0)
    return middle + jnp.pad(leading, lead_pad) + jnp.pad(trailing, trail_pad)


def body(fixed_image, moving_image, source_tile, block_shifts):
    depth, height, width = fixed_image.shape
    yblocks = height // BLK_Y
    xblocks = width // BLK_X
    block_count = yblocks * xblocks
    tile_lists = source_tile[:, 0, :, 0]
    my_tile = lax.axis_index("tile")
    own_list = lax.dynamic_index_in_dim(tile_lists, my_tile, 0, keepdims=False)
    row_steps = jnp.arange(BLK_Y, dtype=jnp.int32)
    initial = jnp.zeros((block_count, depth, BLK_Y, BLK_X), jnp.bfloat16)
    piece = lax.all_gather(moving_image, "tile", axis=1, tiled=True)
    length = piece.shape[1]
    held_blocks = []
    for block_id in range(block_count):
        row_block = block_id // xblocks
        col_block = block_id % xblocks
        wanted = own_list[block_id] * height + row_block * BLK_Y + row_steps
        usable = (wanted >= 0) & (wanted < length)
        columns_part = lax.slice_in_dim(piece, col_block * BLK_X, (col_block + 1) * BLK_X, axis=2)
        taken = jnp.take(columns_part, jnp.clip(wanted, 0, length - 1), axis=1)
        held_blocks.append(jnp.where(usable[None, :, None], taken, initial[block_id]))
    blocks = jnp.stack(held_blocks)
    rolled = jax.vmap(roll_block)(blocks, block_shifts[0, 0])
    warped = (
        rolled.reshape(yblocks, xblocks, depth, BLK_Y, BLK_X)
        .transpose(2, 0, 3, 1, 4)
        .reshape(depth, height, width)
    )
    image_pair = jnp.stack((fixed_image, warped))
    fixed_own = fixed_image.astype(jnp.float32)
    warp_own = warped.astype(jnp.float32)
    extended = with_halo(image_pair, (("tile", 2), ("gz", 1), ("rep", 3)), RAD).astype(jnp.float32)
    term_a, term_b, term_c = window_terms(extended[0], extended[1], RAD)
    terms_ext = with_halo(
        jnp.stack((term_a, term_b, term_c)).astype(jnp.bfloat16),
        (("tile", 2), ("gz", 1), ("rep", 3)),
        RAD,
    ).astype(jnp.float32)
    box_a = window_sum(terms_ext[0], RAD)
    box_b = window_sum(terms_ext[1], RAD)
    box_c = window_sum(terms_ext[2], RAD)
    margin = RAD
    gain = -(fixed_own * box_a + 2.0 * warp_own * box_b + box_c)
    slope_z, slope_y, slope_x = slopes(extended[1], margin, (depth, height, width))
    pieces = jnp.stack((gain * slope_z, gain * slope_y, gain * slope_x))
    depth_total = depth * lax.axis_size("gz")
    depth_knots = (depth_total + SPACING - 1) // SPACING
    table_z = spline_table(lax.axis_index("gz") * depth, depth, 0, depth_knots)
    row_knots = height // SPACING
    table_y = spline_table(my_tile * height, height, my_tile * row_knots - 2, row_knots + 4)
    col_knots = width // SPACING
    rep_index = lax.axis_index("rep")
    table_x = spline_table(rep_index * width, width, rep_index * col_knots - 2, col_knots + 4)
    local_grad = contract(pieces, table_z, table_y, table_x)
    spread = with_halo(local_grad, (("tile", 2), ("rep", 3)), 2)
    owned_grad = fold_rims(fold_rims(spread, 2, row_knots), 3, col_knots)
    return lax.psum(owned_grad, "gz")


EDGE = 2 * RAD
SEND_ROWS = 48


def pack_kernel(tiles, source_ref, moving_ref, fixed_ref, *out_refs):
    me, half = lax.axis_index("tile"), lax.axis_index("gz")
    packs, fixed_out = out_refs[:-1], out_refs[-1]
    height, width = moving_ref.shape[1:]
    xblocks = width // BLK_X
    blocks = (height // BLK_Y) * xblocks
    for step in range(1, tiles):
        pack = packs[step - 1]
        pack[...] = jnp.zeros_like(pack)
        other = lax.bitwise_xor(me, step)
        count = jnp.int32(0)
        for block in range(blocks):
            row, col = (block // xblocks) * BLK_Y, (block % xblocks) * BLK_X
            named = source_ref[other, block] == me

            @pl.when(named)
            def _(pack=pack, count=count, row=row, col=col):
                slot = jnp.minimum(count, pack.shape[0] - 1)
                pack[slot] = moving_ref[:, row : row + BLK_Y, col : col + BLK_X]

            count = count + named.astype(jnp.int32)
    start = pl.multiple_of((1 - half) * BLK_Y, BLK_Y)
    fixed_out[...] = fixed_ref[:, pl.ds(start, SEND_ROWS), :]


def unpack_kernel(tiles, source_ref, shift_ref, moving_ref, fixed_ref, *refs):
    recvs = refs[: tiles - 1]
    own_ref, send_ref, straight_ref, slant_ref, rims = refs[tiles - 1 :]
    me, half = lax.axis_index("tile"), lax.axis_index("gz")
    depth, height, width = moving_ref.shape
    xblocks = width // BLK_X
    blocks = (height // BLK_Y) * xblocks
    cap = recvs[0].shape[0]
    for block in range(blocks):
        row, col = (block // xblocks) * BLK_Y, (block % xblocks) * BLK_X
        source = source_ref[me, block]
        slot = jnp.int32(0)
        for earlier in range(block):
            slot = slot + (source_ref[me, earlier] == source).astype(jnp.int32)
        slot = jnp.minimum(slot, cap - 1)
        step = lax.bitwise_xor(source, me)
        value = moving_ref[:, row : row + BLK_Y, col : col + BLK_X].astype(jnp.float32)
        for other in range(1, tiles):
            value = jnp.where(step == other, recvs[other - 1][slot].astype(jnp.float32), value)
        down = lax.rem(shift_ref[block, 0], BLK_Y)
        right = lax.rem(shift_ref[block, 1], BLK_X)
        value = pltpu.roll(value, right, 2)
        for bit in (1, 2, 4, 8):
            value = jnp.where(lax.bitwise_and(down, bit) != 0, pltpu.roll(value, bit, 1), value)
        own_ref[:, row : row + BLK_Y, col : col + BLK_X] = value.astype(own_ref.dtype)
        if row == 0:
            for plane in range(depth):
                rims[1, 0, plane * EDGE : (plane + 1) * EDGE, col : col + BLK_X] = value[plane, :EDGE]
        if row == height - BLK_Y:
            for plane in range(depth):
                rims[1, 1, plane * EDGE : (plane + 1) * EDGE, col : col + BLK_X] = value[plane, -EDGE:]
    for plane in range(depth):
        top = fixed_ref[plane, :BLK_Y, :].astype(jnp.float32)
        bottom = fixed_ref[plane, height - BLK_Y :, :].astype(jnp.float32)
        rims[0, 0, plane * EDGE : (plane + 1) * EDGE, :] = top[:EDGE]
        rims[0, 1, plane * EDGE : (plane + 1) * EDGE, :] = bottom[-EDGE:]
    for image in range(2):
        straight_ref[image] = rims[image, 1 - half].astype(straight_ref.dtype)
        slant_ref[image] = rims[image, half].astype(slant_ref.dtype)
    start = pl.multiple_of((1 - half) * BLK_Y, BLK_Y)
    send_ref[...] = own_ref[:, pl.ds(start, SEND_ROWS), :]


def five(array, axis):
    size = array.shape[axis]
    pair = array + pltpu.roll(array, 1, axis)
    return pltpu.roll(pair, size - 2, axis) + pair + pltpu.roll(array, 2, axis)


def main_kernel(
    tiles, fixed_own, fixed_got, warp_own, warp_got, straight, slant,
    fixed_own_n, fixed_got_n, warp_own_n, warp_got_n, straight_n, slant_n,
    table_y, table_x, out_ref, images, rows_sum, terms, sums, band,
):
    half, side = lax.axis_index("gz"), lax.axis_index("rep")
    me = lax.axis_index("tile")
    first = jnp.where(half == 0, (me == 0).astype(jnp.int32), 0)
    last = jnp.where(half == 1, (me == tiles - 1).astype(jnp.int32), 0)
    depth = fixed_own.shape[0]
    planes = 2 * depth
    window, span = images.shape[2:]
    width = 2 * BLK_X
    own_col = pl.multiple_of(side * BLK_X, BLK_X)
    new_col = pl.multiple_of((1 - side) * width, BLK_X)
    take = pl.multiple_of(side * BLK_X, BLK_X)
    start = pl.multiple_of(half * BLK_Y, BLK_Y)
    lanes = lax.broadcasted_iota(jnp.int32, (window, span), 1)
    levels = lax.broadcasted_iota(jnp.int32, (window, span), 0)
    low_lane = jnp.where(side == 0, 0, BLK_X - 48)
    high_lane = jnp.where(side == 0, width + 32, span)
    low_row = jnp.where(first != 0, EDGE, RAD)
    high_row = jnp.where(last != 0, window - EDGE, window - RAD)
    inside = (lanes >= low_lane) & (lanes < high_lane) & (levels >= low_row) & (levels < high_row)
    near = lax.broadcasted_iota(jnp.int32, (window, BLK_X), 1)
    near = (near >= low_lane) & (near < jnp.where(side == 0, 32, BLK_X))
    zero_plane = jnp.zeros((window, span), jnp.float32)
    across = lax.broadcasted_iota(jnp.int32, (span, span), 0) - lax.broadcasted_iota(jnp.int32, (span, span), 1)
    band[...] = jnp.where(jnp.abs(across) <= RAD, 1.0, 0.0).astype(band.dtype)
    for pad in (0, 1, planes + 2, planes + 3):
        for which in range(5):
            rows_sum[which, pad] = zero_plane
        for which in range(3):
            terms[which, pad] = zero_plane
    for pad in (0, planes + 1):
        images[1, pad] = zero_plane

    def place(which, plane, value, value_n):
        images[which, plane, :, pl.ds(own_col, width)] = value
        images[which, plane, :, pl.ds(new_col, BLK_X)] = jnp.where(near, value_n, 0.0)

    def shift_in(piece):
        return pltpu.roll(piece, jnp.where(half == 0, EDGE, SEND_ROWS - BLK_Y + EDGE), 0)[:window]

    for which, (own, got, own_n, got_n) in enumerate(
        ((fixed_own, fixed_got, fixed_own_n, fixed_got_n), (warp_own, warp_got, warp_own_n, warp_got_n))
    ):
        for i in range(depth):
            mine, theirs = 1 + half * depth + i, 1 + (1 - half) * depth + i
            place(
                which, mine,
                shift_in(own[i, pl.ds(start, SEND_ROWS), :].astype(jnp.float32)),
                shift_in(own_n[i, pl.ds(start, SEND_ROWS), pl.ds(take, BLK_X)].astype(jnp.float32)),
            )
            place(
                which, theirs,
                shift_in(got[i].astype(jnp.float32)),
                shift_in(got_n[i, :, pl.ds(take, BLK_X)].astype(jnp.float32)),
            )
        outer = (first + last) != 0
        for rim, rim_n, base in ((straight, straight_n, half), (slant, slant_n, 1 - half)):
            value = jnp.where(outer, 0.0, rim[which].astype(jnp.float32))
            value_n = jnp.where(outer, 0.0, rim_n[which, :, pl.ds(take, BLK_X)].astype(jnp.float32))
            value_n = jnp.where(near[: value_n.shape[0]], value_n, 0.0)
            for i in range(depth):
                plane = 1 + base * depth + i
                for at_half, row in ((0, 0), (1, window - EDGE)):

                    @pl.when(half == at_half)
                    def _(plane=plane, row=row, i=i, value=value, value_n=value_n, which=which):
                        images[which, plane, row : row + EDGE, pl.ds(own_col, width)] = value[i * EDGE : (i + 1) * EDGE]
                        images[which, plane, row : row + EDGE, pl.ds(new_col, BLK_X)] = value_n[i * EDGE : (i + 1) * EDGE]

    volume = float((2 * RAD + 1) ** 3)

    def row_pass(z, carry):
        f, w = images[0, z + 1], images[1, z + 1]
        products = [f * f, w * w, f * w]
        low = [value - value.astype(jnp.bfloat16).astype(jnp.float32) for value in products]
        boxed = jnp.dot(
            jnp.concatenate([f, w] + products + low, axis=0).astype(jnp.bfloat16), band[...], preferred_element_type=jnp.float32
        )
        pieces = [boxed[k * window : (k + 1) * window] for k in range(8)]
        for which in range(5):
            value = pieces[which] if which < 2 else pieces[which] + pieces[which + 3]
            rows_sum[which, z + 2] = five(value, 0)
        return carry

    lax.fori_loop(0, planes, row_pass, 0, unroll=8)

    def term_pass(z, carry):
        sum_f, sum_w, sum_ff, sum_ww, sum_fw = (
            rows_sum[which, z] + rows_sum[which, z + 1] + rows_sum[which, z + 2]
            + rows_sum[which, z + 3] + rows_sum[which, z + 4]
            for which in range(5)
        )
        cross = sum_fw - sum_f * sum_w * (1.0 / volume)
        var_f = sum_ff - sum_f * sum_f * (1.0 / volume)
        var_w = sum_ww - sum_w * sum_w * (1.0 / volume)
        inverse = 1.0 / (var_f * var_w + den_floor)
        ratio = cross * inverse
        term_a = 2.0 * ratio
        term_b = -(ratio * ratio) * var_f
        term_c = -(term_a * sum_f + 2.0 * term_b * sum_w) * (1.0 / volume)
        values = [five(jnp.where(inside, value, 0.0), 0) for value in (term_a, term_b, term_c)]
        low = [value - value.astype(jnp.bfloat16).astype(jnp.float32) for value in values]
        boxed = jnp.dot(
            jnp.concatenate(values + low, axis=0).astype(jnp.bfloat16), band[...], preferred_element_type=jnp.float32
        )
        for which in range(3):
            terms[which, z + 2] = boxed[which * window : (which + 1) * window] + boxed[(which + 3) * window : (which + 4) * window]
        return carry

    lax.fori_loop(0, planes, term_pass, 0, unroll=8)
    for d in range(3):
        sums[d] = zero_plane
    owned = (levels >= EDGE) & (levels < window - EDGE)

    def gain_pass(z, carry):
        box_a, box_b, box_c = (
            terms[which, z] + terms[which, z + 1] + terms[which, z + 2] + terms[which, z + 3] + terms[which, z + 4]
            for which in range(3)
        )
        f, w = images[0, z + 1], images[1, z + 1]
        gain = -(f * box_a + 2.0 * w * box_b + box_c)
        u = z.astype(jnp.float32) * (1.0 / SPACING)
        weight = (3.0 * u * u * u - 6.0 * u * u + 4.0) * (0.5 / 6.0)
        gain = jnp.where(owned, gain, 0.0) * weight
        sums[0] += gain * (images[1, z + 2] - images[1, z])
        sums[1] += gain * (pltpu.roll(w, window - 1, 0) - pltpu.roll(w, 1, 0))
        sums[2] += gain * (pltpu.roll(w, span - 1, 1) - pltpu.roll(w, 1, 1))
        return carry

    lax.fori_loop(0, planes, gain_pass, 0, unroll=8)
    for d in range(3):
        along_x = lax.dot_general(
            sums[d], table_x[...], (((1,), (1,)), ((), ())),
            precision=lax.Precision.HIGHEST, preferred_element_type=jnp.float32,
        )
        out_ref[d] = lax.dot_general(
            table_y[...], along_x, (((1,), (0,)), ((), ())),
            precision=lax.Precision.HIGHEST, preferred_element_type=jnp.float32,
        )


def held(array, space=pltpu.VMEM):
    return pltpu.with_memory_space_constraint(array, space)


def local_kernel(kernel, shapes, dtype, scalars, arrays, scratch=()):
    smem, vmem = (pl.BlockSpec(memory_space=space) for space in (pltpu.SMEM, pltpu.VMEM))
    return pl.pallas_call(
        kernel,
        out_shape=[pltpu.VMEM(shape, dtype) for shape in shapes],
        in_specs=[smem] * len(scalars) + [vmem] * len(arrays),
        out_specs=[vmem] * len(shapes),
        scratch_shapes=list(scratch),
    )(*scalars, *(held(array) for array in arrays))


def fast_body(tiles, fixed_image, moving_image, source_tile, block_shifts):
    depth, height, width = fixed_image.shape
    me, half, side = lax.axis_index("tile"), lax.axis_index("gz"), lax.axis_index("rep")
    sources = source_tile[:, 0, :, 0]
    shifts = block_shifts[0, 0]
    blocks = sources.shape[1]
    cap = MAX_NAMED if tiles == 4 else blocks
    pack_shape = (cap, depth, BLK_Y, BLK_X)
    send_shape = (depth, SEND_ROWS, width)
    rim_shape = (2, depth * EDGE, width)
    sources, shifts = held(sources, pltpu.SMEM), held(shifts, pltpu.SMEM)
    moving_image, fixed_image = held(moving_image), held(fixed_image)
    *packs, fixed_send = local_kernel(
        functools.partial(pack_kernel, tiles),
        [pack_shape] * (tiles - 1) + [send_shape],
        jnp.bfloat16,
        [sources],
        [moving_image, fixed_image],
    )

    trio = ("tile", "gz", "rep")

    def number(t, g, r):
        return (t * 2 + g) * 2 + r

    swap = [(0, 1), (1, 0)]
    straight, slant = [], []
    for r in range(2):
        for t in range(tiles):
            for g in range(2):
                to = t + 1 if g == 0 else t - 1
                straight.append((number(t, g, r), number(to, g, r) if 0 <= to < tiles else number(t, 1 - g, r)))
                to = t - 1 if g == 0 else t + 1
                slant.append((number(t, g, r), number(to, 1 - g, r) if 0 <= to < tiles else number(t, g, 1 - r)))

    got = [
        lax.ppermute(pack, "tile", [(t, t ^ step) for t in range(tiles)])
        for step, pack in zip(range(1, tiles), packs)
    ]
    fixed_got = lax.ppermute(fixed_send, "gz", swap)
    fixed_own_n = lax.ppermute(fixed_image, "rep", swap)
    own, send, rim_straight, rim_slant = local_kernel(
        functools.partial(unpack_kernel, tiles),
        [moving_image.shape, send_shape, rim_shape, rim_shape],
        jnp.bfloat16,
        [sources, shifts],
        [moving_image, fixed_image, *got],
        [pltpu.VMEM((2, 2, depth * EDGE, width), jnp.float32)],
    )

    warp_got = lax.ppermute(send, "gz", swap)
    straight_got = lax.ppermute(rim_straight, trio, straight)
    slant_got = lax.ppermute(rim_slant, trio, slant)
    fixed_got_n = lax.ppermute(fixed_got, "rep", swap)
    warp_own_n = lax.ppermute(own, "rep", swap)
    warp_got_n = lax.ppermute(warp_got, "rep", swap)
    straight_n = lax.ppermute(straight_got, "rep", swap)
    slant_n = lax.ppermute(slant_got, "rep", swap)

    window = height // 2 + 2 * EDGE
    span = width + BLK_X
    row_knots, col_knots = height // SPACING, width // SPACING
    row_at = jnp.arange(window, dtype=jnp.int32)
    table_y = spline_table(half * (height // 2) - EDGE, window, -2, row_knots + 4)
    table_y = jnp.where(((row_at >= EDGE) & (row_at < window - EDGE))[:, None], table_y, 0.0).T
    table_x = spline_table(side * BLK_X, span, side * col_knots, col_knots).T
    planes = 2 * depth
    part, = local_kernel(
        functools.partial(main_kernel, tiles),
        [(3, row_knots + 4, col_knots)],
        jnp.float32,
        [],
        [
            fixed_image, fixed_got, own, warp_got, straight_got, slant_got,
            fixed_own_n, fixed_got_n, warp_own_n, warp_got_n, straight_n, slant_n, table_y, table_x,
        ],
        [
            pltpu.VMEM((2, planes + 2, window, span), jnp.float32),
            pltpu.VMEM((5, planes + 4, window, span), jnp.float32),
            pltpu.VMEM((3, planes + 4, window, span), jnp.float32),
            pltpu.VMEM((3, window, span), jnp.float32),
            pltpu.VMEM((span, span), jnp.bfloat16),
        ],
    )
    back = [(b, a) for a, b in straight]
    across = lax.ppermute(part, "gz", swap)
    part_straight = lax.ppermute(part, trio, back)
    part_slant = lax.ppermute(part, trio, slant)
    below = jnp.where(half == 0, part_straight, part_slant)
    above = jnp.where(half == 0, part_slant, part_straight)
    below = jnp.where(me == tiles - 1, 0.0, below[:, :2])
    above = jnp.where(me == 0, 0.0, above[:, row_knots + 2 :])
    middle = part[:, 2 : row_knots + 2] + across[:, 2 : row_knots + 2]
    return (middle + jnp.concatenate([above, below], axis=1))[:, None]


def solution(mesh):
    sizes = mesh.shape
    tiles = sizes["tile"]
    fast = sizes["gz"] == 2 and sizes["rep"] == 2 and tiles & (tiles - 1) == 0 and tiles > 1
    return jax.shard_map(
        functools.partial(fast_body, tiles) if fast else body,
        mesh=mesh,
        in_specs=(
            P(("slab", "gz"), "tile", "rep"),
            P(("slab", "gz"), "tile", "rep"),
            P("slab", "rep", None, None),
            P(("slab", "tile"), "rep", None, None),
        ),
        out_specs=P(None, "slab", "tile", "rep"),
        check_vma=False,
    )
```

```python
import functools

import jax
import jax.numpy as jnp
from jax import lax
from jax.experimental import pallas as pl
from jax.experimental.pallas import tpu as pltpu
from jax.sharding import PartitionSpec as P

BLK_Y = 16
BLK_X = 128
RAD = 2
SPACING = 16
MAX_NAMED = 4


den_floor = 1e-05

def with_halo(array, sides, width):
    for axis, dim in sides:
        count, length = (lax.axis_size(axis), array.shape[dim])
        up = [(i, (i + 1) % count) for i in range(count - 1)]
        down = [(j, i) for i, j in up]
        last = lax.slice_in_dim(array, length - width, length, axis=dim)
        first = lax.slice_in_dim(array, 0, width, axis=dim)
        before = lax.ppermute(last, axis, up)
        after = lax.ppermute(first, axis, down)
        array = jnp.concatenate([before, array, after], axis=dim)
    return array


def window_sum(extended, radius):
    result = extended
    for axis_id in range(3):
        length = result.shape[axis_id] - 2 * radius
        summed = lax.slice_in_dim(result, 0, length, axis=axis_id)
        for offset in range(1, 2 * radius + 1):
            summed = summed + lax.slice_in_dim(result, offset, offset + length, axis=axis_id)
        result = summed
    return result


def window_terms(ext_fixed, ext_warp, radius):
    volume = float((2 * radius + 1) ** 3)
    sum_fixed = window_sum(ext_fixed, radius)
    sum_warp = window_sum(ext_warp, radius)
    sum_fixed_sq = window_sum(ext_fixed * ext_fixed, radius)
    sum_warp_sq = window_sum(ext_warp * ext_warp, radius)
    sum_product = window_sum(ext_fixed * ext_warp, radius)
    cross_term = sum_product - sum_fixed * sum_warp / volume
    fixed_var = sum_fixed_sq - sum_fixed * sum_fixed / volume
    warp_var = sum_warp_sq - sum_warp * sum_warp / volume
    denominator = fixed_var * warp_var + den_floor
    term_a = 2.0 * cross_term / denominator
    term_b = -cross_term * cross_term * fixed_var / (denominator * denominator)
    term_c = -(term_a * sum_fixed + 2.0 * term_b * sum_warp) / volume
    return (term_a, term_b, term_c)


def slopes(extended, margin, extent):
    result = []
    for axis_id in range(3):
        ahead = [margin, margin, margin]
        behind = [margin, margin, margin]
        ahead[axis_id] += 1
        behind[axis_id] -= 1
        upper = lax.slice(
            extended,
            tuple(ahead),
            (ahead[0] + extent[0], ahead[1] + extent[1], ahead[2] + extent[2]),
        )
        lower = lax.slice(
            extended,
            tuple(behind),
            (behind[0] + extent[0], behind[1] + extent[1], behind[2] + extent[2]),
        )
        result.append(0.5 * (upper - lower))
    return result


def spline_table(first_pos, length, first_col, columns):
    places = first_pos + jnp.arange(length, dtype=jnp.int32)
    knots = places // SPACING
    within = (places - knots * SPACING).astype(jnp.float32) / SPACING
    squares = within * within
    cubes = squares * within
    weights = (
        (1.0 - within) ** 3 / 6.0,
        (3.0 * cubes - 6.0 * squares + 4.0) / 6.0,
        (-3.0 * cubes + 3.0 * squares + 3.0 * within + 1.0) / 6.0,
        cubes / 6.0,
    )
    targets = first_col + jnp.arange(columns, dtype=jnp.int32)
    table = jnp.zeros((length, columns), jnp.float32)
    for offset in range(4):
        table = table + jnp.where(
            targets[None, :] == (knots + offset - 1)[:, None], weights[offset][:, None], 0.0
        )
    return table


def contract(pieces, table_z, table_y, table_x):
    highest = lax.Precision.HIGHEST
    along_x = jnp.einsum("czyx,xk->czyk", pieces, table_x, precision=highest)
    along_y = jnp.einsum("czyk,yj->czjk", along_x, table_y, precision=highest)
    return jnp.einsum("czjk,zl->cljk", along_y, table_z, precision=highest)


def roll_block(block, amounts):
    return jnp.roll(jnp.roll(block, amounts[0], axis=1), amounts[1], axis=2)


def fold_rims(extended, axis_id, owned):
    middle = lax.slice_in_dim(extended, 4, owned + 4, axis=axis_id)
    leading = lax.slice_in_dim(extended, 0, 2, axis=axis_id)
    trailing = lax.slice_in_dim(extended, owned + 6, owned + 8, axis=axis_id)
    lead_pad = [(0, 0), (0, 0), (0, 0), (0, 0)]
    trail_pad = [(0, 0), (0, 0), (0, 0), (0, 0)]
    lead_pad[axis_id] = (0, owned - 2)
    trail_pad[axis_id] = (owned - 2, 0)
    return middle + jnp.pad(leading, lead_pad) + jnp.pad(trailing, trail_pad)


def body(fixed_image, moving_image, source_tile, block_shifts):
    depth, height, width = fixed_image.shape
    yblocks = height // BLK_Y
    xblocks = width // BLK_X
    block_count = yblocks * xblocks
    tile_lists = source_tile[:, 0, :, 0]
    my_tile = lax.axis_index("tile")
    own_list = lax.dynamic_index_in_dim(tile_lists, my_tile, 0, keepdims=False)
    row_steps = jnp.arange(BLK_Y, dtype=jnp.int32)
    initial = jnp.zeros((block_count, depth, BLK_Y, BLK_X), jnp.bfloat16)
    piece = lax.all_gather(moving_image, "tile", axis=1, tiled=True)
    length = piece.shape[1]
    held_blocks = []
    for block_id in range(block_count):
        row_block = block_id // xblocks
        col_block = block_id % xblocks
        wanted = own_list[block_id] * height + row_block * BLK_Y + row_steps
        usable = (wanted >= 0) & (wanted < length)
        columns_part = lax.slice_in_dim(piece, col_block * BLK_X, (col_block + 1) * BLK_X, axis=2)
        taken = jnp.take(columns_part, jnp.clip(wanted, 0, length - 1), axis=1)
        held_blocks.append(jnp.where(usable[None, :, None], taken, initial[block_id]))
    blocks = jnp.stack(held_blocks)
    rolled = jax.vmap(roll_block)(blocks, block_shifts[0, 0])
    warped = (
        rolled.reshape(yblocks, xblocks, depth, BLK_Y, BLK_X)
        .transpose(2, 0, 3, 1, 4)
        .reshape(depth, height, width)
    )
    image_pair = jnp.stack((fixed_image, warped))
    fixed_own = fixed_image.astype(jnp.float32)
    warp_own = warped.astype(jnp.float32)
    extended = with_halo(image_pair, (("tile", 2), ("gz", 1), ("rep", 3)), RAD).astype(jnp.float32)
    term_a, term_b, term_c = window_terms(extended[0], extended[1], RAD)
    terms_ext = with_halo(
        jnp.stack((term_a, term_b, term_c)).astype(jnp.bfloat16),
        (("tile", 2), ("gz", 1), ("rep", 3)),
        RAD,
    ).astype(jnp.float32)
    box_a = window_sum(terms_ext[0], RAD)
    box_b = window_sum(terms_ext[1], RAD)
    box_c = window_sum(terms_ext[2], RAD)
    margin = RAD
    gain = -(fixed_own * box_a + 2.0 * warp_own * box_b + box_c)
    slope_z, slope_y, slope_x = slopes(extended[1], margin, (depth, height, width))
    pieces = jnp.stack((gain * slope_z, gain * slope_y, gain * slope_x))
    depth_total = depth * lax.axis_size("gz")
    depth_knots = (depth_total + SPACING - 1) // SPACING
    table_z = spline_table(lax.axis_index("gz") * depth, depth, 0, depth_knots)
    row_knots = height // SPACING
    table_y = spline_table(my_tile * height, height, my_tile * row_knots - 2, row_knots + 4)
    col_knots = width // SPACING
    rep_index = lax.axis_index("rep")
    table_x = spline_table(rep_index * width, width, rep_index * col_knots - 2, col_knots + 4)
    local_grad = contract(pieces, table_z, table_y, table_x)
    spread = with_halo(local_grad, (("tile", 2), ("rep", 3)), 2)
    owned_grad = fold_rims(fold_rims(spread, 2, row_knots), 3, col_knots)
    return lax.psum(owned_grad, "gz")


EDGE = 2 * RAD
SEND_ROWS = 48


def pack_kernel(tiles, source_ref, moving_ref, fixed_ref, *out_refs):
    packs, moving_out, fixed_out = out_refs[:-2], out_refs[-2], out_refs[-1]
    moving_out[...] = moving_ref[...]
    fixed_out[...] = fixed_ref[...]
    me = lax.axis_index("tile")
    height, width = moving_ref.shape[1:]
    xblocks = width // BLK_X
    blocks = (height // BLK_Y) * xblocks
    cap = packs[0].shape[0]
    for step in range(1, tiles):
        other = lax.bitwise_xor(me, step)
        count = jnp.int32(0)
        chosen = [jnp.int32(0)] * cap
        for block in range(blocks):
            named = source_ref[other, block] == me
            chosen = [jnp.where(named & (count == slot), block, old) for slot, old in enumerate(chosen)]
            count = count + named.astype(jnp.int32)
        for slot, block in enumerate(chosen):
            row = pl.multiple_of(block // xblocks * BLK_Y, BLK_Y)
            col = pl.multiple_of(lax.rem(block, xblocks) * BLK_X, BLK_X)
            packs[step - 1][slot] = moving_ref[:, pl.ds(row, BLK_Y), pl.ds(col, BLK_X)]


def unpack_kernel(tiles, source_ref, shift_ref, moving_ref, fixed_ref, *refs):
    recvs = refs[: tiles - 1]
    own_ref, send_ref, straight_ref, slant_ref, rims = refs[tiles - 1 :]
    me, half = lax.axis_index("tile"), lax.axis_index("gz")
    depth, height, width = moving_ref.shape
    xblocks = width // BLK_X
    blocks = (height // BLK_Y) * xblocks
    cap = recvs[0].shape[0]
    for block in range(blocks):
        row, col = (block // xblocks) * BLK_Y, (block % xblocks) * BLK_X
        source = source_ref[me, block]
        slot = jnp.int32(0)
        for earlier in range(block):
            slot = slot + (source_ref[me, earlier] == source).astype(jnp.int32)
        slot = jnp.minimum(slot, cap - 1)
        step = lax.bitwise_xor(source, me)
        value = moving_ref[:, row : row + BLK_Y, col : col + BLK_X].astype(jnp.float32)
        for other in range(1, tiles):
            value = jnp.where(step == other, recvs[other - 1][slot].astype(jnp.float32), value)
        down = lax.rem(shift_ref[block, 0], BLK_Y)
        right = lax.rem(shift_ref[block, 1], BLK_X)
        value = pltpu.roll(value, right, 2)
        for bit in (1, 2, 4, 8):
            value = jnp.where(lax.bitwise_and(down, bit) != 0, pltpu.roll(value, bit, 1), value)
        own_ref[:, row : row + BLK_Y, col : col + BLK_X] = value.astype(own_ref.dtype)
        if row == 0:
            for plane in range(depth):
                rims[1, 0, plane * EDGE : (plane + 1) * EDGE, col : col + BLK_X] = value[plane, :EDGE]
        if row == height - BLK_Y:
            for plane in range(depth):
                rims[1, 1, plane * EDGE : (plane + 1) * EDGE, col : col + BLK_X] = value[plane, -EDGE:]
    for plane in range(depth):
        top = fixed_ref[plane, :BLK_Y, :].astype(jnp.float32)
        bottom = fixed_ref[plane, height - BLK_Y :, :].astype(jnp.float32)
        rims[0, 0, plane * EDGE : (plane + 1) * EDGE, :] = top[:EDGE]
        rims[0, 1, plane * EDGE : (plane + 1) * EDGE, :] = bottom[-EDGE:]
    for image in range(2):
        straight_ref[image] = rims[image, 1 - half].astype(straight_ref.dtype)
        slant_ref[image] = rims[image, half].astype(slant_ref.dtype)
    start = pl.multiple_of((1 - half) * BLK_Y, BLK_Y)
    send_ref[...] = own_ref[:, pl.ds(start, SEND_ROWS), :]


def five(array, axis):
    size = array.shape[axis]
    pair = array + pltpu.roll(array, 1, axis)
    return pltpu.roll(pair, size - 2, axis) + pair + pltpu.roll(array, 2, axis)


def main_kernel(
    tiles, fixed_own, fixed_got, warp_own, warp_got, straight, slant,
    fixed_own_n, fixed_got_n, warp_own_n, warp_got_n, straight_n, slant_n,
    table_y, table_x, out_ref, images, rows_sum, terms, sums, band,
):
    half, side = lax.axis_index("gz"), lax.axis_index("rep")
    me = lax.axis_index("tile")
    first = jnp.where(half == 0, (me == 0).astype(jnp.int32), 0)
    last = jnp.where(half == 1, (me == tiles - 1).astype(jnp.int32), 0)
    depth = fixed_own.shape[0]
    planes = 2 * depth
    window, span = images.shape[2:]
    width = 2 * BLK_X
    own_col = pl.multiple_of(side * BLK_X, BLK_X)
    new_col = pl.multiple_of((1 - side) * width, BLK_X)
    take = pl.multiple_of(side * BLK_X, BLK_X)
    start = pl.multiple_of(half * BLK_Y, BLK_Y)
    lanes = lax.broadcasted_iota(jnp.int32, (window, span), 1)
    levels = lax.broadcasted_iota(jnp.int32, (window, span), 0)
    low_lane = jnp.where(side == 0, 0, BLK_X - 48)
    high_lane = jnp.where(side == 0, width + 32, span)
    low_row = jnp.where(first != 0, EDGE, RAD)
    high_row = jnp.where(last != 0, window - EDGE, window - RAD)
    inside = (lanes >= low_lane) & (lanes < high_lane) & (levels >= low_row) & (levels < high_row)
    near = lax.broadcasted_iota(jnp.int32, (window, BLK_X), 1)
    near = (near >= low_lane) & (near < jnp.where(side == 0, 32, BLK_X))
    zero_plane = jnp.zeros((window, span), jnp.float32)
    across = lax.broadcasted_iota(jnp.int32, (span, span), 0) - lax.broadcasted_iota(jnp.int32, (span, span), 1)
    band[...] = jnp.where(jnp.abs(across) <= RAD, 1.0, 0.0).astype(band.dtype)
    for pad in (0, 1, planes + 2, planes + 3):
        for which in range(5):
            rows_sum[which, pad] = zero_plane
        for which in range(3):
            terms[which, pad] = zero_plane
    for pad in (0, planes + 1):
        images[1, pad] = zero_plane

    def place(which, plane, value, value_n):
        images[which, plane, :, pl.ds(own_col, width)] = value
        images[which, plane, :, pl.ds(new_col, BLK_X)] = jnp.where(near, value_n, 0.0)

    def shift_in(piece):
        return pltpu.roll(piece, jnp.where(half == 0, EDGE, SEND_ROWS - BLK_Y + EDGE), 0)[:window]

    for which, (own, got, own_n, got_n) in enumerate(
        ((fixed_own, fixed_got, fixed_own_n, fixed_got_n), (warp_own, warp_got, warp_own_n, warp_got_n))
    ):
        for i in range(depth):
            mine, theirs = 1 + half * depth + i, 1 + (1 - half) * depth + i
            place(
                which, mine,
                shift_in(own[i, pl.ds(start, SEND_ROWS), :].astype(jnp.float32)),
                shift_in(own_n[i, pl.ds(start, SEND_ROWS), pl.ds(take, BLK_X)].astype(jnp.float32)),
            )
            place(
                which, theirs,
                shift_in(got[i, pl.ds(start if which == 0 else 0, SEND_ROWS), :].astype(jnp.float32)),
                shift_in(got_n[i, pl.ds(start if which == 0 else 0, SEND_ROWS), pl.ds(take, BLK_X)].astype(jnp.float32)),
            )
        outer = (first + last) != 0
        for rim, rim_n, base in ((straight, straight_n, half), (slant, slant_n, 1 - half)):
            value = jnp.where(outer, 0.0, rim[which].astype(jnp.float32))
            value_n = jnp.where(outer, 0.0, rim_n[which, :, pl.ds(take, BLK_X)].astype(jnp.float32))
            value_n = jnp.where(near[: value_n.shape[0]], value_n, 0.0)
            for i in range(depth):
                plane = 1 + base * depth + i
                for at_half, row in ((0, 0), (1, window - EDGE)):

                    @pl.when(half == at_half)
                    def _(plane=plane, row=row, i=i, value=value, value_n=value_n, which=which):
                        images[which, plane, row : row + EDGE, pl.ds(own_col, width)] = value[i * EDGE : (i + 1) * EDGE]
                        images[which, plane, row : row + EDGE, pl.ds(new_col, BLK_X)] = value_n[i * EDGE : (i + 1) * EDGE]

    volume = float((2 * RAD + 1) ** 3)

    def row_pass(z, carry):
        f, w = images[0, z + 1], images[1, z + 1]
        products = [f * f, w * w, f * w]
        low = [value - value.astype(jnp.bfloat16).astype(jnp.float32) for value in products]
        boxed = jnp.dot(
            jnp.concatenate([f, w] + products + low, axis=0).astype(jnp.bfloat16), band[...], preferred_element_type=jnp.float32
        )
        pieces = [boxed[k * window : (k + 1) * window] for k in range(8)]
        for which in range(5):
            value = pieces[which] if which < 2 else pieces[which] + pieces[which + 3]
            rows_sum[which, z + 2] = five(value, 0)
        return carry

    lax.fori_loop(0, planes, row_pass, 0, unroll=8)

    def term_pass(z, carry):
        sum_f, sum_w, sum_ff, sum_ww, sum_fw = (
            rows_sum[which, z] + rows_sum[which, z + 1] + rows_sum[which, z + 2]
            + rows_sum[which, z + 3] + rows_sum[which, z + 4]
            for which in range(5)
        )
        cross = sum_fw - sum_f * sum_w * (1.0 / volume)
        var_f = sum_ff - sum_f * sum_f * (1.0 / volume)
        var_w = sum_ww - sum_w * sum_w * (1.0 / volume)
        inverse = 1.0 / (var_f * var_w + den_floor)
        ratio = cross * inverse
        term_a = 2.0 * ratio
        term_b = -(ratio * ratio) * var_f
        term_c = -(term_a * sum_f + 2.0 * term_b * sum_w) * (1.0 / volume)
        values = [five(jnp.where(inside, value, 0.0), 0) for value in (term_a, term_b, term_c)]
        low = [value - value.astype(jnp.bfloat16).astype(jnp.float32) for value in values]
        boxed = jnp.dot(
            jnp.concatenate(values + low, axis=0).astype(jnp.bfloat16), band[...], preferred_element_type=jnp.float32
        )
        for which in range(3):
            terms[which, z + 2] = boxed[which * window : (which + 1) * window] + boxed[(which + 3) * window : (which + 4) * window]
        return carry

    lax.fori_loop(0, planes, term_pass, 0, unroll=8)
    for d in range(3):
        sums[d] = zero_plane
    owned = (levels >= EDGE) & (levels < window - EDGE)

    def gain_pass(z, carry):
        box_a, box_b, box_c = (
            terms[which, z] + terms[which, z + 1] + terms[which, z + 2] + terms[which, z + 3] + terms[which, z + 4]
            for which in range(3)
        )
        f, w = images[0, z + 1], images[1, z + 1]
        gain = -(f * box_a + 2.0 * w * box_b + box_c)
        u = z.astype(jnp.float32) * (1.0 / SPACING)
        weight = (3.0 * u * u * u - 6.0 * u * u + 4.0) * (0.5 / 6.0)
        gain = jnp.where(owned, gain, 0.0) * weight
        sums[0] += gain * (images[1, z + 2] - images[1, z])
        sums[1] += gain * (pltpu.roll(w, window - 1, 0) - pltpu.roll(w, 1, 0))
        sums[2] += gain * (pltpu.roll(w, span - 1, 1) - pltpu.roll(w, 1, 1))
        return carry

    lax.fori_loop(0, planes, gain_pass, 0, unroll=8)
    for d in range(3):
        along_x = lax.dot_general(
            sums[d], table_x[...], (((1,), (1,)), ((), ())),
            precision=lax.Precision.HIGHEST, preferred_element_type=jnp.float32,
        )
        out_ref[d] = lax.dot_general(
            table_y[...], along_x, (((1,), (0,)), ((), ())),
            precision=lax.Precision.HIGHEST, preferred_element_type=jnp.float32,
        )


def local_kernel(kernel, shapes, dtype, arrays, scratch=()):
    vmem = pl.BlockSpec(memory_space=pltpu.VMEM)
    return pl.pallas_call(
        kernel,
        out_shape=[pltpu.VMEM(shape, dtype) for shape in shapes],
        in_specs=[vmem] * len(arrays),
        out_specs=[vmem] * len(shapes),
        scratch_shapes=list(scratch),
    )(*(pltpu.with_memory_space_constraint(array, pltpu.VMEM) for array in arrays))


def fast_body(tiles, fixed_image, moving_image, source_tile, block_shifts):
    depth, height, width = fixed_image.shape
    me, half, side = lax.axis_index("tile"), lax.axis_index("gz"), lax.axis_index("rep")
    sources = source_tile[:, 0, :, 0]
    shifts = block_shifts[0, 0]
    blocks = sources.shape[1]
    cap = MAX_NAMED if tiles == 4 else blocks
    pack_shape = (cap, depth, BLK_Y, BLK_X)
    send_shape = (depth, SEND_ROWS, width)
    rim_shape = (2, depth * EDGE, width)
    smem, vmem = (pl.BlockSpec(memory_space=space) for space in (pltpu.SMEM, pltpu.VMEM))
    *packs, moving_image, fixed_image = pl.pallas_call(
        functools.partial(pack_kernel, tiles),
        out_shape=[pltpu.VMEM(pack_shape, jnp.bfloat16)] * (tiles - 1)
        + [pltpu.VMEM(moving_image.shape, jnp.bfloat16)] * 2,
        in_specs=[smem, vmem, vmem],
        out_specs=[vmem] * (tiles + 1),
    )(sources, moving_image, fixed_image)

    trio = ("tile", "gz", "rep")

    def number(t, g, r):
        return (t * 2 + g) * 2 + r

    swap = [(0, 1), (1, 0)]
    straight, slant = [], []
    for r in range(2):
        for t in range(tiles):
            for g in range(2):
                to = t + 1 if g == 0 else t - 1
                straight.append((number(t, g, r), number(to, g, r) if 0 <= to < tiles else number(t, 1 - g, r)))
                to = t - 1 if g == 0 else t + 1
                slant.append((number(t, g, r), number(to, 1 - g, r) if 0 <= to < tiles else number(t, g, 1 - r)))

    got = [
        lax.ppermute(pack, "tile", [(t, t ^ step) for t in range(tiles)])
        for step, pack in zip(range(1, tiles), packs)
    ]
    fixed_got = lax.ppermute(fixed_image, "gz", swap)
    fixed_own_n = lax.ppermute(fixed_image, "rep", swap)
    own, send, rim_straight, rim_slant = local_kernel(
        functools.partial(unpack_kernel, tiles),
        [moving_image.shape, send_shape, rim_shape, rim_shape],
        jnp.bfloat16,
        [sources, shifts, moving_image, fixed_image, *got],
        [pltpu.VMEM((2, 2, depth * EDGE, width), jnp.float32)],
    )

    warp_got = lax.ppermute(send, "gz", swap)
    straight_got = lax.ppermute(rim_straight, trio, straight)
    slant_got = lax.ppermute(rim_slant, trio, slant)
    fixed_got_n = lax.ppermute(fixed_got, "rep", swap)
    warp_own_n = lax.ppermute(own, "rep", swap)
    warp_got_n = lax.ppermute(warp_got, "rep", swap)
    straight_n = lax.ppermute(straight_got, "rep", swap)
    slant_n = lax.ppermute(slant_got, "rep", swap)

    window = height // 2 + 2 * EDGE
    span = width + BLK_X
    row_knots, col_knots = height // SPACING, width // SPACING
    row_at = jnp.arange(window, dtype=jnp.int32)
    table_y = spline_table(half * (height // 2) - EDGE, window, -2, row_knots + 4)
    table_y = jnp.where(((row_at >= EDGE) & (row_at < window - EDGE))[:, None], table_y, 0.0).T
    table_x = spline_table(side * BLK_X, span, side * col_knots, col_knots).T
    planes = 2 * depth
    part, = local_kernel(
        functools.partial(main_kernel, tiles),
        [(3, row_knots + 4, col_knots)],
        jnp.float32,
        [
            fixed_image, fixed_got, own, warp_got, straight_got, slant_got,
            fixed_own_n, fixed_got_n, warp_own_n, warp_got_n, straight_n, slant_n, table_y, table_x,
        ],
        [
            pltpu.VMEM((2, planes + 2, window, span), jnp.float32),
            pltpu.VMEM((5, planes + 4, window, span), jnp.float32),
            pltpu.VMEM((3, planes + 4, window, span), jnp.float32),
            pltpu.VMEM((3, window, span), jnp.float32),
            pltpu.VMEM((span, span), jnp.bfloat16),
        ],
    )
    back = [(b, a) for a, b in straight]
    across = lax.ppermute(part, "gz", swap)
    part_straight = lax.ppermute(part, trio, back)
    part_slant = lax.ppermute(part, trio, slant)
    below = jnp.where(half == 0, part_straight, part_slant)
    above = jnp.where(half == 0, part_slant, part_straight)
    below = jnp.where(me == tiles - 1, 0.0, below[:, :2])
    above = jnp.where(me == 0, 0.0, above[:, row_knots + 2 :])
    middle = part[:, 2 : row_knots + 2] + across[:, 2 : row_knots + 2]
    return (middle + jnp.concatenate([above, below], axis=1))[:, None]


def solution(mesh):
    sizes = mesh.shape
    tiles = sizes["tile"]
    fast = sizes["gz"] == 2 and sizes["rep"] == 2 and tiles & (tiles - 1) == 0 and tiles > 1
    return jax.shard_map(
        functools.partial(fast_body, tiles) if fast else body,
        mesh=mesh,
        in_specs=(
            P(("slab", "gz"), "tile", "rep"),
            P(("slab", "gz"), "tile", "rep"),
            P("slab", "rep", None, None),
            P(("slab", "tile"), "rep", None, None),
        ),
        out_specs=P(None, "slab", "tile", "rep"),
        check_vma=False,
    )
```

```python
import functools

import jax
import jax.numpy as jnp
from jax import lax
from jax.experimental import pallas as pl
from jax.experimental.pallas import tpu as pltpu
from jax.sharding import PartitionSpec as P

BLK_Y = 16
BLK_X = 128
RAD = 2
SPACING = 16
MAX_NAMED = 4


den_floor = 1e-05

def with_halo(array, sides, width):
    for axis, dim in sides:
        count, length = (lax.axis_size(axis), array.shape[dim])
        up = [(i, (i + 1) % count) for i in range(count - 1)]
        down = [(j, i) for i, j in up]
        last = lax.slice_in_dim(array, length - width, length, axis=dim)
        first = lax.slice_in_dim(array, 0, width, axis=dim)
        before = lax.ppermute(last, axis, up)
        after = lax.ppermute(first, axis, down)
        array = jnp.concatenate([before, array, after], axis=dim)
    return array


def window_sum(extended, radius):
    result = extended
    for axis_id in range(3):
        length = result.shape[axis_id] - 2 * radius
        summed = lax.slice_in_dim(result, 0, length, axis=axis_id)
        for offset in range(1, 2 * radius + 1):
            summed = summed + lax.slice_in_dim(result, offset, offset + length, axis=axis_id)
        result = summed
    return result


def window_terms(ext_fixed, ext_warp, radius):
    volume = float((2 * radius + 1) ** 3)
    sum_fixed = window_sum(ext_fixed, radius)
    sum_warp = window_sum(ext_warp, radius)
    sum_fixed_sq = window_sum(ext_fixed * ext_fixed, radius)
    sum_warp_sq = window_sum(ext_warp * ext_warp, radius)
    sum_product = window_sum(ext_fixed * ext_warp, radius)
    cross_term = sum_product - sum_fixed * sum_warp / volume
    fixed_var = sum_fixed_sq - sum_fixed * sum_fixed / volume
    warp_var = sum_warp_sq - sum_warp * sum_warp / volume
    denominator = fixed_var * warp_var + den_floor
    term_a = 2.0 * cross_term / denominator
    term_b = -cross_term * cross_term * fixed_var / (denominator * denominator)
    term_c = -(term_a * sum_fixed + 2.0 * term_b * sum_warp) / volume
    return (term_a, term_b, term_c)


def slopes(extended, margin, extent):
    result = []
    for axis_id in range(3):
        ahead = [margin, margin, margin]
        behind = [margin, margin, margin]
        ahead[axis_id] += 1
        behind[axis_id] -= 1
        upper = lax.slice(
            extended,
            tuple(ahead),
            (ahead[0] + extent[0], ahead[1] + extent[1], ahead[2] + extent[2]),
        )
        lower = lax.slice(
            extended,
            tuple(behind),
            (behind[0] + extent[0], behind[1] + extent[1], behind[2] + extent[2]),
        )
        result.append(0.5 * (upper - lower))
    return result


def spline_table(first_pos, length, first_col, columns):
    places = first_pos + jnp.arange(length, dtype=jnp.int32)
    knots = places // SPACING
    within = (places - knots * SPACING).astype(jnp.float32) / SPACING
    squares = within * within
    cubes = squares * within
    weights = (
        (1.0 - within) ** 3 / 6.0,
        (3.0 * cubes - 6.0 * squares + 4.0) / 6.0,
        (-3.0 * cubes + 3.0 * squares + 3.0 * within + 1.0) / 6.0,
        cubes / 6.0,
    )
    targets = first_col + jnp.arange(columns, dtype=jnp.int32)
    table = jnp.zeros((length, columns), jnp.float32)
    for offset in range(4):
        table = table + jnp.where(
            targets[None, :] == (knots + offset - 1)[:, None], weights[offset][:, None], 0.0
        )
    return table


def contract(pieces, table_z, table_y, table_x):
    highest = lax.Precision.HIGHEST
    along_x = jnp.einsum("czyx,xk->czyk", pieces, table_x, precision=highest)
    along_y = jnp.einsum("czyk,yj->czjk", along_x, table_y, precision=highest)
    return jnp.einsum("czjk,zl->cljk", along_y, table_z, precision=highest)


def roll_block(block, amounts):
    return jnp.roll(jnp.roll(block, amounts[0], axis=1), amounts[1], axis=2)


def fold_rims(extended, axis_id, owned):
    middle = lax.slice_in_dim(extended, 4, owned + 4, axis=axis_id)
    leading = lax.slice_in_dim(extended, 0, 2, axis=axis_id)
    trailing = lax.slice_in_dim(extended, owned + 6, owned + 8, axis=axis_id)
    lead_pad = [(0, 0), (0, 0), (0, 0), (0, 0)]
    trail_pad = [(0, 0), (0, 0), (0, 0), (0, 0)]
    lead_pad[axis_id] = (0, owned - 2)
    trail_pad[axis_id] = (owned - 2, 0)
    return middle + jnp.pad(leading, lead_pad) + jnp.pad(trailing, trail_pad)


def body(fixed_image, moving_image, source_tile, block_shifts):
    depth, height, width = fixed_image.shape
    yblocks = height // BLK_Y
    xblocks = width // BLK_X
    block_count = yblocks * xblocks
    tile_lists = source_tile[:, 0, :, 0]
    my_tile = lax.axis_index("tile")
    own_list = lax.dynamic_index_in_dim(tile_lists, my_tile, 0, keepdims=False)
    row_steps = jnp.arange(BLK_Y, dtype=jnp.int32)
    initial = jnp.zeros((block_count, depth, BLK_Y, BLK_X), jnp.bfloat16)
    piece = lax.all_gather(moving_image, "tile", axis=1, tiled=True)
    length = piece.shape[1]
    held_blocks = []
    for block_id in range(block_count):
        row_block = block_id // xblocks
        col_block = block_id % xblocks
        wanted = own_list[block_id] * height + row_block * BLK_Y + row_steps
        usable = (wanted >= 0) & (wanted < length)
        columns_part = lax.slice_in_dim(piece, col_block * BLK_X, (col_block + 1) * BLK_X, axis=2)
        taken = jnp.take(columns_part, jnp.clip(wanted, 0, length - 1), axis=1)
        held_blocks.append(jnp.where(usable[None, :, None], taken, initial[block_id]))
    blocks = jnp.stack(held_blocks)
    rolled = jax.vmap(roll_block)(blocks, block_shifts[0, 0])
    warped = (
        rolled.reshape(yblocks, xblocks, depth, BLK_Y, BLK_X)
        .transpose(2, 0, 3, 1, 4)
        .reshape(depth, height, width)
    )
    image_pair = jnp.stack((fixed_image, warped))
    fixed_own = fixed_image.astype(jnp.float32)
    warp_own = warped.astype(jnp.float32)
    extended = with_halo(image_pair, (("tile", 2), ("gz", 1), ("rep", 3)), RAD).astype(jnp.float32)
    term_a, term_b, term_c = window_terms(extended[0], extended[1], RAD)
    terms_ext = with_halo(
        jnp.stack((term_a, term_b, term_c)).astype(jnp.bfloat16),
        (("tile", 2), ("gz", 1), ("rep", 3)),
        RAD,
    ).astype(jnp.float32)
    box_a = window_sum(terms_ext[0], RAD)
    box_b = window_sum(terms_ext[1], RAD)
    box_c = window_sum(terms_ext[2], RAD)
    margin = RAD
    gain = -(fixed_own * box_a + 2.0 * warp_own * box_b + box_c)
    slope_z, slope_y, slope_x = slopes(extended[1], margin, (depth, height, width))
    pieces = jnp.stack((gain * slope_z, gain * slope_y, gain * slope_x))
    depth_total = depth * lax.axis_size("gz")
    depth_knots = (depth_total + SPACING - 1) // SPACING
    table_z = spline_table(lax.axis_index("gz") * depth, depth, 0, depth_knots)
    row_knots = height // SPACING
    table_y = spline_table(my_tile * height, height, my_tile * row_knots - 2, row_knots + 4)
    col_knots = width // SPACING
    rep_index = lax.axis_index("rep")
    table_x = spline_table(rep_index * width, width, rep_index * col_knots - 2, col_knots + 4)
    local_grad = contract(pieces, table_z, table_y, table_x)
    spread = with_halo(local_grad, (("tile", 2), ("rep", 3)), 2)
    owned_grad = fold_rims(fold_rims(spread, 2, row_knots), 3, col_knots)
    return lax.psum(owned_grad, "gz")


EDGE = 2 * RAD
SEND_ROWS = 48
KERNEL_BYTES = 24 << 20


def pack_kernel(tiles, source_ref, source_in, moving_ref, fixed_ref, *out_refs):
    *packs, source_out, moving_out, fixed_out, send_out = out_refs
    source_out[...] = source_in[...]
    moving_out[...] = moving_ref[...]
    fixed_out[...] = fixed_ref[...]
    me = lax.axis_index("tile")
    half = lax.rem(me + lax.axis_index("gz"), 2)
    start = pl.multiple_of((1 - half) * BLK_Y, BLK_Y)
    send_out[...] = fixed_ref[:, pl.ds(start, SEND_ROWS), :]
    height, width = moving_ref.shape[1:]
    xblocks = width // BLK_X
    blocks = (height // BLK_Y) * xblocks
    cap = packs[0].shape[0]
    for step in range(1, tiles):
        other = lax.bitwise_xor(me, step)
        count = jnp.int32(0)
        chosen = [jnp.int32(0)] * cap
        for block in range(blocks):
            named = source_ref[other, block] == me
            chosen = [jnp.where(named & (count == slot), block, old) for slot, old in enumerate(chosen)]
            count = count + named.astype(jnp.int32)
        for slot, block in enumerate(chosen):
            row = pl.multiple_of(block // xblocks * BLK_Y, BLK_Y)
            col = pl.multiple_of(lax.rem(block, xblocks) * BLK_X, BLK_X)
            packs[step - 1][slot] = moving_ref[:, pl.ds(row, BLK_Y), pl.ds(col, BLK_X)]


def unpack_kernel(tiles, source_ref, shift_ref, moving_ref, *refs):
    recvs = refs[: tiles - 1]
    own_ref, send_ref = refs[tiles - 1 :]
    me = lax.axis_index("tile")
    half = lax.rem(me + lax.axis_index("gz"), 2)
    height, width = moving_ref.shape[1:]
    xblocks = width // BLK_X
    blocks = (height // BLK_Y) * xblocks
    cap = recvs[0].shape[0]
    for block in range(blocks):
        row, col = (block // xblocks) * BLK_Y, (block % xblocks) * BLK_X
        source = source_ref[me, block]
        slot = jnp.int32(0)
        for earlier in range(block):
            slot = slot + (source_ref[me, earlier] == source).astype(jnp.int32)
        slot = jnp.minimum(slot, cap - 1)
        step = lax.bitwise_xor(source, me)
        value = moving_ref[:, row : row + BLK_Y, col : col + BLK_X].astype(jnp.float32)
        for other in range(1, tiles):
            value = jnp.where(step == other, recvs[other - 1][slot].astype(jnp.float32), value)
        down = lax.rem(shift_ref[block, 0], BLK_Y)
        right = lax.rem(shift_ref[block, 1], BLK_X)
        value = pltpu.roll(value, right, 2)
        for bit in (1, 2, 4, 8):
            value = jnp.where(lax.bitwise_and(down, bit) != 0, pltpu.roll(value, bit, 1), value)
        own_ref[:, row : row + BLK_Y, col : col + BLK_X] = value.astype(own_ref.dtype)
    start = pl.multiple_of((1 - half) * BLK_Y, BLK_Y)
    send_ref[...] = own_ref[:, pl.ds(start, SEND_ROWS), :]


def side_kernel(own_ref, got_ref, *refs):
    out_ref = refs[-1]
    group = lax.axis_index("gz")
    half = lax.rem(lax.axis_index("tile") + group, 2)
    depth = own_ref.shape[0]
    col = pl.multiple_of((1 - lax.axis_index("rep")) * BLK_X, BLK_X)
    start = pl.multiple_of(half * BLK_Y, BLK_Y)
    for i in range(depth):
        out_ref[group * depth + i] = own_ref[i, pl.ds(start, SEND_ROWS), pl.ds(col, BLK_X)]
        out_ref[(1 - group) * depth + i] = got_ref[i, :, pl.ds(col, BLK_X)]


def five(array, axis):
    size = array.shape[axis]
    pair = array + pltpu.roll(array, 1, axis)
    return pltpu.roll(pair, size - 2, axis) + pair + pltpu.roll(array, 2, axis)


def lane_limits(side, width, span):
    return jnp.where(side == 0, 0, BLK_X - 48), jnp.where(side == 0, width + 32, span)


def assemble(own, got, near_in, image):
    group, side = lax.axis_index("gz"), lax.axis_index("rep")
    half = lax.rem(lax.axis_index("tile") + group, 2)
    depth, _, width = own.shape
    window, span = image.shape[1:]
    own_col = pl.multiple_of(side * BLK_X, BLK_X)
    new_col = pl.multiple_of((1 - side) * width, BLK_X)
    start = pl.multiple_of(half * BLK_Y, BLK_Y)
    low, high = lane_limits(side, width, span)
    lanes = lax.broadcasted_iota(jnp.int32, (window, BLK_X), 1) + new_col
    levels = lax.broadcasted_iota(jnp.int32, (window, BLK_X), 0)
    inner = (levels >= jnp.where(half == 0, EDGE, 0)) & (levels < jnp.where(half == 0, window, window - EDGE))
    near = inner & (lanes >= low) & (lanes < high)
    turn = jnp.where(half == 0, EDGE, SEND_ROWS - BLK_Y + EDGE)

    def shift_in(piece):
        return pltpu.roll(piece.astype(jnp.float32), turn, 0)[:window]

    for i in range(depth):
        mine, theirs = group * depth + i, (1 - group) * depth + i
        for plane, piece in ((mine, own[i, pl.ds(start, SEND_ROWS), :]), (theirs, got[i])):
            piece = shift_in(piece)
            for part in range(width // BLK_X):
                col = pl.multiple_of(own_col + part * BLK_X, BLK_X)
                value = piece[:, part * BLK_X : (part + 1) * BLK_X]
                image[plane, :, pl.ds(col, BLK_X)] = jnp.where(inner, value, 0.0)
        for plane in (mine, theirs):
            image[plane, :, pl.ds(new_col, BLK_X)] = jnp.where(near, shift_in(near_in[plane]), 0.0)


def fill_band(band):
    span = band.shape[0]
    across = lax.broadcasted_iota(jnp.int32, (span, span), 0) - lax.broadcasted_iota(jnp.int32, (span, span), 1)
    band[...] = jnp.where(jnp.abs(across) <= RAD, 1.0, 0.0).astype(band.dtype)


def lane_sums(exact, products, band):
    rows = (exact + products)[0].shape[0]
    low = [value - value.astype(jnp.bfloat16).astype(jnp.float32) for value in products]
    boxed = jnp.dot(
        jnp.concatenate(exact + products + low, axis=0).astype(jnp.bfloat16), band[...],
        preferred_element_type=jnp.float32,
    )
    pieces = [boxed[k * rows : (k + 1) * rows] for k in range(len(exact) + 2 * len(products))]
    first = len(exact)
    return pieces[:first] + [
        pieces[first + k] + pieces[first + len(products) + k] for k in range(len(products))
    ]


def near_planes(z, planes):
    return range(max(0, z - RAD), min(planes, z + RAD + 1))


def total(values):
    values = list(values)
    result = values[0]
    for value in values[1:]:
        result = result + value
    return result


def sum_planes(rows, boxes):
    for which in range(boxes.shape[0]):
        for z in range(boxes.shape[1]):
            boxes[which, z] = total(rows[which, k] for k in near_planes(z, boxes.shape[1]))


def fixed_kernel(own, got, near_in, image, boxes, band, rows):
    assemble(own, got, near_in, image)
    fill_band(band)
    for z in range(image.shape[0]):
        f = image[z]
        for which, value in enumerate(lane_sums([f], [f * f], band)):
            rows[which, z] = five(value, 0)
    sum_planes(rows, boxes)


def warped_kernel(own, got, near_in, fixed, image, rims):
    assemble(own, got, near_in, image)
    half = lax.rem(lax.axis_index("tile") + lax.axis_index("gz"), 2)
    planes, window, span = image.shape
    upper = lax.broadcasted_iota(jnp.int32, (2 * EDGE, span), 0) < EDGE
    for which, source in enumerate((fixed, image)):
        tiles = []
        for z in range(0, planes, 2):
            low, high = source.at[z], source.at[z + 1]
            top = jnp.where(upper, pltpu.roll(low[: 2 * EDGE], EDGE, 0), high[: 2 * EDGE])
            end = jnp.where(upper, low[window - 2 * EDGE :], pltpu.roll(high[window - 2 * EDGE :], EDGE, 0))
            tiles.append(jnp.where(half == 0, top, end))
        rims[which] = jnp.concatenate(tiles, axis=0).astype(rims.dtype)


def cross_kernel(fixed, warped, band, boxes, rows):
    for z in range(fixed.shape[0]):
        f, w = fixed[z], warped[z]
        for which, value in enumerate(lane_sums([w], [w * w, f * w], band)):
            rows[which, z] = five(value, 0)
    sum_planes(rows, boxes)


def main_kernel(
    tiles, fixed, warped, fixed_boxes, warped_boxes, rims, band, table_y, table_x,
    out_ref, images, edges, terms, sums,
):
    side, me = lax.axis_index("rep"), lax.axis_index("tile")
    half = lax.rem(me + lax.axis_index("gz"), 2)
    first = jnp.where(half == 0, (me == 0).astype(jnp.int32), 0)
    last = jnp.where(half == 1, (me == tiles - 1).astype(jnp.int32), 0)
    planes, window, span = fixed.shape
    tile = 2 * EDGE
    lanes = lax.broadcasted_iota(jnp.int32, (window, span), 1)
    levels = lax.broadcasted_iota(jnp.int32, (window, span), 0)
    low_lane, high_lane = lane_limits(side, span - BLK_X, span)
    low_row = jnp.where(first != 0, EDGE, RAD)
    high_row = jnp.where(last != 0, window - EDGE, window - RAD)
    inside = (lanes >= low_lane) & (lanes < high_lane) & (levels >= low_row) & (levels < high_row)

    outer = (first + last) != 0
    rim_f = jnp.where(outer, 0.0, rims[0].astype(jnp.float32))
    rim_w = jnp.where(outer, 0.0, rims[1].astype(jnp.float32))
    rim_sums = lane_sums([rim_f, rim_w], [rim_f * rim_f, rim_w * rim_w, rim_f * rim_w], band)
    at = lax.broadcasted_iota(jnp.int32, (tile, span), 0)
    upper = at < EDGE
    on_top, on_end = jnp.where(half == 0, 1.0, 0.0), jnp.where(half == 0, 0.0, 1.0)
    held = (at >= jnp.where(half == 0, 0, EDGE)) & (at < jnp.where(half == 0, EDGE, tile))
    reach = (at >= jnp.where(half == 0, 0, RAD)) & (at < jnp.where(half == 0, tile - RAD, tile))

    def rim_tile(rim, z):
        pair = rim[z // 2 * tile : (z // 2 + 1) * tile]
        other = pltpu.roll(pair, EDGE, 0)
        both = jnp.where(upper, pair, other) if z % 2 == 0 else jnp.where(upper, other, pair)
        return jnp.where(held, both, 0.0)

    def with_tile(value, extra):
        return jnp.concatenate(
            [value[:tile] + extra * on_top, value[tile : window - tile], value[window - tile :] + extra * on_end],
            axis=0,
        )

    for which in range(5):
        for z in range(planes):
            edges[which, z] = jnp.where(reach, five(rim_tile(rim_sums[which], z), 0), 0.0)
    for z in range(planes):
        images[z] = with_tile(warped[z], rim_tile(rim_w, z))

    volume = float((2 * RAD + 1) ** 3)
    sources = (fixed_boxes, 0), (warped_boxes, 0), (fixed_boxes, 1), (warped_boxes, 1), (warped_boxes, 2)
    for z in range(planes):
        sum_f, sum_w, sum_ff, sum_ww, sum_fw = (
            with_tile(source[index, z], total(edges[which, k] for k in near_planes(z, planes)))
            for which, (source, index) in enumerate(sources)
        )
        cross = sum_fw - sum_f * sum_w * (1.0 / volume)
        var_f = sum_ff - sum_f * sum_f * (1.0 / volume)
        var_w = sum_ww - sum_w * sum_w * (1.0 / volume)
        inverse = 1.0 / (var_f * var_w + den_floor)
        ratio = cross * inverse
        term_a = 2.0 * ratio
        term_b = -(ratio * ratio) * var_f
        term_c = -(term_a * sum_f + 2.0 * term_b * sum_w) * (1.0 / volume)
        values = [five(jnp.where(inside, value, 0.0), 0) for value in (term_a, term_b, term_c)]
        for which, value in enumerate(lane_sums([], values, band)):
            terms[which, z] = value

    for d in range(3):
        sums[d] = jnp.zeros((window, span), jnp.float32)
    owned = (levels >= EDGE) & (levels < window - EDGE)
    for z in range(planes):
        box_a, box_b, box_c = (total(terms[which, k] for k in near_planes(z, planes)) for which in range(3))
        f, w = fixed[z], images[z]
        gain = -(f * box_a + 2.0 * w * box_b + box_c)
        u = z / SPACING
        weight = (3.0 * u * u * u - 6.0 * u * u + 4.0) * (0.5 / 6.0)
        gain = jnp.where(owned, gain, 0.0) * weight
        ahead = images[z + 1] if z + 1 < planes else 0.0
        behind = images[z - 1] if z > 0 else 0.0
        sums[0] += gain * (ahead - behind)
        sums[1] += gain * (pltpu.roll(w, window - 1, 0) - pltpu.roll(w, 1, 0))
        sums[2] += gain * (pltpu.roll(w, span - 1, 1) - pltpu.roll(w, 1, 1))

    for d in range(3):
        along_x = lax.dot_general(
            sums[d], table_x[...], (((1,), (1,)), ((), ())),
            precision=lax.Precision.HIGHEST, preferred_element_type=jnp.float32,
        )
        out_ref[d] = lax.dot_general(
            table_y[...], along_x, (((1,), (0,)), ((), ())),
            precision=lax.Precision.HIGHEST, preferred_element_type=jnp.float32,
        )


def local_kernel(kernel, outs, arrays, scratch=()):
    vmem = pl.BlockSpec(memory_space=pltpu.VMEM)
    return pl.pallas_call(
        kernel,
        out_shape=[pltpu.VMEM(shape, dtype) for shape, dtype in outs],
        in_specs=[vmem] * len(arrays),
        out_specs=[vmem] * len(outs),
        scratch_shapes=list(scratch),
        compiler_params=pltpu.CompilerParams(vmem_limit_bytes=KERNEL_BYTES),
    )(*(pltpu.with_memory_space_constraint(array, pltpu.VMEM) for array in arrays))


def fast_body(tiles, fixed_image, moving_image, source_tile, block_shifts):
    depth, height, width = fixed_image.shape
    me, group, side = lax.axis_index("tile"), lax.axis_index("gz"), lax.axis_index("rep")
    half = lax.rem(me + group, 2)
    sources = source_tile[:, 0, :, 0]
    shifts = block_shifts[0, 0]
    cap = MAX_NAMED if tiles == 4 else sources.shape[1]
    planes = 2 * depth
    window, span = height // 2 + 2 * EDGE, width + BLK_X
    short, full = jnp.bfloat16, jnp.float32
    whole, send_shape = (fixed_image.shape, short), ((depth, SEND_ROWS, width), short)
    side_shape = ((planes, SEND_ROWS, BLK_X), short)
    image_shape = ((planes, window, span), full)
    smem, vmem = (pl.BlockSpec(memory_space=space) for space in (pltpu.SMEM, pltpu.VMEM))
    outs = [((cap, depth, BLK_Y, BLK_X), short)] * (tiles - 1) + [(sources.shape, jnp.int32), whole, whole, send_shape]
    *packs, sources, moving_image, fixed_image, fixed_send = pl.pallas_call(
        functools.partial(pack_kernel, tiles),
        out_shape=[pltpu.VMEM(*out) for out in outs],
        in_specs=[smem, vmem, vmem, vmem],
        out_specs=[vmem] * len(outs),
    )(sources, sources, moving_image, fixed_image)

    trio = ("tile", "gz", "rep")

    def number(t, g, r):
        return (t * 2 + g) * 2 + r

    swap = [(0, 1), (1, 0)]
    straight, slant = [], []
    for r in range(2):
        for t in range(tiles):
            for g in range(2):
                to = t - 1 if (g + t) % 2 == 0 else t + 1
                there = 0 <= to < tiles
                straight.append((number(t, g, r), number(to, g, r) if there else number(t, g, 1 - r)))
                slant.append((number(t, g, r), number(to if there else t, 1 - g, r)))

    got = [
        lax.ppermute(pack, "tile", [(t, t ^ step) for t in range(tiles)])
        for step, pack in zip(range(1, tiles), packs)
    ]
    fixed_got = lax.ppermute(fixed_send, "gz", swap)
    own, send = local_kernel(
        functools.partial(unpack_kernel, tiles), [whole, send_shape], [sources, shifts, moving_image, *got]
    )
    warp_got = lax.ppermute(send, "gz", swap)
    (fixed_side,) = local_kernel(side_kernel, [side_shape], [fixed_image, fixed_got])
    fixed_near = lax.ppermute(fixed_side, "rep", swap)
    boxes = [(count, planes, window, span) for count in (2, 3)]
    fixed, fixed_boxes, band = local_kernel(
        fixed_kernel,
        [image_shape, (boxes[0], full), ((span, span), short)],
        [fixed_image, fixed_got, fixed_near],
        [pltpu.VMEM(boxes[0], full)],
    )
    (warp_side,) = local_kernel(side_kernel, [side_shape], [own, warp_got, fixed])
    warp_near = lax.ppermute(warp_side, "rep", swap)
    warped, rims = local_kernel(
        warped_kernel,
        [image_shape, ((2, planes * EDGE, span), short)],
        [own, warp_got, warp_near, fixed],
    )
    rims = lax.ppermute(rims, trio, straight)
    (warped_boxes,) = local_kernel(
        cross_kernel, [(boxes[1], full)], [fixed, warped, band], [pltpu.VMEM(boxes[1], full)]
    )

    row_knots, col_knots = height // SPACING, width // SPACING
    row_at = jnp.arange(window, dtype=jnp.int32)
    table_y = spline_table(half * (height // 2) - EDGE, window, -2, row_knots + 4)
    table_y = jnp.where(((row_at >= EDGE) & (row_at < window - EDGE))[:, None], table_y, 0.0).T
    table_x = spline_table(side * BLK_X, span, side * col_knots, col_knots).T
    (part,) = local_kernel(
        functools.partial(main_kernel, tiles),
        [((3, row_knots + 4, col_knots), full)],
        [fixed, warped, fixed_boxes, warped_boxes, rims, band, table_y, table_x],
        [
            pltpu.VMEM((planes, window, span), full),
            pltpu.VMEM((5, planes, 2 * EDGE, span), full),
            pltpu.VMEM((3, planes, window, span), full),
            pltpu.VMEM((3, window, span), full),
        ],
    )
    across = lax.ppermute(part, "gz", swap)
    part_slant = lax.ppermute(part, trio, slant)
    part_straight = lax.ppermute(part, trio, straight)
    below = jnp.where(half == 0, part_slant, part_straight)
    above = jnp.where(half == 0, part_straight, part_slant)
    below = jnp.where(me == tiles - 1, 0.0, below[:, :2])
    above = jnp.where(me == 0, 0.0, above[:, row_knots + 2 :])
    middle = part[:, 2 : row_knots + 2] + across[:, 2 : row_knots + 2]
    return (middle + jnp.concatenate([above, below], axis=1))[:, None]


def solution(mesh):
    sizes = mesh.shape
    tiles = sizes["tile"]
    fast = sizes["gz"] == 2 and sizes["rep"] == 2 and tiles & (tiles - 1) == 0 and tiles > 1
    return jax.shard_map(
        functools.partial(fast_body, tiles) if fast else body,
        mesh=mesh,
        in_specs=(
            P(("slab", "gz"), "tile", "rep"),
            P(("slab", "gz"), "tile", "rep"),
            P("slab", "rep", None, None),
            P(("slab", "tile"), "rep", None, None),
        ),
        out_specs=P(None, "slab", "tile", "rep"),
        check_vma=False,
    )
```

```python
import functools

import jax
import jax.numpy as jnp
from jax import lax
from jax.experimental import pallas as pl
from jax.experimental.pallas import tpu as pltpu
from jax.sharding import PartitionSpec as P

BLK_Y = 16
BLK_X = 128
RAD = 2
SPACING = 16
MAX_NAMED = 4


den_floor = 1e-05

def with_halo(array, sides, width):
    for axis, dim in sides:
        count, length = (lax.axis_size(axis), array.shape[dim])
        up = [(i, (i + 1) % count) for i in range(count - 1)]
        down = [(j, i) for i, j in up]
        last = lax.slice_in_dim(array, length - width, length, axis=dim)
        first = lax.slice_in_dim(array, 0, width, axis=dim)
        before = lax.ppermute(last, axis, up)
        after = lax.ppermute(first, axis, down)
        array = jnp.concatenate([before, array, after], axis=dim)
    return array


def window_sum(extended, radius):
    result = extended
    for axis_id in range(3):
        length = result.shape[axis_id] - 2 * radius
        summed = lax.slice_in_dim(result, 0, length, axis=axis_id)
        for offset in range(1, 2 * radius + 1):
            summed = summed + lax.slice_in_dim(result, offset, offset + length, axis=axis_id)
        result = summed
    return result


def window_terms(ext_fixed, ext_warp, radius):
    volume = float((2 * radius + 1) ** 3)
    sum_fixed = window_sum(ext_fixed, radius)
    sum_warp = window_sum(ext_warp, radius)
    sum_fixed_sq = window_sum(ext_fixed * ext_fixed, radius)
    sum_warp_sq = window_sum(ext_warp * ext_warp, radius)
    sum_product = window_sum(ext_fixed * ext_warp, radius)
    cross_term = sum_product - sum_fixed * sum_warp / volume
    fixed_var = sum_fixed_sq - sum_fixed * sum_fixed / volume
    warp_var = sum_warp_sq - sum_warp * sum_warp / volume
    denominator = fixed_var * warp_var + den_floor
    term_a = 2.0 * cross_term / denominator
    term_b = -cross_term * cross_term * fixed_var / (denominator * denominator)
    term_c = -(term_a * sum_fixed + 2.0 * term_b * sum_warp) / volume
    return (term_a, term_b, term_c)


def slopes(extended, margin, extent):
    result = []
    for axis_id in range(3):
        ahead = [margin, margin, margin]
        behind = [margin, margin, margin]
        ahead[axis_id] += 1
        behind[axis_id] -= 1
        upper = lax.slice(
            extended,
            tuple(ahead),
            (ahead[0] + extent[0], ahead[1] + extent[1], ahead[2] + extent[2]),
        )
        lower = lax.slice(
            extended,
            tuple(behind),
            (behind[0] + extent[0], behind[1] + extent[1], behind[2] + extent[2]),
        )
        result.append(0.5 * (upper - lower))
    return result


def spline_table(first_pos, length, first_col, columns):
    places = first_pos + jnp.arange(length, dtype=jnp.int32)
    knots = places // SPACING
    within = (places - knots * SPACING).astype(jnp.float32) / SPACING
    squares = within * within
    cubes = squares * within
    weights = (
        (1.0 - within) ** 3 / 6.0,
        (3.0 * cubes - 6.0 * squares + 4.0) / 6.0,
        (-3.0 * cubes + 3.0 * squares + 3.0 * within + 1.0) / 6.0,
        cubes / 6.0,
    )
    targets = first_col + jnp.arange(columns, dtype=jnp.int32)
    table = jnp.zeros((length, columns), jnp.float32)
    for offset in range(4):
        table = table + jnp.where(
            targets[None, :] == (knots + offset - 1)[:, None], weights[offset][:, None], 0.0
        )
    return table


def contract(pieces, table_z, table_y, table_x):
    highest = lax.Precision.HIGHEST
    along_x = jnp.einsum("czyx,xk->czyk", pieces, table_x, precision=highest)
    along_y = jnp.einsum("czyk,yj->czjk", along_x, table_y, precision=highest)
    return jnp.einsum("czjk,zl->cljk", along_y, table_z, precision=highest)


def roll_block(block, amounts):
    return jnp.roll(jnp.roll(block, amounts[0], axis=1), amounts[1], axis=2)


def fold_rims(extended, axis_id, owned):
    middle = lax.slice_in_dim(extended, 4, owned + 4, axis=axis_id)
    leading = lax.slice_in_dim(extended, 0, 2, axis=axis_id)
    trailing = lax.slice_in_dim(extended, owned + 6, owned + 8, axis=axis_id)
    lead_pad = [(0, 0), (0, 0), (0, 0), (0, 0)]
    trail_pad = [(0, 0), (0, 0), (0, 0), (0, 0)]
    lead_pad[axis_id] = (0, owned - 2)
    trail_pad[axis_id] = (owned - 2, 0)
    return middle + jnp.pad(leading, lead_pad) + jnp.pad(trailing, trail_pad)


def body(fixed_image, moving_image, source_tile, block_shifts):
    depth, height, width = fixed_image.shape
    yblocks = height // BLK_Y
    xblocks = width // BLK_X
    block_count = yblocks * xblocks
    tile_lists = source_tile[:, 0, :, 0]
    my_tile = lax.axis_index("tile")
    own_list = lax.dynamic_index_in_dim(tile_lists, my_tile, 0, keepdims=False)
    row_steps = jnp.arange(BLK_Y, dtype=jnp.int32)
    initial = jnp.zeros((block_count, depth, BLK_Y, BLK_X), jnp.bfloat16)
    piece = lax.all_gather(moving_image, "tile", axis=1, tiled=True)
    length = piece.shape[1]
    held_blocks = []
    for block_id in range(block_count):
        row_block = block_id // xblocks
        col_block = block_id % xblocks
        wanted = own_list[block_id] * height + row_block * BLK_Y + row_steps
        usable = (wanted >= 0) & (wanted < length)
        columns_part = lax.slice_in_dim(piece, col_block * BLK_X, (col_block + 1) * BLK_X, axis=2)
        taken = jnp.take(columns_part, jnp.clip(wanted, 0, length - 1), axis=1)
        held_blocks.append(jnp.where(usable[None, :, None], taken, initial[block_id]))
    blocks = jnp.stack(held_blocks)
    rolled = jax.vmap(roll_block)(blocks, block_shifts[0, 0])
    warped = (
        rolled.reshape(yblocks, xblocks, depth, BLK_Y, BLK_X)
        .transpose(2, 0, 3, 1, 4)
        .reshape(depth, height, width)
    )
    image_pair = jnp.stack((fixed_image, warped))
    fixed_own = fixed_image.astype(jnp.float32)
    warp_own = warped.astype(jnp.float32)
    extended = with_halo(image_pair, (("tile", 2), ("gz", 1), ("rep", 3)), RAD).astype(jnp.float32)
    term_a, term_b, term_c = window_terms(extended[0], extended[1], RAD)
    terms_ext = with_halo(
        jnp.stack((term_a, term_b, term_c)).astype(jnp.bfloat16),
        (("tile", 2), ("gz", 1), ("rep", 3)),
        RAD,
    ).astype(jnp.float32)
    box_a = window_sum(terms_ext[0], RAD)
    box_b = window_sum(terms_ext[1], RAD)
    box_c = window_sum(terms_ext[2], RAD)
    margin = RAD
    gain = -(fixed_own * box_a + 2.0 * warp_own * box_b + box_c)
    slope_z, slope_y, slope_x = slopes(extended[1], margin, (depth, height, width))
    pieces = jnp.stack((gain * slope_z, gain * slope_y, gain * slope_x))
    depth_total = depth * lax.axis_size("gz")
    depth_knots = (depth_total + SPACING - 1) // SPACING
    table_z = spline_table(lax.axis_index("gz") * depth, depth, 0, depth_knots)
    row_knots = height // SPACING
    table_y = spline_table(my_tile * height, height, my_tile * row_knots - 2, row_knots + 4)
    col_knots = width // SPACING
    rep_index = lax.axis_index("rep")
    table_x = spline_table(rep_index * width, width, rep_index * col_knots - 2, col_knots + 4)
    local_grad = contract(pieces, table_z, table_y, table_x)
    spread = with_halo(local_grad, (("tile", 2), ("rep", 3)), 2)
    owned_grad = fold_rims(fold_rims(spread, 2, row_knots), 3, col_knots)
    return lax.psum(owned_grad, "gz")


EDGE = 2 * RAD
KEEP_ROWS, SEND_ROWS = 48, 40
KERNEL_BYTES = 24 << 20


def far_first(tiles):
    return sorted(range(1, tiles), key=lambda step: (step < 2, step))


def send_window(half, image, out):
    rows = out.shape[1]
    value = image[...].astype(jnp.float32)
    value = jnp.where(half == 1, value[:, :rows], value[:, value.shape[1] - rows :])
    out[...] = value.astype(out.dtype)


def pack_kernel(tiles, source_ref, source_in, moving_ref, fixed_ref, *out_refs):
    *packs, source_out, moving_out, fixed_out, send_out = out_refs
    source_out[...] = source_in[...]
    moving_out[...] = moving_ref[...]
    fixed_out[...] = fixed_ref[...]
    me = lax.axis_index("tile")
    half = lax.rem(me + lax.axis_index("gz"), 2)
    send_window(half, fixed_ref, send_out)
    height, width = moving_ref.shape[1:]
    xblocks = width // BLK_X
    blocks = (height // BLK_Y) * xblocks
    cap = packs[0].shape[0]
    for step, pack in zip(far_first(tiles), packs):
        other = lax.bitwise_xor(me, step)
        count = jnp.int32(0)
        chosen = [jnp.int32(0)] * cap
        for block in range(blocks):
            named = source_ref[other, block] == me
            chosen = [jnp.where(named & (count == slot), block, old) for slot, old in enumerate(chosen)]
            count = count + named.astype(jnp.int32)
        for slot, block in enumerate(chosen):
            row = pl.multiple_of(block // xblocks * BLK_Y, BLK_Y)
            col = pl.multiple_of(lax.rem(block, xblocks) * BLK_X, BLK_X)
            pack[slot] = moving_ref[:, pl.ds(row, BLK_Y), pl.ds(col, BLK_X)]


def unpack_kernel(tiles, source_ref, shift_ref, moving_ref, *refs):
    recvs = dict(zip(far_first(tiles), refs))
    own_ref, send_ref = refs[tiles - 1 :]
    me = lax.axis_index("tile")
    half = lax.rem(me + lax.axis_index("gz"), 2)
    height, width = moving_ref.shape[1:]
    xblocks = width // BLK_X
    blocks = (height // BLK_Y) * xblocks
    cap = refs[0].shape[0]
    for block in range(blocks):
        row, col = (block // xblocks) * BLK_Y, (block % xblocks) * BLK_X
        source = source_ref[me, block]
        slot = jnp.int32(0)
        for earlier in range(block):
            slot = slot + (source_ref[me, earlier] == source).astype(jnp.int32)
        slot = jnp.minimum(slot, cap - 1)
        step = lax.bitwise_xor(source, me)
        value = moving_ref[:, row : row + BLK_Y, col : col + BLK_X].astype(jnp.float32)
        for other in range(1, tiles):
            value = jnp.where(step == other, recvs[other][slot].astype(jnp.float32), value)
        down = lax.rem(shift_ref[block, 0], BLK_Y)
        right = lax.rem(shift_ref[block, 1], BLK_X)
        value = pltpu.roll(value, right, 2)
        for bit in (1, 2, 4, 8):
            value = jnp.where(lax.bitwise_and(down, bit) != 0, pltpu.roll(value, bit, 1), value)
        own_ref[:, row : row + BLK_Y, col : col + BLK_X] = value.astype(own_ref.dtype)
    send_window(half, own_ref, send_ref)


def side_kernel(own_ref, got_ref, *refs):
    out_ref = refs[-1]
    group = lax.axis_index("gz")
    half = lax.rem(lax.axis_index("tile") + group, 2)
    depth = own_ref.shape[0]
    col = pl.multiple_of((1 - lax.axis_index("rep")) * BLK_X, BLK_X)
    start = pl.multiple_of(half * BLK_Y, BLK_Y)
    for i in range(depth):
        out_ref[group * depth + i] = own_ref[i, pl.ds(start, KEEP_ROWS), pl.ds(col, BLK_X)]
        theirs = got_ref[i, :, pl.ds(col, BLK_X)].astype(jnp.float32)
        theirs = jnp.concatenate([theirs, jnp.zeros((KEEP_ROWS - SEND_ROWS, BLK_X), jnp.float32)], axis=0)
        out_ref[(1 - group) * depth + i] = theirs.astype(out_ref.dtype)


def five(array, axis):
    size = array.shape[axis]
    pair = array + pltpu.roll(array, 1, axis)
    return pltpu.roll(pair, size - 2, axis) + pair + pltpu.roll(array, 2, axis)


def lane_limits(side, width, span):
    return jnp.where(side == 0, 0, BLK_X - 48), jnp.where(side == 0, width + 32, span)


def assemble(own, got, near_in, image):
    group, side = lax.axis_index("gz"), lax.axis_index("rep")
    half = lax.rem(lax.axis_index("tile") + group, 2)
    depth, _, width = own.shape
    window, span = image.shape[1:]
    own_col = pl.multiple_of(side * BLK_X, BLK_X)
    new_col = pl.multiple_of((1 - side) * width, BLK_X)
    start = pl.multiple_of(half * BLK_Y, BLK_Y)
    low, high = lane_limits(side, width, span)
    lanes = lax.broadcasted_iota(jnp.int32, (window, BLK_X), 1) + new_col
    levels = lax.broadcasted_iota(jnp.int32, (window, BLK_X), 0)
    inner = (levels >= jnp.where(half == 0, EDGE, 0)) & (levels < jnp.where(half == 0, window, window - EDGE))
    near = inner & (lanes >= low) & (lanes < high)

    def shift_in(piece, skip):
        turn = jnp.where(half == 0, EDGE, piece.shape[0] - skip)
        return pltpu.roll(piece.astype(jnp.float32), turn, 0)[:window]

    for i in range(depth):
        mine, theirs = (group * depth + i, BLK_Y - EDGE), ((1 - group) * depth + i, EDGE)
        for (plane, skip), piece in ((mine, own[i, pl.ds(start, KEEP_ROWS), :]), (theirs, got[i])):
            piece = shift_in(piece, skip)
            for part in range(width // BLK_X):
                col = pl.multiple_of(own_col + part * BLK_X, BLK_X)
                value = piece[:, part * BLK_X : (part + 1) * BLK_X]
                image[plane, :, pl.ds(col, BLK_X)] = jnp.where(inner, value, 0.0)
        for plane, skip in (mine, theirs):
            image[plane, :, pl.ds(new_col, BLK_X)] = jnp.where(near, shift_in(near_in[plane], skip), 0.0)


def fill_band(band):
    span = band.shape[0]
    across = lax.broadcasted_iota(jnp.int32, (span, span), 0) - lax.broadcasted_iota(jnp.int32, (span, span), 1)
    band[...] = jnp.where(jnp.abs(across) <= RAD, 1.0, 0.0).astype(band.dtype)


def halves(value):
    high = value.astype(jnp.bfloat16)
    return high, (value - high.astype(jnp.float32)).astype(jnp.bfloat16)


def table_halves(table):
    high = lax.reduce_precision(table, exponent_bits=8, mantissa_bits=7)
    return high.astype(jnp.bfloat16), (table - high).astype(jnp.bfloat16)


def lane_sums(exact, products, band):
    rows = (exact + products)[0].shape[0]
    low = [value - value.astype(jnp.bfloat16).astype(jnp.float32) for value in products]
    boxed = jnp.dot(
        jnp.concatenate(exact + products + low, axis=0).astype(jnp.bfloat16), band[...],
        preferred_element_type=jnp.float32,
    )
    pieces = [boxed[k * rows : (k + 1) * rows] for k in range(len(exact) + 2 * len(products))]
    first = len(exact)
    return pieces[:first] + [
        pieces[first + k] + pieces[first + len(products) + k] for k in range(len(products))
    ]


def near_planes(z, planes):
    return range(max(0, z - RAD), min(planes, z + RAD + 1))


def total(values):
    values = list(values)
    result = values[0]
    for value in values[1:]:
        result = result + value
    return result


def sum_planes(rows, boxes):
    for which in range(boxes.shape[0]):
        for z in range(boxes.shape[1]):
            boxes[which, z] = total(rows[which, k] for k in near_planes(z, boxes.shape[1]))


def fixed_kernel(own, got, near_in, image, boxes, band, rows):
    assemble(own, got, near_in, image)
    fill_band(band)
    for z in range(image.shape[0]):
        f = image[z]
        for which, value in enumerate(lane_sums([f], [f * f], band)):
            rows[which, z] = five(value, 0)
    sum_planes(rows, boxes)


def warped_kernel(own, got, near_in, fixed, image, rims):
    assemble(own, got, near_in, image)
    half = lax.rem(lax.axis_index("tile") + lax.axis_index("gz"), 2)
    planes, window, span = image.shape
    upper = lax.broadcasted_iota(jnp.int32, (2 * EDGE, span), 0) < EDGE
    for which, source in enumerate((fixed, image)):
        tiles = []
        for z in range(0, planes, 2):
            low, high = source.at[z], source.at[z + 1]
            top = jnp.where(upper, pltpu.roll(low[: 2 * EDGE], EDGE, 0), high[: 2 * EDGE])
            end = jnp.where(upper, low[window - 2 * EDGE :], pltpu.roll(high[window - 2 * EDGE :], EDGE, 0))
            tiles.append(jnp.where(half == 0, top, end))
        rims[which] = jnp.concatenate(tiles, axis=0).astype(rims.dtype)


def cross_kernel(fixed, warped, band, boxes, rows):
    for z in range(fixed.shape[0]):
        f, w = fixed[z], warped[z]
        for which, value in enumerate(lane_sums([w], [w * w, f * w], band)):
            rows[which, z] = five(value, 0)
    sum_planes(rows, boxes)


def main_kernel(
    tiles, fixed, warped, fixed_boxes, warped_boxes, rims, band, table_y, table_x,
    out_ref, images, edges, terms, sums,
):
    side, me = lax.axis_index("rep"), lax.axis_index("tile")
    half = lax.rem(me + lax.axis_index("gz"), 2)
    first = jnp.where(half == 0, (me == 0).astype(jnp.int32), 0)
    last = jnp.where(half == 1, (me == tiles - 1).astype(jnp.int32), 0)
    planes, window, span = fixed.shape
    tile = 2 * EDGE
    lanes = lax.broadcasted_iota(jnp.int32, (window, span), 1)
    levels = lax.broadcasted_iota(jnp.int32, (window, span), 0)
    low_lane, high_lane = lane_limits(side, span - BLK_X, span)
    low_row = jnp.where(first != 0, EDGE, RAD)
    high_row = jnp.where(last != 0, window - EDGE, window - RAD)
    inside = (lanes >= low_lane) & (lanes < high_lane) & (levels >= low_row) & (levels < high_row)

    outer = (first + last) != 0
    rim_f = jnp.where(outer, 0.0, rims[0].astype(jnp.float32))
    rim_w = jnp.where(outer, 0.0, rims[1].astype(jnp.float32))
    rim_sums = lane_sums([rim_f, rim_w], [rim_f * rim_f, rim_w * rim_w, rim_f * rim_w], band)
    at = lax.broadcasted_iota(jnp.int32, (tile, span), 0)
    upper = at < EDGE
    on_top, on_end = jnp.where(half == 0, 1.0, 0.0), jnp.where(half == 0, 0.0, 1.0)
    held = (at >= jnp.where(half == 0, 0, EDGE)) & (at < jnp.where(half == 0, EDGE, tile))
    reach = (at >= jnp.where(half == 0, 0, RAD)) & (at < jnp.where(half == 0, tile - RAD, tile))

    def rim_tile(rim, z):
        pair = rim[z // 2 * tile : (z // 2 + 1) * tile]
        other = pltpu.roll(pair, EDGE, 0)
        both = jnp.where(upper, pair, other) if z % 2 == 0 else jnp.where(upper, other, pair)
        return jnp.where(held, both, 0.0)

    def with_tile(value, extra):
        return jnp.concatenate(
            [value[:tile] + extra * on_top, value[tile : window - tile], value[window - tile :] + extra * on_end],
            axis=0,
        )

    for which in range(5):
        for z in range(planes):
            edges[which, z] = jnp.where(reach, five(rim_tile(rim_sums[which], z), 0), 0.0)
    for z in range(planes):
        images[z] = with_tile(warped[z], rim_tile(rim_w, z))

    volume = float((2 * RAD + 1) ** 3)
    sources = (fixed_boxes, 0), (warped_boxes, 0), (fixed_boxes, 1), (warped_boxes, 1), (warped_boxes, 2)
    for z in range(planes):
        sum_f, sum_w, sum_ff, sum_ww, sum_fw = (
            with_tile(source[index, z], total(edges[which, k] for k in near_planes(z, planes)))
            for which, (source, index) in enumerate(sources)
        )
        cross = sum_fw - sum_f * sum_w * (1.0 / volume)
        var_f = sum_ff - sum_f * sum_f * (1.0 / volume)
        var_w = sum_ww - sum_w * sum_w * (1.0 / volume)
        inverse = 1.0 / (var_f * var_w + den_floor)
        ratio = cross * inverse
        term_a = 2.0 * ratio
        term_b = -(ratio * ratio) * var_f
        term_c = -(term_a * sum_f + 2.0 * term_b * sum_w) * (1.0 / volume)
        values = [five(jnp.where(inside, value, 0.0), 0) for value in (term_a, term_b, term_c)]
        for which, value in enumerate(lane_sums([], values, band)):
            terms[which, z] = value

    sums[...] = jnp.zeros(sums.shape, jnp.float32)
    owned = (levels >= EDGE) & (levels < window - EDGE)
    for z in range(planes):
        box_a, box_b, box_c = (total(terms[which, k] for k in near_planes(z, planes)) for which in range(3))
        f, w = fixed[z], images[z]
        gain = -(f * box_a + 2.0 * w * box_b + box_c)
        u = z / SPACING
        weight = (3.0 * u * u * u - 6.0 * u * u + 4.0) * (0.5 / 6.0)
        gain = jnp.where(owned, gain, 0.0) * weight
        ahead = images[z + 1] if z + 1 < planes else 0.0
        behind = images[z - 1] if z > 0 else 0.0
        sums[:window] += gain * (ahead - behind)
        sums[1 * window : 2 * window] += gain * (pltpu.roll(w, window - 1, 0) - pltpu.roll(w, 1, 0))
        sums[2 * window : 3 * window] += gain * (pltpu.roll(w, span - 1, 1) - pltpu.roll(w, 1, 1))

    boxed = jnp.dot(
        jnp.concatenate(halves(sums[...]), axis=0), table_x[...], preferred_element_type=jnp.float32
    )
    rows, count = sums.shape[0], out_ref.shape[1]
    along_x = boxed[:rows] + pltpu.roll(boxed[:rows], boxed.shape[1] - count, 1) + boxed[rows:]
    high, low = halves(along_x)
    out_ref[...] = jnp.dot(
        table_y[...], jnp.concatenate([high, high, low], axis=0), preferred_element_type=jnp.float32
    )[:, :count]


def local_kernel(kernel, outs, arrays, scratch=()):
    vmem = pl.BlockSpec(memory_space=pltpu.VMEM)
    return pl.pallas_call(
        kernel,
        out_shape=[pltpu.VMEM(shape, dtype) for shape, dtype in outs],
        in_specs=[vmem] * len(arrays),
        out_specs=[vmem] * len(outs),
        scratch_shapes=list(scratch),
        compiler_params=pltpu.CompilerParams(vmem_limit_bytes=KERNEL_BYTES),
    )(*(pltpu.with_memory_space_constraint(array, pltpu.VMEM) for array in arrays))


def fast_body(tiles, fixed_image, moving_image, source_tile, block_shifts):
    depth, height, width = fixed_image.shape
    me, group, side = lax.axis_index("tile"), lax.axis_index("gz"), lax.axis_index("rep")
    half = lax.rem(me + group, 2)
    sources = source_tile[:, 0, :, 0]
    shifts = block_shifts[0, 0]
    cap = MAX_NAMED if tiles == 4 else sources.shape[1]
    planes = 2 * depth
    window, span = height // 2 + 2 * EDGE, width + BLK_X
    short, full = jnp.bfloat16, jnp.float32
    whole, send_shape = (fixed_image.shape, short), ((depth, SEND_ROWS, width), short)
    side_shape = ((planes, KEEP_ROWS, BLK_X), short)
    image_shape = ((planes, window, span), full)
    smem, vmem = (pl.BlockSpec(memory_space=space) for space in (pltpu.SMEM, pltpu.VMEM))
    outs = [((cap, depth, BLK_Y, BLK_X), short)] * (tiles - 1) + [(sources.shape, jnp.int32), whole, whole, send_shape]
    *packs, sources, moving_image, fixed_image, fixed_send = pl.pallas_call(
        functools.partial(pack_kernel, tiles),
        out_shape=[pltpu.VMEM(*out) for out in outs],
        in_specs=[smem, vmem, vmem, vmem],
        out_specs=[vmem] * len(outs),
    )(sources, sources, moving_image, fixed_image)

    trio = ("tile", "gz", "rep")

    def number(t, g, r):
        return (t * 2 + g) * 2 + r

    swap = [(0, 1), (1, 0)]
    straight, slant = [], []
    for r in range(2):
        for t in range(tiles):
            for g in range(2):
                to = t - 1 if (g + t) % 2 == 0 else t + 1
                there = 0 <= to < tiles
                straight.append((number(t, g, r), number(to, g, r) if there else number(t, g, 1 - r)))
                slant.append((number(t, g, r), number(to if there else t, 1 - g, r)))

    got = [
        lax.ppermute(pack, "tile", [(t, t ^ step) for t in range(tiles)])
        for step, pack in zip(far_first(tiles), packs)
    ]
    fixed_got = lax.ppermute(fixed_send, "gz", swap)
    own, send = local_kernel(
        functools.partial(unpack_kernel, tiles), [whole, send_shape], [sources, shifts, moving_image, *got]
    )
    warp_got = lax.ppermute(send, "gz", swap)
    (fixed_side,) = local_kernel(side_kernel, [side_shape], [fixed_image, fixed_got])
    fixed_near = lax.ppermute(fixed_side, "rep", swap)
    boxes = [(count, planes, window, span) for count in (2, 3)]
    fixed, fixed_boxes, band = local_kernel(
        fixed_kernel,
        [image_shape, (boxes[0], full), ((span, span), short)],
        [fixed_image, fixed_got, fixed_near],
        [pltpu.VMEM(boxes[0], full)],
    )
    (warp_side,) = local_kernel(side_kernel, [side_shape], [own, warp_got, fixed])
    warp_near = lax.ppermute(warp_side, "rep", swap)
    warped, rims = local_kernel(
        warped_kernel,
        [image_shape, ((2, planes * EDGE, span), short)],
        [own, warp_got, warp_near, fixed],
    )
    rims = lax.ppermute(rims, trio, straight)
    (warped_boxes,) = local_kernel(
        cross_kernel, [(boxes[1], full)], [fixed, warped, band], [pltpu.VMEM(boxes[1], full)]
    )

    row_knots, col_knots = height // SPACING, width // SPACING
    row_at = jnp.arange(window, dtype=jnp.int32)
    table_y = spline_table(half * (height // 2) - EDGE, window, -2, row_knots + 4)
    table_y = jnp.where(((row_at >= EDGE) & (row_at < window - EDGE))[:, None], table_y, 0.0).T
    stacked = 3 * window + -3 * window % 128
    table_y = jnp.pad(jnp.kron(jnp.eye(3, dtype=full), table_y), ((0, 0), (0, stacked - 3 * window)))
    high, low = table_halves(table_y)
    table_y = jnp.concatenate([high, low, high], axis=1)
    high, low = table_halves(spline_table(side * BLK_X, span, side * col_knots, col_knots))
    table_x = jnp.pad(jnp.concatenate([high, low], axis=1), ((0, 0), (0, -2 * col_knots % 128)))
    (part,) = local_kernel(
        functools.partial(main_kernel, tiles),
        [((3 * (row_knots + 4), col_knots), full)],
        [fixed, warped, fixed_boxes, warped_boxes, rims, band, table_y, table_x],
        [
            pltpu.VMEM((planes, window, span), full),
            pltpu.VMEM((5, planes, 2 * EDGE, span), full),
            pltpu.VMEM((3, planes, window, span), full),
            pltpu.VMEM((stacked, span), full),
        ],
    )
    part = part.reshape(3, row_knots + 4, col_knots)
    across = lax.ppermute(part, "gz", swap)
    part_slant = lax.ppermute(part, trio, slant)
    part_straight = lax.ppermute(part, trio, straight)
    below = jnp.where(half == 0, part_slant, part_straight)
    above = jnp.where(half == 0, part_straight, part_slant)
    below = jnp.where(me == tiles - 1, 0.0, below[:, :2])
    above = jnp.where(me == 0, 0.0, above[:, row_knots + 2 :])
    middle = part[:, 2 : row_knots + 2] + across[:, 2 : row_knots + 2]
    return (middle + jnp.concatenate([above, below], axis=1))[:, None]


def solution(mesh):
    sizes = mesh.shape
    tiles = sizes["tile"]
    fast = sizes["gz"] == 2 and sizes["rep"] == 2 and tiles & (tiles - 1) == 0 and tiles > 1
    return jax.shard_map(
        functools.partial(fast_body, tiles) if fast else body,
        mesh=mesh,
        in_specs=(
            P(("slab", "gz"), "tile", "rep"),
            P(("slab", "gz"), "tile", "rep"),
            P("slab", "rep", None, None),
            P(("slab", "tile"), "rep", None, None),
        ),
        out_specs=P(None, "slab", "tile", "rep"),
        check_vma=False,
    )
```

```python
import functools

import jax
import jax.numpy as jnp
from jax import lax
from jax.experimental import pallas as pl
from jax.experimental.pallas import tpu as pltpu
from jax.sharding import PartitionSpec as P

BLK_Y = 16
BLK_X = 128
RAD = 2
SPACING = 16
MAX_NAMED = 4


den_floor = 1e-05

def with_halo(array, sides, width):
    for axis, dim in sides:
        count, length = (lax.axis_size(axis), array.shape[dim])
        up = [(i, (i + 1) % count) for i in range(count - 1)]
        down = [(j, i) for i, j in up]
        last = lax.slice_in_dim(array, length - width, length, axis=dim)
        first = lax.slice_in_dim(array, 0, width, axis=dim)
        before = lax.ppermute(last, axis, up)
        after = lax.ppermute(first, axis, down)
        array = jnp.concatenate([before, array, after], axis=dim)
    return array


def window_sum(extended, radius):
    result = extended
    for axis_id in range(3):
        length = result.shape[axis_id] - 2 * radius
        summed = lax.slice_in_dim(result, 0, length, axis=axis_id)
        for offset in range(1, 2 * radius + 1):
            summed = summed + lax.slice_in_dim(result, offset, offset + length, axis=axis_id)
        result = summed
    return result


def window_terms(ext_fixed, ext_warp, radius):
    volume = float((2 * radius + 1) ** 3)
    sum_fixed = window_sum(ext_fixed, radius)
    sum_warp = window_sum(ext_warp, radius)
    sum_fixed_sq = window_sum(ext_fixed * ext_fixed, radius)
    sum_warp_sq = window_sum(ext_warp * ext_warp, radius)
    sum_product = window_sum(ext_fixed * ext_warp, radius)
    cross_term = sum_product - sum_fixed * sum_warp / volume
    fixed_var = sum_fixed_sq - sum_fixed * sum_fixed / volume
    warp_var = sum_warp_sq - sum_warp * sum_warp / volume
    denominator = fixed_var * warp_var + den_floor
    term_a = 2.0 * cross_term / denominator
    term_b = -cross_term * cross_term * fixed_var / (denominator * denominator)
    term_c = -(term_a * sum_fixed + 2.0 * term_b * sum_warp) / volume
    return (term_a, term_b, term_c)


def slopes(extended, margin, extent):
    result = []
    for axis_id in range(3):
        ahead = [margin, margin, margin]
        behind = [margin, margin, margin]
        ahead[axis_id] += 1
        behind[axis_id] -= 1
        upper = lax.slice(
            extended,
            tuple(ahead),
            (ahead[0] + extent[0], ahead[1] + extent[1], ahead[2] + extent[2]),
        )
        lower = lax.slice(
            extended,
            tuple(behind),
            (behind[0] + extent[0], behind[1] + extent[1], behind[2] + extent[2]),
        )
        result.append(0.5 * (upper - lower))
    return result


def spline_table(first_pos, length, first_col, columns):
    places = first_pos + jnp.arange(length, dtype=jnp.int32)
    knots = places // SPACING
    within = (places - knots * SPACING).astype(jnp.float32) / SPACING
    squares = within * within
    cubes = squares * within
    weights = (
        (1.0 - within) ** 3 / 6.0,
        (3.0 * cubes - 6.0 * squares + 4.0) / 6.0,
        (-3.0 * cubes + 3.0 * squares + 3.0 * within + 1.0) / 6.0,
        cubes / 6.0,
    )
    targets = first_col + jnp.arange(columns, dtype=jnp.int32)
    table = jnp.zeros((length, columns), jnp.float32)
    for offset in range(4):
        table = table + jnp.where(
            targets[None, :] == (knots + offset - 1)[:, None], weights[offset][:, None], 0.0
        )
    return table


def contract(pieces, table_z, table_y, table_x):
    highest = lax.Precision.HIGHEST
    along_x = jnp.einsum("czyx,xk->czyk", pieces, table_x, precision=highest)
    along_y = jnp.einsum("czyk,yj->czjk", along_x, table_y, precision=highest)
    return jnp.einsum("czjk,zl->cljk", along_y, table_z, precision=highest)


def roll_block(block, amounts):
    return jnp.roll(jnp.roll(block, amounts[0], axis=1), amounts[1], axis=2)


def fold_rims(extended, axis_id, owned):
    middle = lax.slice_in_dim(extended, 4, owned + 4, axis=axis_id)
    leading = lax.slice_in_dim(extended, 0, 2, axis=axis_id)
    trailing = lax.slice_in_dim(extended, owned + 6, owned + 8, axis=axis_id)
    lead_pad = [(0, 0), (0, 0), (0, 0), (0, 0)]
    trail_pad = [(0, 0), (0, 0), (0, 0), (0, 0)]
    lead_pad[axis_id] = (0, owned - 2)
    trail_pad[axis_id] = (owned - 2, 0)
    return middle + jnp.pad(leading, lead_pad) + jnp.pad(trailing, trail_pad)


def body(fixed_image, moving_image, source_tile, block_shifts):
    depth, height, width = fixed_image.shape
    yblocks = height // BLK_Y
    xblocks = width // BLK_X
    block_count = yblocks * xblocks
    tile_lists = source_tile[:, 0, :, 0]
    my_tile = lax.axis_index("tile")
    own_list = lax.dynamic_index_in_dim(tile_lists, my_tile, 0, keepdims=False)
    row_steps = jnp.arange(BLK_Y, dtype=jnp.int32)
    initial = jnp.zeros((block_count, depth, BLK_Y, BLK_X), jnp.bfloat16)
    piece = lax.all_gather(moving_image, "tile", axis=1, tiled=True)
    length = piece.shape[1]
    held_blocks = []
    for block_id in range(block_count):
        row_block = block_id // xblocks
        col_block = block_id % xblocks
        wanted = own_list[block_id] * height + row_block * BLK_Y + row_steps
        usable = (wanted >= 0) & (wanted < length)
        columns_part = lax.slice_in_dim(piece, col_block * BLK_X, (col_block + 1) * BLK_X, axis=2)
        taken = jnp.take(columns_part, jnp.clip(wanted, 0, length - 1), axis=1)
        held_blocks.append(jnp.where(usable[None, :, None], taken, initial[block_id]))
    blocks = jnp.stack(held_blocks)
    rolled = jax.vmap(roll_block)(blocks, block_shifts[0, 0])
    warped = (
        rolled.reshape(yblocks, xblocks, depth, BLK_Y, BLK_X)
        .transpose(2, 0, 3, 1, 4)
        .reshape(depth, height, width)
    )
    image_pair = jnp.stack((fixed_image, warped))
    fixed_own = fixed_image.astype(jnp.float32)
    warp_own = warped.astype(jnp.float32)
    extended = with_halo(image_pair, (("tile", 2), ("gz", 1), ("rep", 3)), RAD).astype(jnp.float32)
    term_a, term_b, term_c = window_terms(extended[0], extended[1], RAD)
    terms_ext = with_halo(
        jnp.stack((term_a, term_b, term_c)).astype(jnp.bfloat16),
        (("tile", 2), ("gz", 1), ("rep", 3)),
        RAD,
    ).astype(jnp.float32)
    box_a = window_sum(terms_ext[0], RAD)
    box_b = window_sum(terms_ext[1], RAD)
    box_c = window_sum(terms_ext[2], RAD)
    margin = RAD
    gain = -(fixed_own * box_a + 2.0 * warp_own * box_b + box_c)
    slope_z, slope_y, slope_x = slopes(extended[1], margin, (depth, height, width))
    pieces = jnp.stack((gain * slope_z, gain * slope_y, gain * slope_x))
    depth_total = depth * lax.axis_size("gz")
    depth_knots = (depth_total + SPACING - 1) // SPACING
    table_z = spline_table(lax.axis_index("gz") * depth, depth, 0, depth_knots)
    row_knots = height // SPACING
    table_y = spline_table(my_tile * height, height, my_tile * row_knots - 2, row_knots + 4)
    col_knots = width // SPACING
    rep_index = lax.axis_index("rep")
    table_x = spline_table(rep_index * width, width, rep_index * col_knots - 2, col_knots + 4)
    local_grad = contract(pieces, table_z, table_y, table_x)
    spread = with_halo(local_grad, (("tile", 2), ("rep", 3)), 2)
    owned_grad = fold_rims(fold_rims(spread, 2, row_knots), 3, col_knots)
    return lax.psum(owned_grad, "gz")


EDGE = 2 * RAD
KEEP_ROWS, SEND_ROWS = 48, 40
KERNEL_BYTES = 24 << 20


def far_first(tiles):
    return sorted(range(1, tiles), key=lambda step: (step < 2, step))


def send_window(half, image, out):
    rows = out.shape[1]
    value = image[...].astype(jnp.float32)
    value = jnp.where(half == 1, value[:, :rows], value[:, value.shape[1] - rows :])
    out[...] = value.astype(out.dtype)


def pack_kernel(tiles, source_ref, source_in, moving_ref, fixed_ref, *out_refs):
    *packs, source_out, moving_out, fixed_out, send_out = out_refs
    source_out[...] = source_in[...]
    moving_out[...] = moving_ref[...]
    fixed_out[...] = fixed_ref[...]
    me = lax.axis_index("tile")
    half = lax.rem(me + lax.axis_index("gz"), 2)
    send_window(half, fixed_ref, send_out)
    height, width = moving_ref.shape[1:]
    xblocks = width // BLK_X
    blocks = (height // BLK_Y) * xblocks
    cap = packs[0].shape[0]
    for step, pack in zip(far_first(tiles), packs):
        other = lax.bitwise_xor(me, step)
        count = jnp.int32(0)
        chosen = [jnp.int32(0)] * cap
        for block in range(blocks):
            named = source_ref[other, block] == me
            chosen = [jnp.where(named & (count == slot), block, old) for slot, old in enumerate(chosen)]
            count = count + named.astype(jnp.int32)
        for slot, block in enumerate(chosen):
            row = pl.multiple_of(block // xblocks * BLK_Y, BLK_Y)
            col = pl.multiple_of(lax.rem(block, xblocks) * BLK_X, BLK_X)
            pack[slot] = moving_ref[:, pl.ds(row, BLK_Y), pl.ds(col, BLK_X)]


def unpack_kernel(tiles, source_ref, shift_ref, moving_ref, *refs):
    recvs = dict(zip(far_first(tiles), refs))
    own_ref, send_ref = refs[tiles - 1 :]
    me = lax.axis_index("tile")
    half = lax.rem(me + lax.axis_index("gz"), 2)
    height, width = moving_ref.shape[1:]
    xblocks = width // BLK_X
    blocks = (height // BLK_Y) * xblocks
    cap = refs[0].shape[0]
    for block in range(blocks):
        row, col = (block // xblocks) * BLK_Y, (block % xblocks) * BLK_X
        source = source_ref[me, block]
        slot = jnp.int32(0)
        for earlier in range(block):
            slot = slot + (source_ref[me, earlier] == source).astype(jnp.int32)
        slot = jnp.minimum(slot, cap - 1)
        step = lax.bitwise_xor(source, me)
        value = moving_ref[:, row : row + BLK_Y, col : col + BLK_X].astype(jnp.float32)
        for other in range(1, tiles):
            value = jnp.where(step == other, recvs[other][slot].astype(jnp.float32), value)
        down = lax.rem(shift_ref[block, 0], BLK_Y)
        right = lax.rem(shift_ref[block, 1], BLK_X)
        value = pltpu.roll(value, right, 2)
        for bit in (1, 2, 4, 8):
            value = jnp.where(lax.bitwise_and(down, bit) != 0, pltpu.roll(value, bit, 1), value)
        own_ref[:, row : row + BLK_Y, col : col + BLK_X] = value.astype(own_ref.dtype)
    send_window(half, own_ref, send_ref)


def side_kernel(own_ref, got_ref, *refs):
    out_ref = refs[-1]
    group = lax.axis_index("gz")
    half = lax.rem(lax.axis_index("tile") + group, 2)
    depth = own_ref.shape[0]
    col = pl.multiple_of((1 - lax.axis_index("rep")) * BLK_X, BLK_X)
    start = pl.multiple_of(half * BLK_Y, BLK_Y)
    for i in range(depth):
        out_ref[group * depth + i] = own_ref[i, pl.ds(start, KEEP_ROWS), pl.ds(col, BLK_X)]
        theirs = got_ref[i, :, pl.ds(col, BLK_X)].astype(jnp.float32)
        theirs = jnp.concatenate([theirs, jnp.zeros((KEEP_ROWS - SEND_ROWS, BLK_X), jnp.float32)], axis=0)
        out_ref[(1 - group) * depth + i] = theirs.astype(out_ref.dtype)


def edge_kernel(own_ref, got_ref, fixed_ref, side_ref, rim_ref, far_ref, rims):
    side_kernel(own_ref, got_ref, side_ref)
    group, side = lax.axis_index("gz"), lax.axis_index("rep")
    half = lax.rem(lax.axis_index("tile") + group, 2)
    depth, height, width = own_ref.shape
    tile = 2 * EDGE
    upper = lax.broadcasted_iota(jnp.int32, (tile, width), 0) < EDGE
    own_start = pl.multiple_of(half * (height - BLK_Y), BLK_Y)
    own_col = pl.multiple_of(side * BLK_X, BLK_X)

    def pair(low, high):
        top = jnp.where(upper, low[:tile], pltpu.roll(high[:tile], EDGE, 0))
        end = jnp.where(upper, pltpu.roll(low[-tile:], EDGE, 0), high[-tile:])
        return jnp.where(half == 0, top, end)

    for i in range(0, depth, 2):
        mine = pl.multiple_of((group * depth + i) * EDGE, tile)
        theirs = pl.multiple_of(((1 - group) * depth + i) * EDGE, tile)
        rims[1, pl.ds(mine, tile), :] = pair(
            *(own_ref[i + k, pl.ds(own_start, BLK_Y), :].astype(jnp.float32) for k in range(2))
        )
        rims[1, pl.ds(theirs, tile), :] = pair(*(got_ref[i + k].astype(jnp.float32) for k in range(2)))
    for z in range(0, 2 * depth, 2):
        low, high = (fixed_ref[z + k, :, pl.ds(own_col, width)] for k in range(2))
        top = jnp.where(upper, pltpu.roll(low[:tile], EDGE, 0), high[:tile])
        end = jnp.where(upper, low[-tile:], pltpu.roll(high[-tile:], EDGE, 0))
        rims[0, z * EDGE : z * EDGE + tile, :] = jnp.where(half == 0, top, end)
    rim_ref[...] = rims[...].astype(rim_ref.dtype)
    far_col = pl.multiple_of((1 - side) * BLK_X, BLK_X)
    far_ref[...] = rims[:, :, pl.ds(far_col, BLK_X)].astype(far_ref.dtype)


def five(array, axis):
    size = array.shape[axis]
    pair = array + pltpu.roll(array, 1, axis)
    return pltpu.roll(pair, size - 2, axis) + pair + pltpu.roll(array, 2, axis)


def lane_limits(side, width, span):
    return jnp.where(side == 0, 0, BLK_X - 48), jnp.where(side == 0, width + 32, span)


def assemble(own, got, near_in, image):
    group, side = lax.axis_index("gz"), lax.axis_index("rep")
    half = lax.rem(lax.axis_index("tile") + group, 2)
    depth, _, width = own.shape
    window, span = image.shape[1:]
    own_col = pl.multiple_of(side * BLK_X, BLK_X)
    new_col = pl.multiple_of((1 - side) * width, BLK_X)
    start = pl.multiple_of(half * BLK_Y, BLK_Y)
    low, high = lane_limits(side, width, span)
    lanes = lax.broadcasted_iota(jnp.int32, (window, BLK_X), 1) + new_col
    levels = lax.broadcasted_iota(jnp.int32, (window, BLK_X), 0)
    inner = (levels >= jnp.where(half == 0, EDGE, 0)) & (levels < jnp.where(half == 0, window, window - EDGE))
    near = inner & (lanes >= low) & (lanes < high)

    def shift_in(piece, skip):
        turn = jnp.where(half == 0, EDGE, piece.shape[0] - skip)
        return pltpu.roll(piece.astype(jnp.float32), turn, 0)[:window]

    for i in range(depth):
        mine, theirs = (group * depth + i, BLK_Y - EDGE), ((1 - group) * depth + i, EDGE)
        for (plane, skip), piece in ((mine, own[i, pl.ds(start, KEEP_ROWS), :]), (theirs, got[i])):
            piece = shift_in(piece, skip)
            for part in range(width // BLK_X):
                col = pl.multiple_of(own_col + part * BLK_X, BLK_X)
                value = piece[:, part * BLK_X : (part + 1) * BLK_X]
                image[plane, :, pl.ds(col, BLK_X)] = jnp.where(inner, value, 0.0)
        for plane, skip in (mine, theirs):
            image[plane, :, pl.ds(new_col, BLK_X)] = jnp.where(near, shift_in(near_in[plane], skip), 0.0)


def fill_band(band):
    span = band.shape[0]
    across = lax.broadcasted_iota(jnp.int32, (span, span), 0) - lax.broadcasted_iota(jnp.int32, (span, span), 1)
    band[...] = jnp.where(jnp.abs(across) <= RAD, 1.0, 0.0).astype(band.dtype)


def halves(value):
    high = value.astype(jnp.bfloat16)
    return high, (value - high.astype(jnp.float32)).astype(jnp.bfloat16)


def table_halves(table):
    high = lax.reduce_precision(table, exponent_bits=8, mantissa_bits=7)
    return high.astype(jnp.bfloat16), (table - high).astype(jnp.bfloat16)


def lane_sums(exact, products, band):
    rows = (exact + products)[0].shape[0]
    low = [value - value.astype(jnp.bfloat16).astype(jnp.float32) for value in products]
    boxed = jnp.dot(
        jnp.concatenate(exact + products + low, axis=0).astype(jnp.bfloat16), band[...],
        preferred_element_type=jnp.float32,
    )
    pieces = [boxed[k * rows : (k + 1) * rows] for k in range(len(exact) + 2 * len(products))]
    first = len(exact)
    return pieces[:first] + [
        pieces[first + k] + pieces[first + len(products) + k] for k in range(len(products))
    ]


def near_planes(z, planes):
    return range(max(0, z - RAD), min(planes, z + RAD + 1))


def total(values):
    values = list(values)
    result = values[0]
    for value in values[1:]:
        result = result + value
    return result


def sum_planes(rows, boxes):
    for which in range(boxes.shape[0]):
        for z in range(boxes.shape[1]):
            boxes[which, z] = total(rows[which, k] for k in near_planes(z, boxes.shape[1]))


def fixed_kernel(own, got, near_in, image, boxes, band, rows):
    assemble(own, got, near_in, image)
    fill_band(band)
    for z in range(image.shape[0]):
        f = image[z]
        for which, value in enumerate(lane_sums([f], [f * f], band)):
            rows[which, z] = five(value, 0)
    sum_planes(rows, boxes)


def warped_kernel(own, got, near_in, image):
    assemble(own, got, near_in, image)


def cross_kernel(fixed, warped, band, boxes, rows):
    for z in range(fixed.shape[0]):
        f, w = fixed[z], warped[z]
        for which, value in enumerate(lane_sums([w], [w * w, f * w], band)):
            rows[which, z] = five(value, 0)
    sum_planes(rows, boxes)


def main_kernel(
    tiles, fixed, warped, fixed_boxes, warped_boxes, rims, far_rims, band, table_x,
    out_ref, images, edges, terms, sums, whole_rims,
):
    side, me = lax.axis_index("rep"), lax.axis_index("tile")
    half = lax.rem(me + lax.axis_index("gz"), 2)
    first = jnp.where(half == 0, (me == 0).astype(jnp.int32), 0)
    last = jnp.where(half == 1, (me == tiles - 1).astype(jnp.int32), 0)
    planes, window, span = fixed.shape
    tile = 2 * EDGE
    lanes = lax.broadcasted_iota(jnp.int32, (window, span), 1)
    levels = lax.broadcasted_iota(jnp.int32, (window, span), 0)
    low_lane, high_lane = lane_limits(side, span - BLK_X, span)
    low_row = jnp.where(first != 0, EDGE, RAD)
    high_row = jnp.where(last != 0, window - EDGE, window - RAD)
    inside = (lanes >= low_lane) & (lanes < high_lane) & (levels >= low_row) & (levels < high_row)

    outer = (first + last) != 0
    width = rims.shape[2]
    own_col = pl.multiple_of(side * BLK_X, BLK_X)
    new_col = pl.multiple_of((1 - side) * width, BLK_X)
    far_lanes = lax.broadcasted_iota(jnp.int32, far_rims.shape[1:], 1) + new_col
    far = (far_lanes >= low_lane) & (far_lanes < high_lane)
    for which in range(2):
        whole_rims[which, :, pl.ds(own_col, width)] = rims[which].astype(jnp.float32)
        whole_rims[which, :, pl.ds(new_col, BLK_X)] = jnp.where(far, far_rims[which].astype(jnp.float32), 0.0)
    rim_f = jnp.where(outer, 0.0, whole_rims[0])
    rim_w = jnp.where(outer, 0.0, whole_rims[1])
    rim_sums = lane_sums([rim_f, rim_w], [rim_f * rim_f, rim_w * rim_w, rim_f * rim_w], band)
    at = lax.broadcasted_iota(jnp.int32, (tile, span), 0)
    upper = at < EDGE
    on_top, on_end = jnp.where(half == 0, 1.0, 0.0), jnp.where(half == 0, 0.0, 1.0)
    held = (at >= jnp.where(half == 0, 0, EDGE)) & (at < jnp.where(half == 0, EDGE, tile))
    reach = (at >= jnp.where(half == 0, 0, RAD)) & (at < jnp.where(half == 0, tile - RAD, tile))

    def rim_tile(rim, z):
        pair = rim[z // 2 * tile : (z // 2 + 1) * tile]
        other = pltpu.roll(pair, EDGE, 0)
        both = jnp.where(upper, pair, other) if z % 2 == 0 else jnp.where(upper, other, pair)
        return jnp.where(held, both, 0.0)

    def with_tile(value, extra):
        return jnp.concatenate(
            [value[:tile] + extra * on_top, value[tile : window - tile], value[window - tile :] + extra * on_end],
            axis=0,
        )

    for which in range(5):
        for z in range(planes):
            edges[which, z] = jnp.where(reach, five(rim_tile(rim_sums[which], z), 0), 0.0)
    for z in range(planes):
        images[z] = with_tile(warped[z], rim_tile(rim_w, z))

    volume = float((2 * RAD + 1) ** 3)
    sources = (fixed_boxes, 0), (warped_boxes, 0), (fixed_boxes, 1), (warped_boxes, 1), (warped_boxes, 2)
    for z in range(planes):
        sum_f, sum_w, sum_ff, sum_ww, sum_fw = (
            with_tile(source[index, z], total(edges[which, k] for k in near_planes(z, planes)))
            for which, (source, index) in enumerate(sources)
        )
        cross = sum_fw - sum_f * sum_w * (1.0 / volume)
        var_f = sum_ff - sum_f * sum_f * (1.0 / volume)
        var_w = sum_ww - sum_w * sum_w * (1.0 / volume)
        inverse = 1.0 / (var_f * var_w + den_floor)
        ratio = cross * inverse
        term_a = 2.0 * ratio
        term_b = -(ratio * ratio) * var_f
        term_c = -(term_a * sum_f + 2.0 * term_b * sum_w) * (1.0 / volume)
        values = [five(jnp.where(inside, value, 0.0), 0) for value in (term_a, term_b, term_c)]
        for which, value in enumerate(lane_sums([], values, band)):
            terms[which, z] = value

    for d in range(3):
        sums[d] = jnp.zeros((window, span), jnp.float32)
    owned = (levels >= EDGE) & (levels < window - EDGE)
    for z in range(planes):
        box_a, box_b, box_c = (total(terms[which, k] for k in near_planes(z, planes)) for which in range(3))
        f, w = fixed[z], images[z]
        gain = -(f * box_a + 2.0 * w * box_b + box_c)
        u = z / SPACING
        weight = (3.0 * u * u * u - 6.0 * u * u + 4.0) * (0.5 / 6.0)
        gain = jnp.where(owned, gain, 0.0) * weight
        ahead = images[z + 1] if z + 1 < planes else 0.0
        behind = images[z - 1] if z > 0 else 0.0
        sums[0] += gain * (ahead - behind)
        sums[1] += gain * (pltpu.roll(w, window - 1, 0) - pltpu.roll(w, 1, 0))
        sums[2] += gain * (pltpu.roll(w, span - 1, 1) - pltpu.roll(w, 1, 1))

    knots = window // SPACING
    at_row = lax.broadcasted_iota(jnp.int32, (window, BLK_X), 0) - EDGE
    knot = lax.shift_right_arithmetic(at_row, 4)
    u = (at_row - knot * SPACING).astype(jnp.float32) * (1.0 / SPACING)
    square = u * u
    cube = square * u
    weights = (
        (1.0 - u) * (1.0 - u) * (1.0 - u) * (1.0 / 6.0),
        (3.0 * cube - 6.0 * square + 4.0) * (1.0 / 6.0),
        (-3.0 * cube + 3.0 * square + 3.0 * u + 1.0) * (1.0 / 6.0),
        cube * (1.0 / 6.0),
    )
    at_knot = lax.broadcasted_iota(jnp.int32, (tile, span), 0)
    stack = []
    columns = []
    for target in range(knots + 3):
        column = jnp.zeros((window, BLK_X), jnp.float32)
        for offset in range(4):
            column = jnp.where(knot == target - offset, weights[offset], column)
        column = jnp.where((at_row >= 0) & (at_row < window - tile), column, 0.0)
        columns.append(jnp.concatenate([column] * (span // BLK_X), axis=1))
    for d in range(3):
        found = jnp.zeros((tile, span), jnp.float32)
        for target, column in enumerate(columns):
            line = jnp.sum(sums[d] * column, axis=0, keepdims=True)
            found = jnp.where(at_knot == target, line, found)
        stack.append(jnp.where(half == 0, pltpu.roll(found, 1, 0), pltpu.roll(found, 1 + knots, 0)))
    boxed = jnp.dot(
        jnp.concatenate(halves(jnp.concatenate(stack, axis=0)), axis=0), table_x[...],
        preferred_element_type=jnp.float32,
    )
    rows, count = out_ref.shape
    along_x = boxed[:rows] + pltpu.roll(boxed[:rows], boxed.shape[1] - count, 1) + boxed[rows:]
    out_ref[...] = along_x[:, :count]


def local_kernel(kernel, outs, arrays, scratch=()):
    vmem = pl.BlockSpec(memory_space=pltpu.VMEM)
    return pl.pallas_call(
        kernel,
        out_shape=[pltpu.VMEM(shape, dtype) for shape, dtype in outs],
        in_specs=[vmem] * len(arrays),
        out_specs=[vmem] * len(outs),
        scratch_shapes=list(scratch),
        compiler_params=pltpu.CompilerParams(vmem_limit_bytes=KERNEL_BYTES),
    )(*(pltpu.with_memory_space_constraint(array, pltpu.VMEM) for array in arrays))


def fast_body(tiles, fixed_image, moving_image, source_tile, block_shifts):
    depth, height, width = fixed_image.shape
    me, group, side = lax.axis_index("tile"), lax.axis_index("gz"), lax.axis_index("rep")
    half = lax.rem(me + group, 2)
    sources = source_tile[:, 0, :, 0]
    shifts = block_shifts[0, 0]
    cap = MAX_NAMED if tiles == 4 else sources.shape[1]
    planes = 2 * depth
    window, span = height // 2 + 2 * EDGE, width + BLK_X
    short, full = jnp.bfloat16, jnp.float32
    whole, send_shape = (fixed_image.shape, short), ((depth, SEND_ROWS, width), short)
    side_shape = ((planes, KEEP_ROWS, BLK_X), short)
    image_shape = ((planes, window, span), full)
    smem, vmem = (pl.BlockSpec(memory_space=space) for space in (pltpu.SMEM, pltpu.VMEM))
    outs = [((cap, depth, BLK_Y, BLK_X), short)] * (tiles - 1) + [(sources.shape, jnp.int32), whole, whole, send_shape]
    *packs, sources, moving_image, fixed_image, fixed_send = pl.pallas_call(
        functools.partial(pack_kernel, tiles),
        out_shape=[pltpu.VMEM(*out) for out in outs],
        in_specs=[smem, vmem, vmem, vmem],
        out_specs=[vmem] * len(outs),
    )(sources, sources, moving_image, fixed_image)

    trio = ("tile", "gz", "rep")

    def number(t, g, r):
        return (t * 2 + g) * 2 + r

    swap = [(0, 1), (1, 0)]
    straight, slant, crossed = [], [], []
    for r in range(2):
        for t in range(tiles):
            for g in range(2):
                to = t - 1 if (g + t) % 2 == 0 else t + 1
                there = 0 <= to < tiles
                straight.append((number(t, g, r), number(to, g, r) if there else number(t, g, 1 - r)))
                crossed.append((number(t, g, r), number(to if there else t, g, 1 - r)))
                slant.append((number(t, g, r), number(to if there else t, 1 - g, r)))

    got = [
        lax.ppermute(pack, "tile", [(t, t ^ step) for t in range(tiles)])
        for step, pack in zip(far_first(tiles), packs)
    ]
    fixed_got = lax.ppermute(fixed_send, "gz", swap)
    own, send = local_kernel(
        functools.partial(unpack_kernel, tiles), [whole, send_shape], [sources, shifts, moving_image, *got]
    )
    warp_got = lax.ppermute(send, "gz", swap)
    (fixed_side,) = local_kernel(side_kernel, [side_shape], [fixed_image, fixed_got])
    fixed_near = lax.ppermute(fixed_side, "rep", swap)
    boxes = [(count, planes, window, span) for count in (2, 3)]
    fixed, fixed_boxes, band = local_kernel(
        fixed_kernel,
        [image_shape, (boxes[0], full), ((span, span), short)],
        [fixed_image, fixed_got, fixed_near],
        [pltpu.VMEM(boxes[0], full)],
    )
    rim_shape = (2, planes * EDGE, width)
    warp_side, rims, far_rims = local_kernel(
        edge_kernel,
        [side_shape, (rim_shape, short), ((2, planes * EDGE, BLK_X), short)],
        [own, warp_got, fixed],
        [pltpu.VMEM(rim_shape, full)],
    )
    warp_near = lax.ppermute(warp_side, "rep", swap)
    rims = lax.ppermute(rims, trio, straight)
    far_rims = lax.ppermute(far_rims, trio, crossed)
    (warped,) = local_kernel(warped_kernel, [image_shape], [own, warp_got, warp_near])
    (warped_boxes,) = local_kernel(
        cross_kernel, [(boxes[1], full)], [fixed, warped, band], [pltpu.VMEM(boxes[1], full)]
    )

    row_knots, col_knots = height // SPACING, width // SPACING
    high, low = table_halves(spline_table(side * BLK_X, span, side * col_knots, col_knots))
    table_x = jnp.pad(jnp.concatenate([high, low], axis=1), ((0, 0), (0, -2 * col_knots % 128)))
    (part,) = local_kernel(
        functools.partial(main_kernel, tiles),
        [((3 * (row_knots + 4), col_knots), full)],
        [fixed, warped, fixed_boxes, warped_boxes, rims, far_rims, band, table_x],
        [
            pltpu.VMEM((planes, window, span), full),
            pltpu.VMEM((5, planes, 2 * EDGE, span), full),
            pltpu.VMEM((3, planes, window, span), full),
            pltpu.VMEM((3, window, span), full),
            pltpu.VMEM((2, planes * EDGE, span), full),
        ],
    )
    part = part.reshape(3, row_knots + 4, col_knots)
    across = lax.ppermute(part, "gz", swap)
    part_slant = lax.ppermute(part, trio, slant)
    part_straight = lax.ppermute(part, trio, straight)
    below = jnp.where(half == 0, part_slant, part_straight)
    above = jnp.where(half == 0, part_straight, part_slant)
    below = jnp.where(me == tiles - 1, 0.0, below[:, :2])
    above = jnp.where(me == 0, 0.0, above[:, row_knots + 2 :])
    middle = part[:, 2 : row_knots + 2] + across[:, 2 : row_knots + 2]
    return (middle + jnp.concatenate([above, below], axis=1))[:, None]


def solution(mesh):
    sizes = mesh.shape
    tiles = sizes["tile"]
    fast = sizes["gz"] == 2 and sizes["rep"] == 2 and tiles & (tiles - 1) == 0 and tiles > 1
    return jax.shard_map(
        functools.partial(fast_body, tiles) if fast else body,
        mesh=mesh,
        in_specs=(
            P(("slab", "gz"), "tile", "rep"),
            P(("slab", "gz"), "tile", "rep"),
            P("slab", "rep", None, None),
            P(("slab", "tile"), "rep", None, None),
        ),
        out_specs=P(None, "slab", "tile", "rep"),
        check_vma=False,
    )
```

```python
import functools

import jax
import jax.numpy as jnp
from jax import lax
from jax.experimental import pallas as pl
from jax.experimental.pallas import tpu as pltpu
from jax.sharding import PartitionSpec as P

BLK_Y = 16
BLK_X = 128
RAD = 2
SPACING = 16
MAX_NAMED = 4


den_floor = 1e-05

def with_halo(array, sides, width):
    for axis, dim in sides:
        count, length = (lax.axis_size(axis), array.shape[dim])
        up = [(i, (i + 1) % count) for i in range(count - 1)]
        down = [(j, i) for i, j in up]
        last = lax.slice_in_dim(array, length - width, length, axis=dim)
        first = lax.slice_in_dim(array, 0, width, axis=dim)
        before = lax.ppermute(last, axis, up)
        after = lax.ppermute(first, axis, down)
        array = jnp.concatenate([before, array, after], axis=dim)
    return array


def window_sum(extended, radius):
    result = extended
    for axis_id in range(3):
        length = result.shape[axis_id] - 2 * radius
        summed = lax.slice_in_dim(result, 0, length, axis=axis_id)
        for offset in range(1, 2 * radius + 1):
            summed = summed + lax.slice_in_dim(result, offset, offset + length, axis=axis_id)
        result = summed
    return result


def window_terms(ext_fixed, ext_warp, radius):
    volume = float((2 * radius + 1) ** 3)
    sum_fixed = window_sum(ext_fixed, radius)
    sum_warp = window_sum(ext_warp, radius)
    sum_fixed_sq = window_sum(ext_fixed * ext_fixed, radius)
    sum_warp_sq = window_sum(ext_warp * ext_warp, radius)
    sum_product = window_sum(ext_fixed * ext_warp, radius)
    cross_term = sum_product - sum_fixed * sum_warp / volume
    fixed_var = sum_fixed_sq - sum_fixed * sum_fixed / volume
    warp_var = sum_warp_sq - sum_warp * sum_warp / volume
    denominator = fixed_var * warp_var + den_floor
    term_a = 2.0 * cross_term / denominator
    term_b = -cross_term * cross_term * fixed_var / (denominator * denominator)
    term_c = -(term_a * sum_fixed + 2.0 * term_b * sum_warp) / volume
    return (term_a, term_b, term_c)


def slopes(extended, margin, extent):
    result = []
    for axis_id in range(3):
        ahead = [margin, margin, margin]
        behind = [margin, margin, margin]
        ahead[axis_id] += 1
        behind[axis_id] -= 1
        upper = lax.slice(
            extended,
            tuple(ahead),
            (ahead[0] + extent[0], ahead[1] + extent[1], ahead[2] + extent[2]),
        )
        lower = lax.slice(
            extended,
            tuple(behind),
            (behind[0] + extent[0], behind[1] + extent[1], behind[2] + extent[2]),
        )
        result.append(0.5 * (upper - lower))
    return result


def spline_table(first_pos, length, first_col, columns):
    places = first_pos + jnp.arange(length, dtype=jnp.int32)
    knots = places // SPACING
    within = (places - knots * SPACING).astype(jnp.float32) / SPACING
    squares = within * within
    cubes = squares * within
    weights = (
        (1.0 - within) ** 3 / 6.0,
        (3.0 * cubes - 6.0 * squares + 4.0) / 6.0,
        (-3.0 * cubes + 3.0 * squares + 3.0 * within + 1.0) / 6.0,
        cubes / 6.0,
    )
    targets = first_col + jnp.arange(columns, dtype=jnp.int32)
    table = jnp.zeros((length, columns), jnp.float32)
    for offset in range(4):
        table = table + jnp.where(
            targets[None, :] == (knots + offset - 1)[:, None], weights[offset][:, None], 0.0
        )
    return table


def contract(pieces, table_z, table_y, table_x):
    highest = lax.Precision.HIGHEST
    along_x = jnp.einsum("czyx,xk->czyk", pieces, table_x, precision=highest)
    along_y = jnp.einsum("czyk,yj->czjk", along_x, table_y, precision=highest)
    return jnp.einsum("czjk,zl->cljk", along_y, table_z, precision=highest)


def roll_block(block, amounts):
    return jnp.roll(jnp.roll(block, amounts[0], axis=1), amounts[1], axis=2)


def fold_rims(extended, axis_id, owned):
    middle = lax.slice_in_dim(extended, 4, owned + 4, axis=axis_id)
    leading = lax.slice_in_dim(extended, 0, 2, axis=axis_id)
    trailing = lax.slice_in_dim(extended, owned + 6, owned + 8, axis=axis_id)
    lead_pad = [(0, 0), (0, 0), (0, 0), (0, 0)]
    trail_pad = [(0, 0), (0, 0), (0, 0), (0, 0)]
    lead_pad[axis_id] = (0, owned - 2)
    trail_pad[axis_id] = (owned - 2, 0)
    return middle + jnp.pad(leading, lead_pad) + jnp.pad(trailing, trail_pad)


def body(fixed_image, moving_image, source_tile, block_shifts):
    depth, height, width = fixed_image.shape
    yblocks = height // BLK_Y
    xblocks = width // BLK_X
    block_count = yblocks * xblocks
    tile_lists = source_tile[:, 0, :, 0]
    my_tile = lax.axis_index("tile")
    own_list = lax.dynamic_index_in_dim(tile_lists, my_tile, 0, keepdims=False)
    row_steps = jnp.arange(BLK_Y, dtype=jnp.int32)
    initial = jnp.zeros((block_count, depth, BLK_Y, BLK_X), jnp.bfloat16)
    piece = lax.all_gather(moving_image, "tile", axis=1, tiled=True)
    length = piece.shape[1]
    held_blocks = []
    for block_id in range(block_count):
        row_block = block_id // xblocks
        col_block = block_id % xblocks
        wanted = own_list[block_id] * height + row_block * BLK_Y + row_steps
        usable = (wanted >= 0) & (wanted < length)
        columns_part = lax.slice_in_dim(piece, col_block * BLK_X, (col_block + 1) * BLK_X, axis=2)
        taken = jnp.take(columns_part, jnp.clip(wanted, 0, length - 1), axis=1)
        held_blocks.append(jnp.where(usable[None, :, None], taken, initial[block_id]))
    blocks = jnp.stack(held_blocks)
    rolled = jax.vmap(roll_block)(blocks, block_shifts[0, 0])
    warped = (
        rolled.reshape(yblocks, xblocks, depth, BLK_Y, BLK_X)
        .transpose(2, 0, 3, 1, 4)
        .reshape(depth, height, width)
    )
    image_pair = jnp.stack((fixed_image, warped))
    fixed_own = fixed_image.astype(jnp.float32)
    warp_own = warped.astype(jnp.float32)
    extended = with_halo(image_pair, (("tile", 2), ("gz", 1), ("rep", 3)), RAD).astype(jnp.float32)
    term_a, term_b, term_c = window_terms(extended[0], extended[1], RAD)
    terms_ext = with_halo(
        jnp.stack((term_a, term_b, term_c)).astype(jnp.bfloat16),
        (("tile", 2), ("gz", 1), ("rep", 3)),
        RAD,
    ).astype(jnp.float32)
    box_a = window_sum(terms_ext[0], RAD)
    box_b = window_sum(terms_ext[1], RAD)
    box_c = window_sum(terms_ext[2], RAD)
    margin = RAD
    gain = -(fixed_own * box_a + 2.0 * warp_own * box_b + box_c)
    slope_z, slope_y, slope_x = slopes(extended[1], margin, (depth, height, width))
    pieces = jnp.stack((gain * slope_z, gain * slope_y, gain * slope_x))
    depth_total = depth * lax.axis_size("gz")
    depth_knots = (depth_total + SPACING - 1) // SPACING
    table_z = spline_table(lax.axis_index("gz") * depth, depth, 0, depth_knots)
    row_knots = height // SPACING
    table_y = spline_table(my_tile * height, height, my_tile * row_knots - 2, row_knots + 4)
    col_knots = width // SPACING
    rep_index = lax.axis_index("rep")
    table_x = spline_table(rep_index * width, width, rep_index * col_knots - 2, col_knots + 4)
    local_grad = contract(pieces, table_z, table_y, table_x)
    spread = with_halo(local_grad, (("tile", 2), ("rep", 3)), 2)
    owned_grad = fold_rims(fold_rims(spread, 2, row_knots), 3, col_knots)
    return lax.psum(owned_grad, "gz")


EDGE = 2 * RAD
KEEP_ROWS, SEND_ROWS = 48, 40
KERNEL_BYTES = 24 << 20


def far_first(tiles):
    return sorted(range(1, tiles), key=lambda step: (step < 2, step))


def send_window(half, image, out):
    rows = out.shape[1]
    value = image[...].astype(jnp.float32)
    value = jnp.where(half == 1, value[:, :rows], value[:, value.shape[1] - rows :])
    out[...] = value.astype(out.dtype)


def pack_kernel(tiles, source_ref, source_in, moving_ref, fixed_ref, *out_refs):
    *packs, source_out, moving_out, fixed_out, send_out = out_refs
    source_out[...] = source_in[...]
    moving_out[...] = moving_ref[...]
    fixed_out[...] = fixed_ref[...]
    me = lax.axis_index("tile")
    half = lax.rem(me + lax.axis_index("gz"), 2)
    send_window(half, fixed_ref, send_out)
    height, width = moving_ref.shape[1:]
    xblocks = width // BLK_X
    blocks = (height // BLK_Y) * xblocks
    cap = packs[0].shape[0]
    for step, pack in zip(far_first(tiles), packs):
        other = lax.bitwise_xor(me, step)
        count = jnp.int32(0)
        chosen = [jnp.int32(0)] * cap
        for block in range(blocks):
            named = source_ref[other, block] == me
            chosen = [jnp.where(named & (count == slot), block, old) for slot, old in enumerate(chosen)]
            count = count + named.astype(jnp.int32)
        for slot, block in enumerate(chosen):
            row = pl.multiple_of(block // xblocks * BLK_Y, BLK_Y)
            col = pl.multiple_of(lax.rem(block, xblocks) * BLK_X, BLK_X)
            pack[slot] = moving_ref[:, pl.ds(row, BLK_Y), pl.ds(col, BLK_X)]


def unpack_kernel(tiles, source_ref, shift_ref, moving_ref, *refs):
    recvs = dict(zip(far_first(tiles), refs))
    own_ref, send_ref = refs[tiles - 1 :]
    me = lax.axis_index("tile")
    half = lax.rem(me + lax.axis_index("gz"), 2)
    height, width = moving_ref.shape[1:]
    xblocks = width // BLK_X
    blocks = (height // BLK_Y) * xblocks
    cap = refs[0].shape[0]
    for block in range(blocks):
        row, col = (block // xblocks) * BLK_Y, (block % xblocks) * BLK_X
        source = source_ref[me, block]
        slot = jnp.int32(0)
        for earlier in range(block):
            slot = slot + (source_ref[me, earlier] == source).astype(jnp.int32)
        slot = jnp.minimum(slot, cap - 1)
        step = lax.bitwise_xor(source, me)
        value = moving_ref[:, row : row + BLK_Y, col : col + BLK_X].astype(jnp.float32)
        for other in range(1, tiles):
            value = jnp.where(step == other, recvs[other][slot].astype(jnp.float32), value)
        down = lax.rem(shift_ref[block, 0], BLK_Y)
        right = lax.rem(shift_ref[block, 1], BLK_X)
        value = pltpu.roll(value, right, 2)
        for bit in (1, 2, 4, 8):
            value = jnp.where(lax.bitwise_and(down, bit) != 0, pltpu.roll(value, bit, 1), value)
        own_ref[:, row : row + BLK_Y, col : col + BLK_X] = value.astype(own_ref.dtype)
    send_window(half, own_ref, send_ref)


def side_kernel(own_ref, got_ref, *refs):
    out_ref = refs[-1]
    group = lax.axis_index("gz")
    half = lax.rem(lax.axis_index("tile") + group, 2)
    depth = own_ref.shape[0]
    col = pl.multiple_of((1 - lax.axis_index("rep")) * BLK_X, BLK_X)
    start = pl.multiple_of(half * BLK_Y, BLK_Y)
    for i in range(depth):
        out_ref[group * depth + i] = own_ref[i, pl.ds(start, KEEP_ROWS), pl.ds(col, BLK_X)]
        theirs = got_ref[i, :, pl.ds(col, BLK_X)].astype(jnp.float32)
        theirs = jnp.concatenate([theirs, jnp.zeros((KEEP_ROWS - SEND_ROWS, BLK_X), jnp.float32)], axis=0)
        out_ref[(1 - group) * depth + i] = theirs.astype(out_ref.dtype)


def edge_kernel(own_ref, got_ref, fixed_ref, side_ref, rim_ref, far_ref, rims):
    side_kernel(own_ref, got_ref, side_ref)
    group, side = lax.axis_index("gz"), lax.axis_index("rep")
    half = lax.rem(lax.axis_index("tile") + group, 2)
    depth, height, width = own_ref.shape
    tile = 2 * EDGE
    upper = lax.broadcasted_iota(jnp.int32, (tile, width), 0) < EDGE
    own_start = pl.multiple_of(half * (height - BLK_Y), BLK_Y)
    own_col = pl.multiple_of(side * BLK_X, BLK_X)

    def pair(low, high):
        top = jnp.where(upper, low[:tile], pltpu.roll(high[:tile], EDGE, 0))
        end = jnp.where(upper, pltpu.roll(low[-tile:], EDGE, 0), high[-tile:])
        return jnp.where(half == 0, top, end)

    for i in range(0, depth, 2):
        mine = pl.multiple_of((group * depth + i) * EDGE, tile)
        theirs = pl.multiple_of(((1 - group) * depth + i) * EDGE, tile)
        rims[1, pl.ds(mine, tile), :] = pair(
            *(own_ref[i + k, pl.ds(own_start, BLK_Y), :].astype(jnp.float32) for k in range(2))
        )
        rims[1, pl.ds(theirs, tile), :] = pair(*(got_ref[i + k].astype(jnp.float32) for k in range(2)))
    for z in range(0, 2 * depth, 2):
        low, high = (fixed_ref[z + k, :, pl.ds(own_col, width)] for k in range(2))
        top = jnp.where(upper, pltpu.roll(low[:tile], EDGE, 0), high[:tile])
        end = jnp.where(upper, low[-tile:], pltpu.roll(high[-tile:], EDGE, 0))
        rims[0, z * EDGE : z * EDGE + tile, :] = jnp.where(half == 0, top, end)
    rim_ref[...] = rims[...].astype(rim_ref.dtype)
    far_col = pl.multiple_of((1 - side) * BLK_X, BLK_X)
    far_ref[...] = rims[:, :, pl.ds(far_col, BLK_X)].astype(far_ref.dtype)


def five(array, axis):
    size = array.shape[axis]
    pair = array + pltpu.roll(array, 1, axis)
    return pltpu.roll(pair, size - 2, axis) + pair + pltpu.roll(array, 2, axis)


def lane_limits(side, width, span):
    return jnp.where(side == 0, 0, BLK_X - 48), jnp.where(side == 0, width + 32, span)


def assemble(own, got, near_in, image):
    group, side = lax.axis_index("gz"), lax.axis_index("rep")
    half = lax.rem(lax.axis_index("tile") + group, 2)
    depth, _, width = own.shape
    window, span = image.shape[1:]
    own_col = pl.multiple_of(side * BLK_X, BLK_X)
    new_col = pl.multiple_of((1 - side) * width, BLK_X)
    start = pl.multiple_of(half * BLK_Y, BLK_Y)
    low, high = lane_limits(side, width, span)
    lanes = lax.broadcasted_iota(jnp.int32, (window, BLK_X), 1) + new_col
    levels = lax.broadcasted_iota(jnp.int32, (window, BLK_X), 0)
    inner = (levels >= jnp.where(half == 0, EDGE, 0)) & (levels < jnp.where(half == 0, window, window - EDGE))
    near = inner & (lanes >= low) & (lanes < high)

    def shift_in(piece, skip):
        turn = jnp.where(half == 0, EDGE, piece.shape[0] - skip)
        return pltpu.roll(piece.astype(jnp.float32), turn, 0)[:window]

    for i in range(depth):
        mine, theirs = (group * depth + i, BLK_Y - EDGE), ((1 - group) * depth + i, EDGE)
        for (plane, skip), piece in ((mine, own[i, pl.ds(start, KEEP_ROWS), :]), (theirs, got[i])):
            piece = shift_in(piece, skip)
            for part in range(width // BLK_X):
                col = pl.multiple_of(own_col + part * BLK_X, BLK_X)
                value = piece[:, part * BLK_X : (part + 1) * BLK_X]
                image[plane, :, pl.ds(col, BLK_X)] = jnp.where(inner, value, 0.0)
        for plane, skip in (mine, theirs):
            image[plane, :, pl.ds(new_col, BLK_X)] = jnp.where(near, shift_in(near_in[plane], skip), 0.0)


def fill_band(band):
    span = band.shape[0]
    across = lax.broadcasted_iota(jnp.int32, (span, span), 0) - lax.broadcasted_iota(jnp.int32, (span, span), 1)
    band[...] = jnp.where(jnp.abs(across) <= RAD, 1.0, 0.0).astype(band.dtype)


def halves(value):
    high = value.astype(jnp.bfloat16)
    return high, (value - high.astype(jnp.float32)).astype(jnp.bfloat16)


def table_halves(table):
    high = lax.reduce_precision(table, exponent_bits=8, mantissa_bits=7)
    return high.astype(jnp.bfloat16), (table - high).astype(jnp.bfloat16)


def lane_sums(exact, products, band):
    rows = (exact + products)[0].shape[0]
    skip = len(exact) * rows
    value = jnp.concatenate(exact + products, axis=0)
    high = value.astype(jnp.bfloat16)
    low = (value - high.astype(jnp.float32))[skip:].astype(jnp.bfloat16)
    boxed = jnp.dot(high, band[...], preferred_element_type=jnp.float32)
    rest = boxed[skip:] + jnp.dot(low, band[...], preferred_element_type=jnp.float32)
    return [boxed[k * rows : (k + 1) * rows] for k in range(len(exact))] + [
        rest[k * rows : (k + 1) * rows] for k in range(len(products))
    ]


def near_planes(z, planes):
    return range(max(0, z - RAD), min(planes, z + RAD + 1))


def total(values):
    values = list(values)
    result = values[0]
    for value in values[1:]:
        result = result + value
    return result


def sum_planes(rows, boxes):
    for which in range(boxes.shape[0]):
        for z in range(boxes.shape[1]):
            boxes[which, z] = total(rows[which, k] for k in near_planes(z, boxes.shape[1]))


def fixed_kernel(own, got, near_in, image, boxes, band, rows):
    assemble(own, got, near_in, image)
    fill_band(band)
    for z in range(image.shape[0]):
        f = image[z]
        for which, value in enumerate(lane_sums([f], [f * f], band)):
            rows[which, z] = five(value, 0)
    sum_planes(rows, boxes)


def warped_kernel(own, got, near_in, image):
    assemble(own, got, near_in, image)


def cross_kernel(fixed, warped, band, boxes, rows):
    for z in range(fixed.shape[0]):
        f, w = fixed[z], warped[z]
        for which, value in enumerate(lane_sums([w], [w * w, f * w], band)):
            rows[which, z] = five(value, 0)
    sum_planes(rows, boxes)


def main_kernel(
    tiles, fixed, warped, fixed_boxes, warped_boxes, rims, far_rims, band, table_x,
    out_ref, images, edges, terms, sums, whole_rims,
):
    side, me = lax.axis_index("rep"), lax.axis_index("tile")
    half = lax.rem(me + lax.axis_index("gz"), 2)
    first = jnp.where(half == 0, (me == 0).astype(jnp.int32), 0)
    last = jnp.where(half == 1, (me == tiles - 1).astype(jnp.int32), 0)
    planes, window, span = fixed.shape
    tile = 2 * EDGE
    lanes = lax.broadcasted_iota(jnp.int32, (window, span), 1)
    levels = lax.broadcasted_iota(jnp.int32, (window, span), 0)
    low_lane, high_lane = lane_limits(side, span - BLK_X, span)
    low_row = jnp.where(first != 0, EDGE, RAD)
    high_row = jnp.where(last != 0, window - EDGE, window - RAD)
    inside = (lanes >= low_lane) & (lanes < high_lane) & (levels >= low_row) & (levels < high_row)

    outer = (first + last) != 0
    width = rims.shape[2]
    own_col = pl.multiple_of(side * BLK_X, BLK_X)
    new_col = pl.multiple_of((1 - side) * width, BLK_X)
    far_lanes = lax.broadcasted_iota(jnp.int32, far_rims.shape[1:], 1) + new_col
    far = (far_lanes >= low_lane) & (far_lanes < high_lane)
    for which in range(2):
        whole_rims[which, :, pl.ds(own_col, width)] = rims[which].astype(jnp.float32)
        whole_rims[which, :, pl.ds(new_col, BLK_X)] = jnp.where(far, far_rims[which].astype(jnp.float32), 0.0)
    rim_f = jnp.where(outer, 0.0, whole_rims[0])
    rim_w = jnp.where(outer, 0.0, whole_rims[1])
    rim_sums = lane_sums([rim_f, rim_w], [rim_f * rim_f, rim_w * rim_w, rim_f * rim_w], band)
    at = lax.broadcasted_iota(jnp.int32, (tile, span), 0)
    upper = at < EDGE
    on_top, on_end = jnp.where(half == 0, 1.0, 0.0), jnp.where(half == 0, 0.0, 1.0)
    held = (at >= jnp.where(half == 0, 0, EDGE)) & (at < jnp.where(half == 0, EDGE, tile))
    reach = (at >= jnp.where(half == 0, 0, RAD)) & (at < jnp.where(half == 0, tile - RAD, tile))

    def rim_tile(rim, z):
        pair = rim[z // 2 * tile : (z // 2 + 1) * tile]
        other = pltpu.roll(pair, EDGE, 0)
        both = jnp.where(upper, pair, other) if z % 2 == 0 else jnp.where(upper, other, pair)
        return jnp.where(held, both, 0.0)

    def with_tile(value, extra):
        return jnp.concatenate(
            [value[:tile] + extra * on_top, value[tile : window - tile], value[window - tile :] + extra * on_end],
            axis=0,
        )

    for which in range(5):
        for z in range(planes):
            edges[which, z] = jnp.where(reach, five(rim_tile(rim_sums[which], z), 0), 0.0)
    for z in range(planes):
        images[z] = with_tile(warped[z], rim_tile(rim_w, z))

    volume = float((2 * RAD + 1) ** 3)
    sources = (fixed_boxes, 0), (warped_boxes, 0), (fixed_boxes, 1), (warped_boxes, 1), (warped_boxes, 2)
    for z in range(planes):
        sum_f, sum_w, sum_ff, sum_ww, sum_fw = (
            with_tile(source[index, z], total(edges[which, k] for k in near_planes(z, planes)))
            for which, (source, index) in enumerate(sources)
        )
        cross = sum_fw - sum_f * sum_w * (1.0 / volume)
        var_f = sum_ff - sum_f * sum_f * (1.0 / volume)
        var_w = sum_ww - sum_w * sum_w * (1.0 / volume)
        inverse = 1.0 / (var_f * var_w + den_floor)
        ratio = cross * inverse
        term_a = 2.0 * ratio
        term_b = -(ratio * ratio) * var_f
        term_c = -(term_a * sum_f + 2.0 * term_b * sum_w) * (1.0 / volume)
        values = [five(jnp.where(inside, value, 0.0), 0) for value in (term_a, term_b, term_c)]
        for which, value in enumerate(lane_sums([], values, band)):
            terms[which, z] = value

    for d in range(3):
        sums[d] = jnp.zeros((window, span), jnp.float32)
    owned = (levels >= EDGE) & (levels < window - EDGE)
    for z in range(planes):
        box_a, box_b, box_c = (total(terms[which, k] for k in near_planes(z, planes)) for which in range(3))
        f, w = fixed[z], images[z]
        gain = -(f * box_a + 2.0 * w * box_b + box_c)
        u = z / SPACING
        weight = (3.0 * u * u * u - 6.0 * u * u + 4.0) * (0.5 / 6.0)
        gain = jnp.where(owned, gain, 0.0) * weight
        ahead = images[z + 1] if z + 1 < planes else 0.0
        behind = images[z - 1] if z > 0 else 0.0
        sums[0] += gain * (ahead - behind)
        sums[1] += gain * (pltpu.roll(w, window - 1, 0) - pltpu.roll(w, 1, 0))
        sums[2] += gain * (pltpu.roll(w, span - 1, 1) - pltpu.roll(w, 1, 1))

    knots = window // SPACING
    at_row = lax.broadcasted_iota(jnp.int32, (window, BLK_X), 0) - EDGE
    knot = lax.shift_right_arithmetic(at_row, 4)
    u = (at_row - knot * SPACING).astype(jnp.float32) * (1.0 / SPACING)
    square = u * u
    cube = square * u
    weights = (
        (1.0 - u) * (1.0 - u) * (1.0 - u) * (1.0 / 6.0),
        (3.0 * cube - 6.0 * square + 4.0) * (1.0 / 6.0),
        (-3.0 * cube + 3.0 * square + 3.0 * u + 1.0) * (1.0 / 6.0),
        cube * (1.0 / 6.0),
    )
    at_knot = lax.broadcasted_iota(jnp.int32, (tile, span), 0)
    stack = []
    columns = []
    for target in range(knots + 3):
        column = jnp.zeros((window, BLK_X), jnp.float32)
        for offset in range(4):
            column = jnp.where(knot == target - offset, weights[offset], column)
        column = jnp.where((at_row >= 0) & (at_row < window - tile), column, 0.0)
        columns.append(jnp.concatenate([column] * (span // BLK_X), axis=1))
    for d in range(3):
        found = jnp.zeros((tile, span), jnp.float32)
        for target, column in enumerate(columns):
            line = jnp.sum(sums[d] * column, axis=0, keepdims=True)
            found = jnp.where(at_knot == target, line, found)
        stack.append(jnp.where(half == 0, pltpu.roll(found, 1, 0), pltpu.roll(found, 1 + knots, 0)))
    boxed = jnp.dot(
        jnp.concatenate(halves(jnp.concatenate(stack, axis=0)), axis=0), table_x[...],
        preferred_element_type=jnp.float32,
    )
    rows, count = out_ref.shape
    along_x = boxed[:rows] + pltpu.roll(boxed[:rows], boxed.shape[1] - count, 1) + boxed[rows:]
    out_ref[...] = along_x[:, :count]


def local_kernel(kernel, outs, arrays, scratch=()):
    vmem = pl.BlockSpec(memory_space=pltpu.VMEM)
    return pl.pallas_call(
        kernel,
        out_shape=[pltpu.VMEM(shape, dtype) for shape, dtype in outs],
        in_specs=[vmem] * len(arrays),
        out_specs=[vmem] * len(outs),
        scratch_shapes=list(scratch),
        compiler_params=pltpu.CompilerParams(vmem_limit_bytes=KERNEL_BYTES),
    )(*(pltpu.with_memory_space_constraint(array, pltpu.VMEM) for array in arrays))


def fast_body(tiles, fixed_image, moving_image, source_tile, block_shifts):
    depth, height, width = fixed_image.shape
    me, group, side = lax.axis_index("tile"), lax.axis_index("gz"), lax.axis_index("rep")
    half = lax.rem(me + group, 2)
    sources = source_tile[:, 0, :, 0]
    shifts = block_shifts[0, 0]
    cap = MAX_NAMED if tiles == 4 else sources.shape[1]
    planes = 2 * depth
    window, span = height // 2 + 2 * EDGE, width + BLK_X
    short, full = jnp.bfloat16, jnp.float32
    whole, send_shape = (fixed_image.shape, short), ((depth, SEND_ROWS, width), short)
    side_shape = ((planes, KEEP_ROWS, BLK_X), short)
    image_shape = ((planes, window, span), full)
    smem, vmem = (pl.BlockSpec(memory_space=space) for space in (pltpu.SMEM, pltpu.VMEM))
    outs = [((cap, depth, BLK_Y, BLK_X), short)] * (tiles - 1) + [(sources.shape, jnp.int32), whole, whole, send_shape]
    *packs, sources, moving_image, fixed_image, fixed_send = pl.pallas_call(
        functools.partial(pack_kernel, tiles),
        out_shape=[pltpu.VMEM(*out) for out in outs],
        in_specs=[smem, vmem, vmem, vmem],
        out_specs=[vmem] * len(outs),
    )(sources, sources, moving_image, fixed_image)

    trio = ("tile", "gz", "rep")

    def number(t, g, r):
        return (t * 2 + g) * 2 + r

    swap = [(0, 1), (1, 0)]
    straight, slant, crossed = [], [], []
    for r in range(2):
        for t in range(tiles):
            for g in range(2):
                to = t - 1 if (g + t) % 2 == 0 else t + 1
                there = 0 <= to < tiles
                straight.append((number(t, g, r), number(to, g, r) if there else number(t, g, 1 - r)))
                crossed.append((number(t, g, r), number(to if there else t, g, 1 - r)))
                slant.append((number(t, g, r), number(to if there else t, 1 - g, r)))

    got = [
        lax.ppermute(pack, "tile", [(t, t ^ step) for t in range(tiles)])
        for step, pack in zip(far_first(tiles), packs)
    ]
    fixed_got = lax.ppermute(fixed_send, "gz", swap)
    own, send = local_kernel(
        functools.partial(unpack_kernel, tiles), [whole, send_shape], [sources, shifts, moving_image, *got]
    )
    warp_got = lax.ppermute(send, "gz", swap)
    (fixed_side,) = local_kernel(side_kernel, [side_shape], [fixed_image, fixed_got])
    fixed_near = lax.ppermute(fixed_side, "rep", swap)
    boxes = [(count, planes, window, span) for count in (2, 3)]
    fixed, fixed_boxes, band = local_kernel(
        fixed_kernel,
        [image_shape, (boxes[0], full), ((span, span), short)],
        [fixed_image, fixed_got, fixed_near],
        [pltpu.VMEM(boxes[0], full)],
    )
    rim_shape = (2, planes * EDGE, width)
    warp_side, rims, far_rims = local_kernel(
        edge_kernel,
        [side_shape, (rim_shape, short), ((2, planes * EDGE, BLK_X), short)],
        [own, warp_got, fixed],
        [pltpu.VMEM(rim_shape, full)],
    )
    warp_near = lax.ppermute(warp_side, "rep", swap)
    rims = lax.ppermute(rims, trio, straight)
    far_rims = lax.ppermute(far_rims, trio, crossed)
    (warped,) = local_kernel(warped_kernel, [image_shape], [own, warp_got, warp_near])
    (warped_boxes,) = local_kernel(
        cross_kernel, [(boxes[1], full)], [fixed, warped, band], [pltpu.VMEM(boxes[1], full)]
    )

    row_knots, col_knots = height // SPACING, width // SPACING
    high, low = table_halves(spline_table(side * BLK_X, span, side * col_knots, col_knots))
    table_x = jnp.pad(jnp.concatenate([high, low], axis=1), ((0, 0), (0, -2 * col_knots % 128)))
    (part,) = local_kernel(
        functools.partial(main_kernel, tiles),
        [((3 * (row_knots + 4), col_knots), full)],
        [fixed, warped, fixed_boxes, warped_boxes, rims, far_rims, band, table_x],
        [
            pltpu.VMEM((planes, window, span), full),
            pltpu.VMEM((5, planes, 2 * EDGE, span), full),
            pltpu.VMEM((3, planes, window, span), full),
            pltpu.VMEM((3, window, span), full),
            pltpu.VMEM((2, planes * EDGE, span), full),
        ],
    )
    part = part.reshape(3, row_knots + 4, col_knots)
    across = lax.ppermute(part, "gz", swap)
    part_slant = lax.ppermute(part, trio, slant)
    part_straight = lax.ppermute(part, trio, straight)
    below = jnp.where(half == 0, part_slant, part_straight)
    above = jnp.where(half == 0, part_straight, part_slant)
    below = jnp.where(me == tiles - 1, 0.0, below[:, :2])
    above = jnp.where(me == 0, 0.0, above[:, row_knots + 2 :])
    middle = part[:, 2 : row_knots + 2] + across[:, 2 : row_knots + 2]
    return (middle + jnp.concatenate([above, below], axis=1))[:, None]


def solution(mesh):
    sizes = mesh.shape
    tiles = sizes["tile"]
    fast = sizes["gz"] == 2 and sizes["rep"] == 2 and tiles & (tiles - 1) == 0 and tiles > 1
    return jax.shard_map(
        functools.partial(fast_body, tiles) if fast else body,
        mesh=mesh,
        in_specs=(
            P(("slab", "gz"), "tile", "rep"),
            P(("slab", "gz"), "tile", "rep"),
            P("slab", "rep", None, None),
            P(("slab", "tile"), "rep", None, None),
        ),
        out_specs=P(None, "slab", "tile", "rep"),
        check_vma=False,
    )
```

```python
import functools

import jax
import jax.numpy as jnp
from jax import lax
from jax.experimental import pallas as pl
from jax.experimental.pallas import tpu as pltpu
from jax.sharding import PartitionSpec as P

BLK_Y = 16
BLK_X = 128
RAD = 2
SPACING = 16
MAX_NAMED = 4


den_floor = 1e-05

def with_halo(array, sides, width):
    for axis, dim in sides:
        count, length = (lax.axis_size(axis), array.shape[dim])
        up = [(i, (i + 1) % count) for i in range(count - 1)]
        down = [(j, i) for i, j in up]
        last = lax.slice_in_dim(array, length - width, length, axis=dim)
        first = lax.slice_in_dim(array, 0, width, axis=dim)
        before = lax.ppermute(last, axis, up)
        after = lax.ppermute(first, axis, down)
        array = jnp.concatenate([before, array, after], axis=dim)
    return array


def window_sum(extended, radius):
    result = extended
    for axis_id in range(3):
        length = result.shape[axis_id] - 2 * radius
        summed = lax.slice_in_dim(result, 0, length, axis=axis_id)
        for offset in range(1, 2 * radius + 1):
            summed = summed + lax.slice_in_dim(result, offset, offset + length, axis=axis_id)
        result = summed
    return result


def window_terms(ext_fixed, ext_warp, radius):
    volume = float((2 * radius + 1) ** 3)
    sum_fixed = window_sum(ext_fixed, radius)
    sum_warp = window_sum(ext_warp, radius)
    sum_fixed_sq = window_sum(ext_fixed * ext_fixed, radius)
    sum_warp_sq = window_sum(ext_warp * ext_warp, radius)
    sum_product = window_sum(ext_fixed * ext_warp, radius)
    cross_term = sum_product - sum_fixed * sum_warp / volume
    fixed_var = sum_fixed_sq - sum_fixed * sum_fixed / volume
    warp_var = sum_warp_sq - sum_warp * sum_warp / volume
    denominator = fixed_var * warp_var + den_floor
    term_a = 2.0 * cross_term / denominator
    term_b = -cross_term * cross_term * fixed_var / (denominator * denominator)
    term_c = -(term_a * sum_fixed + 2.0 * term_b * sum_warp) / volume
    return (term_a, term_b, term_c)


def slopes(extended, margin, extent):
    result = []
    for axis_id in range(3):
        ahead = [margin, margin, margin]
        behind = [margin, margin, margin]
        ahead[axis_id] += 1
        behind[axis_id] -= 1
        upper = lax.slice(
            extended,
            tuple(ahead),
            (ahead[0] + extent[0], ahead[1] + extent[1], ahead[2] + extent[2]),
        )
        lower = lax.slice(
            extended,
            tuple(behind),
            (behind[0] + extent[0], behind[1] + extent[1], behind[2] + extent[2]),
        )
        result.append(0.5 * (upper - lower))
    return result


def spline_table(first_pos, length, first_col, columns):
    places = first_pos + jnp.arange(length, dtype=jnp.int32)
    knots = places // SPACING
    within = (places - knots * SPACING).astype(jnp.float32) / SPACING
    squares = within * within
    cubes = squares * within
    weights = (
        (1.0 - within) ** 3 / 6.0,
        (3.0 * cubes - 6.0 * squares + 4.0) / 6.0,
        (-3.0 * cubes + 3.0 * squares + 3.0 * within + 1.0) / 6.0,
        cubes / 6.0,
    )
    targets = first_col + jnp.arange(columns, dtype=jnp.int32)
    table = jnp.zeros((length, columns), jnp.float32)
    for offset in range(4):
        table = table + jnp.where(
            targets[None, :] == (knots + offset - 1)[:, None], weights[offset][:, None], 0.0
        )
    return table


def contract(pieces, table_z, table_y, table_x):
    highest = lax.Precision.HIGHEST
    along_x = jnp.einsum("czyx,xk->czyk", pieces, table_x, precision=highest)
    along_y = jnp.einsum("czyk,yj->czjk", along_x, table_y, precision=highest)
    return jnp.einsum("czjk,zl->cljk", along_y, table_z, precision=highest)


def roll_block(block, amounts):
    return jnp.roll(jnp.roll(block, amounts[0], axis=1), amounts[1], axis=2)


def fold_rims(extended, axis_id, owned):
    middle = lax.slice_in_dim(extended, 4, owned + 4, axis=axis_id)
    leading = lax.slice_in_dim(extended, 0, 2, axis=axis_id)
    trailing = lax.slice_in_dim(extended, owned + 6, owned + 8, axis=axis_id)
    lead_pad = [(0, 0), (0, 0), (0, 0), (0, 0)]
    trail_pad = [(0, 0), (0, 0), (0, 0), (0, 0)]
    lead_pad[axis_id] = (0, owned - 2)
    trail_pad[axis_id] = (owned - 2, 0)
    return middle + jnp.pad(leading, lead_pad) + jnp.pad(trailing, trail_pad)


def body(fixed_image, moving_image, source_tile, block_shifts):
    depth, height, width = fixed_image.shape
    yblocks = height // BLK_Y
    xblocks = width // BLK_X
    block_count = yblocks * xblocks
    tile_lists = source_tile[:, 0, :, 0]
    my_tile = lax.axis_index("tile")
    own_list = lax.dynamic_index_in_dim(tile_lists, my_tile, 0, keepdims=False)
    row_steps = jnp.arange(BLK_Y, dtype=jnp.int32)
    initial = jnp.zeros((block_count, depth, BLK_Y, BLK_X), jnp.bfloat16)
    piece = lax.all_gather(moving_image, "tile", axis=1, tiled=True)
    length = piece.shape[1]
    held_blocks = []
    for block_id in range(block_count):
        row_block = block_id // xblocks
        col_block = block_id % xblocks
        wanted = own_list[block_id] * height + row_block * BLK_Y + row_steps
        usable = (wanted >= 0) & (wanted < length)
        columns_part = lax.slice_in_dim(piece, col_block * BLK_X, (col_block + 1) * BLK_X, axis=2)
        taken = jnp.take(columns_part, jnp.clip(wanted, 0, length - 1), axis=1)
        held_blocks.append(jnp.where(usable[None, :, None], taken, initial[block_id]))
    blocks = jnp.stack(held_blocks)
    rolled = jax.vmap(roll_block)(blocks, block_shifts[0, 0])
    warped = (
        rolled.reshape(yblocks, xblocks, depth, BLK_Y, BLK_X)
        .transpose(2, 0, 3, 1, 4)
        .reshape(depth, height, width)
    )
    image_pair = jnp.stack((fixed_image, warped))
    fixed_own = fixed_image.astype(jnp.float32)
    warp_own = warped.astype(jnp.float32)
    extended = with_halo(image_pair, (("tile", 2), ("gz", 1), ("rep", 3)), RAD).astype(jnp.float32)
    term_a, term_b, term_c = window_terms(extended[0], extended[1], RAD)
    terms_ext = with_halo(
        jnp.stack((term_a, term_b, term_c)).astype(jnp.bfloat16),
        (("tile", 2), ("gz", 1), ("rep", 3)),
        RAD,
    ).astype(jnp.float32)
    box_a = window_sum(terms_ext[0], RAD)
    box_b = window_sum(terms_ext[1], RAD)
    box_c = window_sum(terms_ext[2], RAD)
    margin = RAD
    gain = -(fixed_own * box_a + 2.0 * warp_own * box_b + box_c)
    slope_z, slope_y, slope_x = slopes(extended[1], margin, (depth, height, width))
    pieces = jnp.stack((gain * slope_z, gain * slope_y, gain * slope_x))
    depth_total = depth * lax.axis_size("gz")
    depth_knots = (depth_total + SPACING - 1) // SPACING
    table_z = spline_table(lax.axis_index("gz") * depth, depth, 0, depth_knots)
    row_knots = height // SPACING
    table_y = spline_table(my_tile * height, height, my_tile * row_knots - 2, row_knots + 4)
    col_knots = width // SPACING
    rep_index = lax.axis_index("rep")
    table_x = spline_table(rep_index * width, width, rep_index * col_knots - 2, col_knots + 4)
    local_grad = contract(pieces, table_z, table_y, table_x)
    spread = with_halo(local_grad, (("tile", 2), ("rep", 3)), 2)
    owned_grad = fold_rims(fold_rims(spread, 2, row_knots), 3, col_knots)
    return lax.psum(owned_grad, "gz")


EDGE = 2 * RAD
KEEP_ROWS, SEND_ROWS = 48, 40
KERNEL_BYTES = 24 << 20


def far_first(tiles):
    return sorted(range(1, tiles), key=lambda step: (step < 2, step))


def send_window(half, image, out):
    rows = out.shape[1]
    value = image[...].astype(jnp.float32)
    value = jnp.where(half == 1, value[:, :rows], value[:, value.shape[1] - rows :])
    out[...] = value.astype(out.dtype)


def pack_kernel(tiles, source_ref, source_in, moving_ref, fixed_ref, *out_refs):
    *packs, source_out, moving_out, fixed_out, send_out = out_refs
    source_out[...] = source_in[...]
    moving_out[...] = moving_ref[...]
    fixed_out[...] = fixed_ref[...]
    me = lax.axis_index("tile")
    half = lax.rem(me + lax.axis_index("gz"), 2)
    send_window(half, fixed_ref, send_out)
    height, width = moving_ref.shape[1:]
    xblocks = width // BLK_X
    blocks = (height // BLK_Y) * xblocks
    cap = packs[0].shape[0]
    for step, pack in zip(far_first(tiles), packs):
        other = lax.bitwise_xor(me, step)
        count = jnp.int32(0)
        chosen = [jnp.int32(0)] * cap
        for block in range(blocks):
            named = source_ref[other, block] == me
            chosen = [jnp.where(named & (count == slot), block, old) for slot, old in enumerate(chosen)]
            count = count + named.astype(jnp.int32)
        for slot, block in enumerate(chosen):
            row = pl.multiple_of(block // xblocks * BLK_Y, BLK_Y)
            col = pl.multiple_of(lax.rem(block, xblocks) * BLK_X, BLK_X)
            pack[slot] = moving_ref[:, pl.ds(row, BLK_Y), pl.ds(col, BLK_X)]


def unpack_kernel(tiles, source_ref, shift_ref, moving_ref, *refs):
    recvs = dict(zip(far_first(tiles), refs))
    own_ref, send_ref = refs[tiles - 1 :]
    me = lax.axis_index("tile")
    half = lax.rem(me + lax.axis_index("gz"), 2)
    height, width = moving_ref.shape[1:]
    xblocks = width // BLK_X
    blocks = (height // BLK_Y) * xblocks
    cap = refs[0].shape[0]
    for block in range(blocks):
        row, col = (block // xblocks) * BLK_Y, (block % xblocks) * BLK_X
        source = source_ref[me, block]
        slot = jnp.int32(0)
        for earlier in range(block):
            slot = slot + (source_ref[me, earlier] == source).astype(jnp.int32)
        slot = jnp.minimum(slot, cap - 1)
        step = lax.bitwise_xor(source, me)
        value = moving_ref[:, row : row + BLK_Y, col : col + BLK_X].astype(jnp.float32)
        for other in range(1, tiles):
            value = jnp.where(step == other, recvs[other][slot].astype(jnp.float32), value)
        down = lax.rem(shift_ref[block, 0], BLK_Y)
        right = lax.rem(shift_ref[block, 1], BLK_X)
        value = pltpu.roll(value, right, 2)
        for bit in (1, 2, 4, 8):
            value = jnp.where(lax.bitwise_and(down, bit) != 0, pltpu.roll(value, bit, 1), value)
        own_ref[:, row : row + BLK_Y, col : col + BLK_X] = value.astype(own_ref.dtype)
    send_window(half, own_ref, send_ref)


def side_kernel(own_ref, got_ref, *refs):
    out_ref = refs[-1]
    group = lax.axis_index("gz")
    half = lax.rem(lax.axis_index("tile") + group, 2)
    depth = own_ref.shape[0]
    col = pl.multiple_of((1 - lax.axis_index("rep")) * BLK_X, BLK_X)
    start = pl.multiple_of(half * BLK_Y, BLK_Y)
    for i in range(depth):
        out_ref[group * depth + i] = own_ref[i, pl.ds(start, KEEP_ROWS), pl.ds(col, BLK_X)]
        theirs = got_ref[i, :, pl.ds(col, BLK_X)].astype(jnp.float32)
        theirs = jnp.concatenate([theirs, jnp.zeros((KEEP_ROWS - SEND_ROWS, BLK_X), jnp.float32)], axis=0)
        out_ref[(1 - group) * depth + i] = theirs.astype(out_ref.dtype)


def edge_kernel(own_ref, got_ref, fixed_ref, side_ref, rim_ref, far_ref, rims):
    side_kernel(own_ref, got_ref, side_ref)
    group, side = lax.axis_index("gz"), lax.axis_index("rep")
    half = lax.rem(lax.axis_index("tile") + group, 2)
    depth, height, width = own_ref.shape
    tile = 2 * EDGE
    upper = lax.broadcasted_iota(jnp.int32, (tile, width), 0) < EDGE
    own_start = pl.multiple_of(half * (height - BLK_Y), BLK_Y)
    own_col = pl.multiple_of(side * BLK_X, BLK_X)

    def pair(low, high):
        top = jnp.where(upper, low[:tile], pltpu.roll(high[:tile], EDGE, 0))
        end = jnp.where(upper, pltpu.roll(low[-tile:], EDGE, 0), high[-tile:])
        return jnp.where(half == 0, top, end)

    for i in range(0, depth, 2):
        mine = pl.multiple_of((group * depth + i) * EDGE, tile)
        theirs = pl.multiple_of(((1 - group) * depth + i) * EDGE, tile)
        rims[1, pl.ds(mine, tile), :] = pair(
            *(own_ref[i + k, pl.ds(own_start, BLK_Y), :].astype(jnp.float32) for k in range(2))
        )
        rims[1, pl.ds(theirs, tile), :] = pair(*(got_ref[i + k].astype(jnp.float32) for k in range(2)))
    for z in range(0, 2 * depth, 2):
        low, high = (fixed_ref[z + k, :, pl.ds(own_col, width)] for k in range(2))
        top = jnp.where(upper, pltpu.roll(low[:tile], EDGE, 0), high[:tile])
        end = jnp.where(upper, low[-tile:], pltpu.roll(high[-tile:], EDGE, 0))
        rims[0, z * EDGE : z * EDGE + tile, :] = jnp.where(half == 0, top, end)
    rim_ref[...] = rims[...].astype(rim_ref.dtype)
    far_col = pl.multiple_of((1 - side) * BLK_X, BLK_X)
    far_ref[...] = rims[:, :, pl.ds(far_col, BLK_X)].astype(far_ref.dtype)


def five(array, axis):
    size = array.shape[axis]
    pair = array + pltpu.roll(array, 1, axis)
    return pltpu.roll(pair, size - 2, axis) + pair + pltpu.roll(array, 2, axis)


def lane_limits(side, width, span):
    return jnp.where(side == 0, 0, BLK_X - 48), jnp.where(side == 0, width + 32, span)


def assemble(own, got, near_in, image):
    group, side = lax.axis_index("gz"), lax.axis_index("rep")
    half = lax.rem(lax.axis_index("tile") + group, 2)
    depth, _, width = own.shape
    window, span = image.shape[1:]
    own_col = pl.multiple_of(side * BLK_X, BLK_X)
    new_col = pl.multiple_of((1 - side) * width, BLK_X)
    start = pl.multiple_of(half * BLK_Y, BLK_Y)
    low, high = lane_limits(side, width, span)
    lanes = lax.broadcasted_iota(jnp.int32, (window, BLK_X), 1) + new_col
    levels = lax.broadcasted_iota(jnp.int32, (window, BLK_X), 0)
    inner = (levels >= jnp.where(half == 0, EDGE, 0)) & (levels < jnp.where(half == 0, window, window - EDGE))
    near = inner & (lanes >= low) & (lanes < high)

    def shift_in(piece, skip):
        turn = jnp.where(half == 0, EDGE, piece.shape[0] - skip)
        return pltpu.roll(piece.astype(jnp.float32), turn, 0)[:window]

    for i in range(depth):
        mine, theirs = (group * depth + i, BLK_Y - EDGE), ((1 - group) * depth + i, EDGE)
        for (plane, skip), piece in ((mine, own[i, pl.ds(start, KEEP_ROWS), :]), (theirs, got[i])):
            piece = shift_in(piece, skip)
            for part in range(width // BLK_X):
                col = pl.multiple_of(own_col + part * BLK_X, BLK_X)
                value = piece[:, part * BLK_X : (part + 1) * BLK_X]
                image[plane, :, pl.ds(col, BLK_X)] = jnp.where(inner, value, 0.0)
        for plane, skip in (mine, theirs):
            image[plane, :, pl.ds(new_col, BLK_X)] = jnp.where(near, shift_in(near_in[plane], skip), 0.0)


def fill_band(band):
    span = band.shape[0]
    across = lax.broadcasted_iota(jnp.int32, (span, span), 0) - lax.broadcasted_iota(jnp.int32, (span, span), 1)
    band[...] = jnp.where(jnp.abs(across) <= RAD, 1.0, 0.0).astype(band.dtype)


def halves(value):
    high = value.astype(jnp.bfloat16)
    return high, (value - high.astype(jnp.float32)).astype(jnp.bfloat16)


def table_halves(table):
    high = lax.reduce_precision(table, exponent_bits=8, mantissa_bits=7)
    return high.astype(jnp.bfloat16), (table - high).astype(jnp.bfloat16)


def lane_sums(exact, products, band):
    rows = (exact + products)[0].shape[0]
    low = [value - value.astype(jnp.bfloat16).astype(jnp.float32) for value in products]
    boxed = jnp.dot(
        jnp.concatenate(exact + products + low, axis=0).astype(jnp.bfloat16), band[...],
        preferred_element_type=jnp.float32,
    )
    pieces = [boxed[k * rows : (k + 1) * rows] for k in range(len(exact) + 2 * len(products))]
    first = len(exact)
    return pieces[:first] + [
        pieces[first + k] + pieces[first + len(products) + k] for k in range(len(products))
    ]


def near_planes(z, planes):
    return range(max(0, z - RAD), min(planes, z + RAD + 1))


def total(values):
    values = list(values)
    result = values[0]
    for value in values[1:]:
        result = result + value
    return result


def sum_planes(rows, boxes):
    for which in range(boxes.shape[0]):
        for z in range(boxes.shape[1]):
            boxes[which, z] = total(rows[which, k] for k in near_planes(z, boxes.shape[1]))


def fixed_kernel(own, got, near_in, image, boxes, band, rows):
    assemble(own, got, near_in, image)
    fill_band(band)
    for z in range(image.shape[0]):
        f = image[z]
        for which, value in enumerate(lane_sums([f], [f * f], band)):
            rows[which, z] = five(value, 0)
    sum_planes(rows, boxes)


def warped_kernel(own, got, near_in, image):
    assemble(own, got, near_in, image)


def cross_kernel(fixed, warped, band, boxes, rows):
    for z in range(fixed.shape[0]):
        f, w = fixed[z], warped[z]
        for which, value in enumerate(lane_sums([w], [w * w, f * w], band)):
            rows[which, z] = five(value, 0)
    sum_planes(rows, boxes)


def main_kernel(
    tiles, fixed, warped, fixed_boxes, warped_boxes, rims, far_rims, band, table_x,
    out_ref, images, edges, terms, sums, whole_rims,
):
    side, me = lax.axis_index("rep"), lax.axis_index("tile")
    half = lax.rem(me + lax.axis_index("gz"), 2)
    first = jnp.where(half == 0, (me == 0).astype(jnp.int32), 0)
    last = jnp.where(half == 1, (me == tiles - 1).astype(jnp.int32), 0)
    planes, window, span = fixed.shape
    tile = 2 * EDGE
    lanes = lax.broadcasted_iota(jnp.int32, (window, span), 1)
    levels = lax.broadcasted_iota(jnp.int32, (window, span), 0)
    low_lane, high_lane = lane_limits(side, span - BLK_X, span)
    low_row = jnp.where(first != 0, EDGE, RAD)
    high_row = jnp.where(last != 0, window - EDGE, window - RAD)
    inside = (lanes >= low_lane) & (lanes < high_lane) & (levels >= low_row) & (levels < high_row)

    outer = (first + last) != 0
    width = rims.shape[2]
    own_col = pl.multiple_of(side * BLK_X, BLK_X)
    new_col = pl.multiple_of((1 - side) * width, BLK_X)
    far_lanes = lax.broadcasted_iota(jnp.int32, far_rims.shape[1:], 1) + new_col
    far = (far_lanes >= low_lane) & (far_lanes < high_lane)
    for which in range(2):
        whole_rims[which, :, pl.ds(own_col, width)] = rims[which].astype(jnp.float32)
        whole_rims[which, :, pl.ds(new_col, BLK_X)] = jnp.where(far, far_rims[which].astype(jnp.float32), 0.0)
    rim_f = jnp.where(outer, 0.0, whole_rims[0])
    rim_w = jnp.where(outer, 0.0, whole_rims[1])
    rim_sums = lane_sums([rim_f, rim_w], [rim_f * rim_f, rim_w * rim_w, rim_f * rim_w], band)
    at = lax.broadcasted_iota(jnp.int32, (tile, span), 0)
    upper = at < EDGE
    on_top, on_end = jnp.where(half == 0, 1.0, 0.0), jnp.where(half == 0, 0.0, 1.0)
    held = (at >= jnp.where(half == 0, 0, EDGE)) & (at < jnp.where(half == 0, EDGE, tile))
    reach = (at >= jnp.where(half == 0, 0, RAD)) & (at < jnp.where(half == 0, tile - RAD, tile))

    def rim_tile(rim, z):
        pair = rim[z // 2 * tile : (z // 2 + 1) * tile]
        other = pltpu.roll(pair, EDGE, 0)
        both = jnp.where(upper, pair, other) if z % 2 == 0 else jnp.where(upper, other, pair)
        return jnp.where(held, both, 0.0)

    def with_tile(value, extra):
        return jnp.concatenate(
            [value[:tile] + extra * on_top, value[tile : window - tile], value[window - tile :] + extra * on_end],
            axis=0,
        )

    for which in range(5):
        for z in range(planes):
            edges[which, z] = jnp.where(reach, five(rim_tile(rim_sums[which], z), 0), 0.0)
    for z in range(planes):
        images[z] = with_tile(warped[z], rim_tile(rim_w, z))

    volume = float((2 * RAD + 1) ** 3)
    sources = (fixed_boxes, 0), (warped_boxes, 0), (fixed_boxes, 1), (warped_boxes, 1), (warped_boxes, 2)
    for z in range(planes):
        sum_f, sum_w, sum_ff, sum_ww, sum_fw = (
            with_tile(source[index, z], total(edges[which, k] for k in near_planes(z, planes)))
            for which, (source, index) in enumerate(sources)
        )
        cross = sum_fw - sum_f * sum_w * (1.0 / volume)
        var_f = sum_ff - sum_f * sum_f * (1.0 / volume)
        var_w = sum_ww - sum_w * sum_w * (1.0 / volume)
        inverse = 1.0 / (var_f * var_w + den_floor)
        ratio = cross * inverse
        term_a = 2.0 * ratio
        term_b = -(ratio * ratio) * var_f
        term_c = -(term_a * sum_f + 2.0 * term_b * sum_w) * (1.0 / volume)
        values = [five(jnp.where(inside, value, 0.0), 0) for value in (term_a, term_b, term_c)]
        high, low = halves(jnp.concatenate(values, axis=0))
        boxed = jnp.dot(high, band[...], preferred_element_type=jnp.float32) + jnp.dot(
            low, band[...], preferred_element_type=jnp.float32
        )
        for which in range(3):
            terms[which, z] = boxed[which * window : (which + 1) * window]

    for d in range(3):
        sums[d] = jnp.zeros((window, span), jnp.float32)
    owned = (levels >= EDGE) & (levels < window - EDGE)
    for z in range(planes):
        box_a, box_b, box_c = (total(terms[which, k] for k in near_planes(z, planes)) for which in range(3))
        f, w = fixed[z], images[z]
        gain = -(f * box_a + 2.0 * w * box_b + box_c)
        u = z / SPACING
        weight = (3.0 * u * u * u - 6.0 * u * u + 4.0) * (0.5 / 6.0)
        gain = jnp.where(owned, gain, 0.0) * weight
        ahead = images[z + 1] if z + 1 < planes else 0.0
        behind = images[z - 1] if z > 0 else 0.0
        sums[0] += gain * (ahead - behind)
        sums[1] += gain * (pltpu.roll(w, window - 1, 0) - pltpu.roll(w, 1, 0))
        sums[2] += gain * (pltpu.roll(w, span - 1, 1) - pltpu.roll(w, 1, 1))

    knots = window // SPACING
    at_row = lax.broadcasted_iota(jnp.int32, (window, BLK_X), 0) - EDGE
    knot = lax.shift_right_arithmetic(at_row, 4)
    u = (at_row - knot * SPACING).astype(jnp.float32) * (1.0 / SPACING)
    square = u * u
    cube = square * u
    weights = (
        (1.0 - u) * (1.0 - u) * (1.0 - u) * (1.0 / 6.0),
        (3.0 * cube - 6.0 * square + 4.0) * (1.0 / 6.0),
        (-3.0 * cube + 3.0 * square + 3.0 * u + 1.0) * (1.0 / 6.0),
        cube * (1.0 / 6.0),
    )
    at_knot = lax.broadcasted_iota(jnp.int32, (tile, span), 0)
    stack = []
    columns = []
    for target in range(knots + 3):
        column = jnp.zeros((window, BLK_X), jnp.float32)
        for offset in range(4):
            column = jnp.where(knot == target - offset, weights[offset], column)
        column = jnp.where((at_row >= 0) & (at_row < window - tile), column, 0.0)
        columns.append(jnp.concatenate([column] * (span // BLK_X), axis=1))
    for d in range(3):
        found = jnp.zeros((tile, span), jnp.float32)
        for target, column in enumerate(columns):
            line = jnp.sum(sums[d] * column, axis=0, keepdims=True)
            found = jnp.where(at_knot == target, line, found)
        stack.append(jnp.where(half == 0, pltpu.roll(found, 1, 0), pltpu.roll(found, 1 + knots, 0)))
    boxed = jnp.dot(
        jnp.concatenate(halves(jnp.concatenate(stack, axis=0)), axis=0), table_x[...],
        preferred_element_type=jnp.float32,
    )
    rows, count = out_ref.shape
    along_x = boxed[:rows] + pltpu.roll(boxed[:rows], boxed.shape[1] - count, 1) + boxed[rows:]
    out_ref[...] = along_x[:, :count]


def local_kernel(kernel, outs, arrays, scratch=()):
    vmem = pl.BlockSpec(memory_space=pltpu.VMEM)
    return pl.pallas_call(
        kernel,
        out_shape=[pltpu.VMEM(shape, dtype) for shape, dtype in outs],
        in_specs=[vmem] * len(arrays),
        out_specs=[vmem] * len(outs),
        scratch_shapes=list(scratch),
        compiler_params=pltpu.CompilerParams(vmem_limit_bytes=KERNEL_BYTES),
    )(*(pltpu.with_memory_space_constraint(array, pltpu.VMEM) for array in arrays))


def fast_body(tiles, fixed_image, moving_image, source_tile, block_shifts):
    depth, height, width = fixed_image.shape
    me, group, side = lax.axis_index("tile"), lax.axis_index("gz"), lax.axis_index("rep")
    half = lax.rem(me + group, 2)
    sources = source_tile[:, 0, :, 0]
    shifts = block_shifts[0, 0]
    cap = MAX_NAMED if tiles == 4 else sources.shape[1]
    planes = 2 * depth
    window, span = height // 2 + 2 * EDGE, width + BLK_X
    short, full = jnp.bfloat16, jnp.float32
    whole, send_shape = (fixed_image.shape, short), ((depth, SEND_ROWS, width), short)
    side_shape = ((planes, KEEP_ROWS, BLK_X), short)
    image_shape = ((planes, window, span), full)
    smem, vmem = (pl.BlockSpec(memory_space=space) for space in (pltpu.SMEM, pltpu.VMEM))
    outs = [((cap, depth, BLK_Y, BLK_X), short)] * (tiles - 1) + [(sources.shape, jnp.int32), whole, whole, send_shape]
    *packs, sources, moving_image, fixed_image, fixed_send = pl.pallas_call(
        functools.partial(pack_kernel, tiles),
        out_shape=[pltpu.VMEM(*out) for out in outs],
        in_specs=[smem, vmem, vmem, vmem],
        out_specs=[vmem] * len(outs),
    )(sources, sources, moving_image, fixed_image)

    trio = ("tile", "gz", "rep")

    def number(t, g, r):
        return (t * 2 + g) * 2 + r

    swap = [(0, 1), (1, 0)]
    straight, slant, crossed = [], [], []
    for r in range(2):
        for t in range(tiles):
            for g in range(2):
                to = t - 1 if (g + t) % 2 == 0 else t + 1
                there = 0 <= to < tiles
                straight.append((number(t, g, r), number(to, g, r) if there else number(t, g, 1 - r)))
                crossed.append((number(t, g, r), number(to if there else t, g, 1 - r)))
                slant.append((number(t, g, r), number(to if there else t, 1 - g, r)))

    got = [
        lax.ppermute(pack, "tile", [(t, t ^ step) for t in range(tiles)])
        for step, pack in zip(far_first(tiles), packs)
    ]
    fixed_got = lax.ppermute(fixed_send, "gz", swap)
    own, send = local_kernel(
        functools.partial(unpack_kernel, tiles), [whole, send_shape], [sources, shifts, moving_image, *got]
    )
    warp_got = lax.ppermute(send, "gz", swap)
    (fixed_side,) = local_kernel(side_kernel, [side_shape], [fixed_image, fixed_got])
    fixed_near = lax.ppermute(fixed_side, "rep", swap)
    boxes = [(count, planes, window, span) for count in (2, 3)]
    fixed, fixed_boxes, band = local_kernel(
        fixed_kernel,
        [image_shape, (boxes[0], full), ((span, span), short)],
        [fixed_image, fixed_got, fixed_near],
        [pltpu.VMEM(boxes[0], full)],
    )
    rim_shape = (2, planes * EDGE, width)
    warp_side, rims, far_rims = local_kernel(
        edge_kernel,
        [side_shape, (rim_shape, short), ((2, planes * EDGE, BLK_X), short)],
        [own, warp_got, fixed],
        [pltpu.VMEM(rim_shape, full)],
    )
    warp_near = lax.ppermute(warp_side, "rep", swap)
    rims = lax.ppermute(rims, trio, straight)
    far_rims = lax.ppermute(far_rims, trio, crossed)
    (warped,) = local_kernel(warped_kernel, [image_shape], [own, warp_got, warp_near])
    (warped_boxes,) = local_kernel(
        cross_kernel, [(boxes[1], full)], [fixed, warped, band], [pltpu.VMEM(boxes[1], full)]
    )

    row_knots, col_knots = height // SPACING, width // SPACING
    high, low = table_halves(spline_table(side * BLK_X, span, side * col_knots, col_knots))
    table_x = jnp.pad(jnp.concatenate([high, low], axis=1), ((0, 0), (0, -2 * col_knots % 128)))
    (part,) = local_kernel(
        functools.partial(main_kernel, tiles),
        [((3 * (row_knots + 4), col_knots), full)],
        [fixed, warped, fixed_boxes, warped_boxes, rims, far_rims, band, table_x],
        [
            pltpu.VMEM((planes, window, span), full),
            pltpu.VMEM((5, planes, 2 * EDGE, span), full),
            pltpu.VMEM((3, planes, window, span), full),
            pltpu.VMEM((3, window, span), full),
            pltpu.VMEM((2, planes * EDGE, span), full),
        ],
    )
    part = part.reshape(3, row_knots + 4, col_knots)
    across = lax.ppermute(part, "gz", swap)
    part_slant = lax.ppermute(part, trio, slant)
    part_straight = lax.ppermute(part, trio, straight)
    below = jnp.where(half == 0, part_slant, part_straight)
    above = jnp.where(half == 0, part_straight, part_slant)
    below = jnp.where(me == tiles - 1, 0.0, below[:, :2])
    above = jnp.where(me == 0, 0.0, above[:, row_knots + 2 :])
    middle = part[:, 2 : row_knots + 2] + across[:, 2 : row_knots + 2]
    return (middle + jnp.concatenate([above, below], axis=1))[:, None]


def solution(mesh):
    sizes = mesh.shape
    tiles = sizes["tile"]
    fast = sizes["gz"] == 2 and sizes["rep"] == 2 and tiles & (tiles - 1) == 0 and tiles > 1
    return jax.shard_map(
        functools.partial(fast_body, tiles) if fast else body,
        mesh=mesh,
        in_specs=(
            P(("slab", "gz"), "tile", "rep"),
            P(("slab", "gz"), "tile", "rep"),
            P("slab", "rep", None, None),
            P(("slab", "tile"), "rep", None, None),
        ),
        out_specs=P(None, "slab", "tile", "rep"),
        check_vma=False,
    )
```
